32 devices in a mesh: grp: 8 (over z, core), shard: 4 (over y, x).
Axes of the slice: x: 2, y: 2, z: 4, core: 2. Of those that a mesh axis runs over, the one named last changes fastest.
Arguments:
- tokens: bfloat16 [64, 128, 2048], P(('grp', 'shard')), may hold values from -6 to 6
- cotangent: bfloat16 [64, 128, 2048], P(('grp', 'shard')), may hold values from -6 to 6
- lengths: int32 [64, 4], P('grp'), may hold values from 0 to 128, as said below
- dealing: int32 [64], P('grp'), may hold values from 0 to 63, as said below
- first_gain: bfloat16 [2048], P(('grp', 'shard')), may hold values from 0.5 to 1.5
- first_shift: bfloat16 [2048], P(('grp', 'shard')), may hold values from -3 to 3
- query_weight: bfloat16 [2048, 2048], P(('grp', 'shard')), may hold values from -0.125 to 0.125
- query_bias: bfloat16 [2048], P(('grp', 'shard')), may hold values from -3 to 3
- keyval_weight: bfloat16 [2048, 256], P(('grp', 'shard')), may hold values from -0.125 to 0.125
- value_bias: bfloat16 [128], P(('grp', 'shard')), may hold values from -3 to 3
- out_weight: bfloat16 [2048, 2048], P(('grp', 'shard')), may hold values from -0.375 to 0.375
- out_bias: bfloat16 [2048], P(('grp', 'shard')), may hold values from -3 to 3
- second_gain: bfloat16 [2048], P(('grp', 'shard')), may hold values from 0.5 to 1.5
- second_shift: bfloat16 [2048], P(('grp', 'shard')), may hold values from -3 to 3
- up_weight: bfloat16 [2048, 8192], P(('grp', 'shard')), may hold values from -0.125 to 0.125
- up_bias: bfloat16 [8192], P(('grp', 'shard')), may hold values from -3 to 3
- down_weight: bfloat16 [8192, 2048], P(('grp', 'shard')), may hold values from -0.0625 to 0.0625
- down_bias: bfloat16 [2048], P(('grp', 'shard')), may hold values from -3 to 3
Outputs:
- block_output: bfloat16 [64, 128, 2048], P(('grp', 'shard'))
- input_grad: bfloat16 [64, 128, 2048], P(('grp', 'shard'))
- first_gain_grad: float32 [2048], P('shard')
- first_shift_grad: float32 [2048], P('shard')
- query_weight_grad: float32 [2048, 2048], P('shard')
- query_bias_grad: float32 [2048], P('shard')
- keyval_weight_grad: float32 [2048, 256], P('shard')
- value_bias_grad: float32 [128], P('shard')
- out_weight_grad: float32 [2048, 2048], P('shard')
- out_bias_grad: float32 [2048], P('shard')
- second_gain_grad: float32 [2048], P('shard')
- second_shift_grad: float32 [2048], P('shard')
- up_weight_grad: float32 [2048, 8192], P('shard')
- up_bias_grad: float32 [8192], P('shard')
- down_weight_grad: float32 [8192, 2048], P('shard')
- down_bias_grad: float32 [2048], P('shard')
The draws below stay inside these ranges and needn't reach their ends.
Inputs may be any that keep to these rules, and one draw needn't show every extreme that they name: The 4 lengths of a row sum to 102 or more and to 128 at most; positions after that sum are padding; a length may be 0; in every draw some row holds a single document of 128 tokens. dealing is a permutation of the rows, and dealing[j] lies in the same group of 8 rows as j (rows g * 8 to (g + 1) * 8 - 1).
All inputs are finite; a program needn't handle non-finite values.
Results may differ from the reference program's by a relative error of at most 0.019.
Values may be sent and summed in bfloat16 or wider, within the bound.
A program may use at most 448 MiB of HBM per device.

```python
import jax
import jax.numpy as jnp
from jax import lax

D = 2048
HEADS = 16
HD = 128
FF = 8192
CAP = 128
DOCS = 4
ROWS = 64
GROUP_ROWS = 8


def draw_lengths(key, part):
    key = jax.random.fold_in(key, 11)
    key_used, key_cuts, key_single = jax.random.split(key, 3)
    used = jax.random.randint(key_used, (ROWS, 1), CAP * 4 // 5, CAP + 1).astype(jnp.int32)
    cuts = jax.random.randint(key_cuts, (ROWS, DOCS - 1), 0, CAP + 1).astype(jnp.int32)
    cuts = jnp.sort(jnp.minimum(cuts, used), axis=1)
    edges = jnp.concatenate([jnp.zeros((ROWS, 1), jnp.int32), cuts, used], axis=1)
    pieces = edges[:, 1:] - edges[:, :-1]
    chosen = jax.random.randint(key_single, (), 0, ROWS)
    single = jnp.concatenate([jnp.full((1,), CAP, jnp.int32), jnp.zeros((DOCS - 1,), jnp.int32)])
    picked = jnp.arange(ROWS)[:, None] == chosen
    return jnp.where(picked, single[None, :], pieces).astype(jnp.int32)


def draw_dealing(key, part):
    key = jax.random.fold_in(key, 23)
    groups = ROWS // GROUP_ROWS
    group_keys = jax.random.split(key, groups)

    def one_group(group_key):
        return jax.random.permutation(group_key, GROUP_ROWS).astype(jnp.int32)
    orders = jax.vmap(one_group)(group_keys)
    offsets = (jnp.arange(groups, dtype=jnp.int32) * GROUP_ROWS)[:, None]
    return (orders + offsets).reshape(ROWS).astype(jnp.int32)


def block_levels(rng, dims, cuts, low, top_value):
    level = 1.0
    for axis_at, shards_of in cuts:
        heights = jax.random.uniform(jax.random.fold_in(jax.random.fold_in(rng, 6), axis_at), (shards_of,), jnp.float32, low / len(cuts), top_value / len(cuts))
        level = level * jnp.repeat(jnp.exp(heights), dims[axis_at] // shards_of).reshape((-1,) + (1,) * (len(dims) - 1 - axis_at))
    return level


def centred(rng, dims, scale, reach, shards=(), kind=jnp.bfloat16):
    values = scale * jax.random.normal(rng, dims, jnp.float32)
    if shards:
        values = values * block_levels(rng, dims, shards, -0.22, 0.18)
    return jnp.clip(values, -reach, reach).astype(kind)


def setup_inputs(seed: int = 0) -> dict:
    streams_of = jax.random.split(jax.random.key(seed), 19)
    tokens = centred(streams_of[0], (ROWS, CAP, D), 1.0, 6.0, ((0, 32),))
    cotangent = centred(streams_of[1], (ROWS, CAP, D), 1.0, 6.0, ((0, 32),))
    lengths = draw_lengths(jax.random.fold_in(streams_of[18], 71), 0)
    dealing = draw_dealing(jax.random.fold_in(streams_of[18], 71), 0)
    first_gain = jnp.clip(1.0 + 0.1 * jax.random.normal(streams_of[4], (D,), jnp.float32), 0.5, 1.5).astype(jnp.bfloat16)
    first_shift = centred(streams_of[5], (D,), 0.5, 3.0, ((0, 32),))
    query_weight = centred(streams_of[6], (D, D), D ** -0.5, 0.125, ((0, 32),))
    query_bias = centred(streams_of[7], (D,), 0.5, 3.0, ((0, 32),))
    keyval_weight = centred(streams_of[8], (D, 2 * HD), D ** -0.5, 0.125, ((0, 32),))
    value_bias = centred(streams_of[9], (HD,), 0.5, 3.0, ((0, 32),))
    out_weight = centred(streams_of[10], (D, D), (D // 8) ** -0.5, 0.375, ((0, 32),))
    out_bias = centred(streams_of[11], (D,), 0.5, 3.0, ((0, 32),))
    second_gain = jnp.clip(1.0 + 0.1 * jax.random.normal(streams_of[12], (D,), jnp.float32), 0.5, 1.5).astype(jnp.bfloat16)
    second_shift = centred(streams_of[13], (D,), 0.5, 3.0, ((0, 32),))
    up_weight = centred(streams_of[14], (D, FF), D ** -0.5, 0.125, ((0, 32),))
    up_bias = centred(streams_of[15], (FF,), 0.5, 3.0, ((0, 32),))
    down_weight = centred(streams_of[16], (FF, D), FF ** -0.5, 0.0625, ((0, 32),))
    down_bias = centred(streams_of[17], (D,), 0.5, 3.0, ((0, 32),))
    return dict(tokens=tokens, cotangent=cotangent, lengths=lengths, dealing=dealing, first_gain=first_gain, first_shift=first_shift, query_weight=query_weight, query_bias=query_bias, keyval_weight=keyval_weight, value_bias=value_bias, out_weight=out_weight, out_bias=out_bias, second_gain=second_gain, second_shift=second_shift, up_weight=up_weight, up_bias=up_bias, down_weight=down_weight, down_bias=down_bias)


EPS = 1e-05
NEGATIVE = -1e+30
HIGH = lax.Precision.HIGHEST

@jax.custom_vjp
def low(v):
    return lax.optimization_barrier(v.astype(jnp.bfloat16)).astype(jnp.float32)

@jax.custom_vjp
def low_back(v):
    return v

def low_keep(v):
    return (low(v), None)

def low_pass(kept, grad):
    return (grad,)

def back_keep(v):
    return (v, None)

def back_low(kept, grad):
    return (low(grad),)
low.defvjp(low_keep, low_pass)
low_back.defvjp(back_keep, back_low)

def layer_norm(values, gain, shift):
    centre = lax.optimization_barrier(jnp.mean(values, axis=-1, keepdims=True))
    offset = values - centre
    spread = lax.optimization_barrier(jnp.mean(offset * offset, axis=-1, keepdims=True))
    return offset * lax.rsqrt(spread + EPS) * gain + shift

def matmul(left, right):
    return jnp.dot(left, right, precision=HIGH, preferred_element_type=jnp.float32)

def row_masks(lengths_row):
    doc_ends = jnp.cumsum(lengths_row)
    places = jnp.arange(CAP, dtype=jnp.int32)
    segment = lax.optimization_barrier(jnp.sum((places[:, None] >= doc_ends[None, :]).astype(jnp.int32), axis=1))
    live_mask = (places < doc_ends[-1]).astype(jnp.float32)
    allowed = (segment[:, None] == segment[None, :]) & (places[None, :] <= places[:, None])
    return (live_mask, allowed)

def row_forward(params, row_tokens, lengths_row):
    gain_one, shift_one, weight_query, bias_query, weight_keyval, bias_value, weight_out, bias_out, gain_two, shift_two, weight_up, bias_up, weight_down, bias_down = params
    live_mask, allowed = row_masks(lengths_row)
    normed_one = low(layer_norm(row_tokens, gain_one, shift_one))
    queries = low_back(low(matmul(normed_one, weight_query) + bias_query))
    value_pad = jnp.concatenate([jnp.zeros((HD,), jnp.float32), bias_value])
    keyvals = low_back(low(matmul(normed_one, weight_keyval) + value_pad))
    key_rows = keyvals[:, :HD]
    value_rows = keyvals[:, HD:]
    query_rows = queries.reshape(CAP * HEADS, HD)
    scores = low_back(matmul(query_rows, key_rows.T) * HD ** (-0.5))
    scores = jnp.where(jnp.repeat(allowed, HEADS, axis=0), scores, NEGATIVE)
    probs = low(jax.nn.softmax(scores, axis=-1))
    attended = low_back(low(matmul(probs, value_rows))).reshape(CAP, D)
    branch = low_back(matmul(attended, weight_out) + bias_out)
    middle = row_tokens + branch
    normed_two = low(layer_norm(middle, gain_two, shift_two))
    hidden_pre = low_back(matmul(normed_two, weight_up) + bias_up)
    activated = low(jax.nn.gelu(hidden_pre, approximate=True))
    branch_two = low_back(matmul(activated, weight_down) + bias_down)
    return (middle + branch_two) * live_mask[:, None]

def reference(tokens, cotangent, lengths, dealing, first_gain, first_shift, query_weight, query_bias, keyval_weight, value_bias, out_weight, out_bias, second_gain, second_shift, up_weight, up_bias, down_weight, down_bias):
    params = tuple((item.astype(jnp.float32) for item in (first_gain, first_shift, query_weight, query_bias, keyval_weight, value_bias, out_weight, out_bias, second_gain, second_shift, up_weight, up_bias, down_weight, down_bias)))
    dealt_lengths = jnp.take(lengths, dealing, axis=0)

    def forward(inputs, weights):
        dealt = jnp.take(inputs, dealing, axis=0)

        def one_row(item):
            return row_forward(weights, item[0], item[1])
        return lax.map(jax.checkpoint(one_row), (dealt, dealt_lengths))
    result, pullback = jax.vjp(forward, tokens.astype(jnp.float32), params)
    grad_tokens, grads = pullback(cotangent.astype(jnp.float32))
    return (result.astype(jnp.bfloat16), grad_tokens.astype(jnp.bfloat16), grads[0], grads[1], grads[2], grads[3], grads[4], grads[5], grads[6], grads[7], grads[8], grads[9], grads[10], grads[11], grads[12], grads[13])
```

```python
from functools import partial

import jax
import jax.numpy as jnp
from jax import lax
from jax.sharding import PartitionSpec as P

HEADS = 16
HD = 128
EPS = 1e-05
NEGATIVE = -1e30
BF = jnp.bfloat16
F32 = jnp.float32


def mm(left, right):
    return jnp.dot(left, right, preferred_element_type=F32)


def mm_tn(left, right):
    return lax.dot_general(left, right, (((0,), (0,)), ((), ())), preferred_element_type=F32)


def mm_nt(left, right):
    return lax.dot_general(left, right, (((1,), (1,)), ((), ())), preferred_element_type=F32)


def normalize(values):
    centre = jnp.mean(values, axis=-1, keepdims=True)
    offset = values - centre
    spread = jnp.mean(offset * offset, axis=-1, keepdims=True)
    rate = lax.rsqrt(spread + EPS)
    return offset * rate, rate


def norm_back(grad, unit, rate, gain):
    e = grad * gain
    back = rate * (
        e - jnp.mean(e, axis=-1, keepdims=True) - unit * jnp.mean(e * unit, axis=-1, keepdims=True)
    )
    return back, jnp.sum(grad * unit, axis=0), jnp.sum(grad, axis=0)


def row_ends(lengths_row):
    docs = lengths_row.shape[0]
    at = jnp.arange(docs, dtype=jnp.int32)
    return jnp.sum(jnp.where(at[None, :] <= at[:, None], lengths_row[None, :], 0), axis=1)


def live(lengths_row, length):
    places = jnp.arange(length, dtype=jnp.int32)
    return (places < jnp.sum(lengths_row)).astype(F32)


def allowed_pairs(lengths_row, length):
    ends = row_ends(lengths_row)
    places = jnp.arange(length, dtype=jnp.int32)
    segment = jnp.sum((places[:, None] >= ends[None, :]).astype(jnp.int32), axis=1)
    return (segment[:, None] == segment[None, :]) & (places[None, :] <= places[:, None])


def flips(count, mask):
    return [(i, i ^ mask) for i in range(count)]


def cube_orders(count):
    order = list(range(count.bit_length() - 1))
    return order, order[::-1]


def cube_gather(halves, count, axis):
    orders = cube_orders(count)
    held = [{0: half} for half in halves]
    for step in range(len(orders[0])):
        for k in range(2):
            mask = 1 << orders[k][step]
            keys = sorted(held[k])
            pack = jnp.stack([held[k][q] for q in keys])
            got = lax.ppermute(pack, axis, flips(count, mask))
            for i, q in enumerate(keys):
                held[k][q ^ mask] = got[i]
    return held


def cube_scatter(blocks, count, axis):
    orders = cube_orders(count)
    held = [dict(b) for b in blocks]
    for step in range(len(orders[0])):
        for k in range(2):
            mask = 1 << orders[k][step]
            away = [q for q in sorted(held[k]) if q & mask]
            pack = jnp.stack([held[k].pop(q) for q in away])
            got = lax.ppermute(pack, axis, flips(count, mask))
            for i, q in enumerate(away):
                held[k][q ^ mask] = held[k][q ^ mask] + got[i]
    return held[0][0], held[1][0]


def line_stages(groups):
    chips = groups // 2
    both = lambda pairs: [(2 * a + c, 2 * b + c) for a, b in pairs for c in range(2)]
    stages = []
    for hop in range(1, chips // 2):
        stages.append(("in", both([(hop - 1, hop), (chips - hop, chips - 1 - hop)]), None))
    low, high = chips // 2 - 1, chips // 2
    stages.append(("in", both([(low, high), (high, low)]), None))
    for hop in range(1, chips // 2):
        a, b = low + 1 - hop, high - 1 + hop
        stages.append(("out", both([(a, a - 1), (b, b + 1)]), (a - 1, b + 1)))
    return stages


def line_sum(chunks, groups, axis):
    stages = line_stages(groups)
    place = lax.axis_index(axis) // 2
    state = [None] * len(chunks)
    last = ()
    for turn in range(len(chunks) + len(stages) - 1):
        work = [k for k in range(len(chunks)) if 0 <= turn - k < len(stages)]
        sends = [chunks[k] if turn == k else state[k] for k in work]
        if last:
            tied = lax.optimization_barrier(tuple(sends) + last)
            sends = tied[: len(sends)]
        got = []
        for k, send in zip(work, sends):
            kind, pairs, ends = stages[turn - k]
            arrived = lax.ppermute(send, axis, pairs)
            got.append(arrived)
            if kind == "in":
                state[k] = send + arrived
            else:
                state[k] = jnp.where((place == ends[0]) | (place == ends[1]), arrived, send)
        last = tuple(got)
    return state


def shards(
    groups,
    count,
    tokens,
    cotangent,
    lengths,
    dealing,
    first_gain,
    first_shift,
    query_weight,
    query_bias,
    keyval_weight,
    value_bias,
    out_weight,
    out_bias,
    second_gain,
    second_shift,
    up_weight,
    up_bias,
    down_weight,
    down_bias,
):
    both = ("grp", "shard")
    micro, length, width = tokens.shape
    group_rows = dealing.shape[0]
    group = lax.axis_index("grp")
    me = lax.axis_index("shard")
    core = group % 2
    half = micro // 2
    block = down_weight.shape[0]
    hidden = block * groups
    rows = micro * length

    local_deal = dealing - group * group_rows
    steps = jnp.arange(group_rows, dtype=jnp.int32)
    inverse = jnp.sum(jnp.where(local_deal[:, None] == steps[None, :], steps[:, None], 0), axis=0)
    pick = lambda table, at: lax.dynamic_index_in_dim(table, at, 0, keepdims=False)

    small = (
        first_gain, first_shift, query_bias, value_bias, out_bias,
        second_gain, second_shift, up_bias, down_bias,
    )
    packed = lax.all_gather(jnp.concatenate(small), both, axis=0)
    wide = []
    at = 0
    for item in small:
        wide.append(packed[:, at : at + item.shape[0]].astype(F32))
        at += item.shape[0]
    up_part = pick(wide[7].reshape(groups, count, block).swapaxes(0, 1), me).reshape(hidden)
    gain_one, shift_one, bias_query, bias_value, bias_out, gain_two, shift_two, _, bias_down = [
        item.reshape(-1) for item in wide
    ]

    weight_query = lax.all_gather(query_weight, both, axis=0, tiled=True)
    weight_keyval = lax.all_gather(keyval_weight, both, axis=0, tiled=True)
    weight_out = lax.all_gather(out_weight, both, axis=0, tiled=True)
    up_rows = up_weight.shape[0]
    up_cut = up_weight.reshape(up_rows, groups, count, block).transpose(2, 0, 1, 3)
    up_cut = lax.all_to_all(up_cut.reshape(count, up_rows, hidden), "shard", 0, 0)
    weight_up = lax.all_gather(up_cut.reshape(count * up_rows, hidden), "grp", axis=0, tiled=True)
    weight_down = lax.all_gather(down_weight, "grp", axis=0, tiled=True)

    def gather_rows(values, place_of):
        held = cube_gather((values[:half], values[half:]), count, "shard")
        out = jnp.zeros((group_rows, length, width), values.dtype)
        for q in range(count):
            for k in range(2):
                for i in range(half):
                    row = (me ^ q) * micro + k * half + i
                    out = lax.dynamic_update_slice(out, held[k][q][i][None], (place_of(row), 0, 0))
        return out.reshape(group_rows * length, width)

    def scatter_rows(values, place_of):
        blocks = []
        for k in range(2):
            terms = {}
            for q in range(count):
                terms[q] = jnp.stack(
                    [pick(values, place_of((me ^ q) * micro + k * half + i)) for i in range(half)]
                )
            blocks.append(terms)
        return jnp.concatenate(cube_scatter(blocks, count, "shard"))

    dealt_place = lambda row: pick(inverse, row)
    same_place = lambda row: row

    cot_rows = gather_rows(cotangent, same_place).reshape(group_rows, length, width)
    dealt_live = jnp.stack([live(pick(lengths, local_deal[j]), length) for j in range(group_rows)])
    grad_down = (cot_rows.astype(F32) * dealt_live[:, :, None]).astype(BF)
    own_live = jnp.stack([pick(dealt_live, me * micro + m) for m in range(micro)])

    scale = HD**-0.5
    own_lengths = [pick(lengths, me * micro + m) for m in range(micro)]
    inputs = tokens.astype(F32).reshape(rows, width)
    unit_one, rate_one = normalize(inputs)
    normed_one = (unit_one * gain_one + shift_one).astype(BF)
    queries = (mm(normed_one, weight_query) + bias_query).astype(BF)
    value_pad = jnp.concatenate([jnp.zeros((HD,), F32), bias_value])
    keyvals = (mm(normed_one, weight_keyval) + value_pad).astype(BF)
    kept = []
    attended = []
    for m in range(micro):
        mask = jnp.repeat(allowed_pairs(own_lengths[m], length), HEADS, axis=0)
        query_rows = queries[m * length : (m + 1) * length].reshape(length * HEADS, HD)
        key_rows = keyvals[m * length : (m + 1) * length, :HD]
        value_rows = keyvals[m * length : (m + 1) * length, HD:]
        scores = jnp.where(mask, mm_nt(query_rows, key_rows) * scale, NEGATIVE)
        top = jnp.max(scores, axis=1, keepdims=True)
        powers = jnp.exp(scores - top)
        totals = jnp.sum(powers, axis=1, keepdims=True)
        probs = powers / totals
        probs_low = probs.astype(BF)
        attended.append(mm(probs_low, value_rows).reshape(length, width).astype(BF))
        kept.append((mask, query_rows, key_rows, value_rows, top + jnp.log(totals), probs_low))
    attended = jnp.concatenate(attended)
    middle = inputs + mm(attended, weight_out) + bias_out
    unit_two, rate_two = normalize(middle)
    normed_two_own = (unit_two * gain_two + shift_two).astype(BF)

    normed_two = gather_rows(normed_two_own.reshape(micro, length, width), dealt_place)
    hidden_pre = mm(normed_two, weight_up) + up_part
    gelu_tanh = partial(jax.nn.gelu, approximate=True)
    activated_wide, gelu_pull = jax.vjp(gelu_tanh, hidden_pre)
    activated = activated_wide.astype(BF)
    grad_down = grad_down.reshape(group_rows * length, width)
    grad_hidden = gelu_pull(mm_nt(grad_down, weight_down))[0].astype(BF)
    grad_two = mm_nt(grad_hidden, weight_up).astype(BF).reshape(group_rows, length, width)
    grad_normed_two = scatter_rows(grad_two, dealt_place).astype(F32).reshape(rows, width)
    down_grad = mm_tn(activated, grad_down).astype(BF)
    up_grad = mm_tn(normed_two, grad_hidden).astype(BF)

    result = mm(activated, weight_down).astype(BF).reshape(group_rows, length, width)
    middle_rows = middle.reshape(micro, length, width)
    for m in range(micro):
        at = dealt_place(me * micro + m)
        row = (pick(result, at).astype(F32) + middle_rows[m]).astype(BF)
        result = lax.dynamic_update_slice(result, row[None], (at, 0, 0))
    result = scatter_rows(result, same_place).astype(F32)
    block_output = ((result + bias_down) * own_live[:, :, None]).astype(BF)

    pairs = flips(groups, 1)

    def pair_sum(values):
        mine = lax.dynamic_index_in_dim(values, core, 1, keepdims=False)
        other = lax.dynamic_index_in_dim(values, 1 - core, 1, keepdims=False)
        return mine + lax.ppermute(other, "grp", pairs)

    slab = hidden // count
    down_half = pair_sum(down_grad.reshape(count, 2, slab // 2, width))
    down_half = lax.all_to_all(down_half, "shard", 0, 0)
    up_half = pair_sum(up_grad.reshape(count, 2, width // count // 2, hidden))
    up_half = lax.all_to_all(up_half, "shard", 0, 0)

    own_cot = jnp.stack([pick(cot_rows, dealt_place(me * micro + m)) for m in range(micro)])
    given_live = jnp.stack([live(own_lengths[m], length) for m in range(micro)])
    grad_out = (own_cot.astype(F32) * given_live[:, :, None]).reshape(rows, width)
    down_bias_grad = jnp.sum(grad_out.astype(BF).astype(F32), axis=0)
    back_two, gain_two_grad, shift_two_grad = norm_back(grad_normed_two, unit_two, rate_two, gain_two)
    grad_middle = back_two + grad_out
    grad_branch = grad_middle.astype(BF)
    out_bias_grad = jnp.sum(grad_branch.astype(F32), axis=0)
    out_grad = mm_tn(attended, grad_branch).astype(BF)
    grad_attended = mm_nt(grad_branch, weight_out).astype(BF)
    grad_queries = []
    grad_keyvals = []
    for m in range(micro):
        mask, query_rows, key_rows, value_rows, log_total, probs_low = kept[m]
        grad_rows = grad_attended[m * length : (m + 1) * length].reshape(length * HEADS, HD)
        again = jnp.where(mask, mm_nt(query_rows, key_rows) * scale, NEGATIVE)
        probs = jnp.exp(again - log_total)
        grad_probs = mm_nt(grad_rows, value_rows)
        centre = jnp.sum(probs * grad_probs, axis=1, keepdims=True)
        grad_scores = (probs * (grad_probs - centre)).astype(BF)
        grad_queries.append((mm(grad_scores, key_rows) * scale).reshape(length, width).astype(BF))
        grad_keys = mm_tn(grad_scores, query_rows) * scale
        grad_values = mm_tn(probs_low, grad_rows)
        grad_keyvals.append(jnp.concatenate([grad_keys, grad_values], axis=1).astype(BF))
    grad_queries = jnp.concatenate(grad_queries)
    grad_keyvals = jnp.concatenate(grad_keyvals)
    query_grad = mm_tn(normed_one, grad_queries).astype(BF)
    keyval_grad = mm_tn(normed_one, grad_keyvals).astype(BF)
    grad_normed_one = mm_nt(grad_queries, weight_query) + mm_nt(grad_keyvals, weight_keyval)
    back_one, gain_one_grad, shift_one_grad = norm_back(grad_normed_one, unit_one, rate_one, gain_one)
    input_grad = (back_one + grad_middle).astype(BF).reshape(micro, length, width)

    def slices(values):
        part = lax.psum_scatter(values, "shard", scatter_dimension=0, tiled=True)
        return pair_sum(part.reshape(1, 2, part.shape[0] // 2, part.shape[1]))[0]

    out_half, query_half, keyval_half = slices(out_grad), slices(query_grad), slices(keyval_grad)

    chunks = [down_half[q] for q in range(count)] + [up_half[q] for q in range(count)]
    chunks = chunks + [out_half, query_half, keyval_half]
    chunks = line_sum(chunks, groups, "grp")

    def whole(halves):
        other = lax.ppermute(halves, "grp", pairs)
        first = jnp.where(core == 0, halves, other)
        second = jnp.where(core == 0, other, halves)
        return jnp.stack([first, second]).astype(F32)

    down_full = whole(jnp.stack(chunks[:count]))
    per = groups // count
    down_full = down_full.transpose(1, 0, 2, 3).reshape(count, per, block, width)
    down_full = down_full.transpose(1, 0, 2, 3).reshape(per * count * block, width)
    up_full = whole(jnp.stack(chunks[count : 2 * count]))
    up_full = up_full.reshape(2, count, width // count // 2, groups, block)
    up_full = up_full.transpose(0, 2, 3, 1, 4).reshape(width // count, groups * count * block)
    tail = chunks[2 * count :]
    out_full, query_full, keyval_full = [
        whole(item).reshape(2 * item.shape[0], item.shape[1]) for item in tail
    ]

    up_bias_part = jnp.sum(grad_hidden.astype(F32), axis=0).reshape(groups, 1, block)
    value_bias_grad = jnp.sum(grad_keyvals[:, HD:].astype(F32), axis=0)
    query_bias_grad = jnp.sum(grad_queries.astype(F32), axis=0)
    spot = (jnp.arange(count, dtype=jnp.int32) == me)[None, :, None]
    up_bias_grad = jnp.where(spot, up_bias_part, 0.0).reshape(-1)
    vectors = (
        gain_one_grad, shift_one_grad, query_bias_grad, value_bias_grad, out_bias_grad,
        gain_two_grad, shift_two_grad, up_bias_grad, down_bias_grad,
    )
    summed = lax.psum(jnp.concatenate(vectors), both)
    parts = []
    at = 0
    for item in vectors:
        size = item.shape[0] // count
        parts.append(lax.dynamic_slice(summed, (at + me * size,), (size,)))
        at += item.shape[0]

    return (
        block_output, input_grad, parts[0], parts[1], query_full, parts[2], keyval_full, parts[3],
        out_full, parts[4], parts[5], parts[6], up_full, parts[7], down_full, parts[8],
    )


def solution(mesh):
    rows = P(("grp", "shard"), None, None)
    flat = P(("grp", "shard"))
    tall = P(("grp", "shard"), None)
    vector, matrix = P("shard"), P("shard", None)
    return jax.shard_map(
        partial(shards, mesh.shape["grp"], mesh.shape["shard"]),
        mesh=mesh,
        in_specs=(
            rows, rows, P("grp", None), P("grp"), flat, flat, tall, flat, tall, flat,
            tall, flat, flat, flat, tall, flat, tall, flat,
        ),
        out_specs=(
            rows, rows, vector, vector, matrix, vector, matrix, vector,
            matrix, vector, vector, vector, matrix, vector, matrix, vector,
        ),
        check_vma=False,
    )
```

```python
import functools
from functools import partial

import jax
import jax.numpy as jnp
from jax import lax
from jax.experimental import pallas as pl
from jax.experimental.pallas import tpu as pltpu
from jax.sharding import PartitionSpec as P

HEADS = 16
HD = 128
EPS = 1e-05
NEGATIVE = -1e30
BF = jnp.bfloat16
F32 = jnp.float32
MESH = pl.DeviceIdType.MESH
LAG_MID = 2
LAG_OUT = 4


def mm(left, right):
    return jnp.dot(left, right, preferred_element_type=F32)


def mm_tn(left, right):
    return lax.dot_general(left, right, (((0,), (0,)), ((), ())), preferred_element_type=F32)


def mm_nt(left, right):
    return lax.dot_general(left, right, (((1,), (1,)), ((), ())), preferred_element_type=F32)


def normalize(values):
    centre = jnp.mean(values, axis=-1, keepdims=True)
    offset = values - centre
    spread = jnp.mean(offset * offset, axis=-1, keepdims=True)
    rate = lax.rsqrt(spread + EPS)
    return offset * rate, rate


def norm_back(grad, unit, rate, gain):
    e = grad * gain
    back = rate * (
        e - jnp.mean(e, axis=-1, keepdims=True) - unit * jnp.mean(e * unit, axis=-1, keepdims=True)
    )
    return back, jnp.sum(grad * unit, axis=0), jnp.sum(grad, axis=0)


def row_ends(lengths_row):
    docs = lengths_row.shape[0]
    at = jnp.arange(docs, dtype=jnp.int32)
    return jnp.sum(jnp.where(at[None, :] <= at[:, None], lengths_row[None, :], 0), axis=1)


def live(lengths_row, length):
    places = jnp.arange(length, dtype=jnp.int32)
    return (places < jnp.sum(lengths_row)).astype(F32)


def allowed_pairs(lengths_row, length):
    ends = row_ends(lengths_row)
    places = jnp.arange(length, dtype=jnp.int32)
    segment = jnp.sum((places[:, None] >= ends[None, :]).astype(jnp.int32), axis=1)
    return (segment[:, None] == segment[None, :]) & (places[None, :] <= places[:, None])


def flips(count, mask):
    return [(i, i ^ mask) for i in range(count)]


def cube_orders(count):
    order = list(range(count.bit_length() - 1))
    return order, order[::-1]


def cube_gather(halves, count, axis):
    orders = cube_orders(count)
    held = [{0: half} for half in halves]
    for step in range(len(orders[0])):
        for k in range(2):
            mask = 1 << orders[k][step]
            keys = sorted(held[k])
            pack = jnp.stack([held[k][q] for q in keys])
            got = lax.ppermute(pack, axis, flips(count, mask))
            for i, q in enumerate(keys):
                held[k][q ^ mask] = got[i]
    return held


def cube_scatter(blocks, count, axis):
    orders = cube_orders(count)
    held = [dict(b) for b in blocks]
    for step in range(len(orders[0])):
        for k in range(2):
            mask = 1 << orders[k][step]
            away = [q for q in sorted(held[k]) if q & mask]
            pack = jnp.stack([held[k].pop(q) for q in away])
            got = lax.ppermute(pack, axis, flips(count, mask))
            for i, q in enumerate(away):
                held[k][q ^ mask] = held[k][q ^ mask] + got[i]
    return held[0][0], held[1][0]


def near_first(count):
    return sorted(range(1, count), key=lambda q: (bin(q).count("1"), q))


def cube_tree(count, parity, q):
    order = list(range(count.bit_length() - 1))
    if parity:
        order = order[::-1]
    at = max([i for i, d in enumerate(order) if q >> d & 1], default=-1)
    return [1 << d for d in order[at + 1 :]]


def near_first(count):
    return sorted(range(1, count), key=lambda q: (bin(q).count("1"), q))


def gather_kernel(
    groups, count, wq, wo, kvs, upc, q_all, o_all, kvs_all, up_all,
    zs, zr, ps, pr, bs, br, us, ur, loc,
):
    chips = groups // 2
    g, me = lax.axis_index("grp"), lax.axis_index("shard")
    p, c = lax.div(g, 2), lax.rem(g, 2)

    barrier = pltpu.get_barrier_semaphore()

    def greet(target):
        pl.semaphore_signal(barrier, inc=1, device_id=target, device_id_type=MESH)

    greet((g + 1 - 2 * c, me))
    for q in range(1, count):
        greet((g, lax.bitwise_xor(me, q)))

    @pl.when(p < chips - 1)
    def _():
        greet((g + 2, me))

    @pl.when(p > 0)
    def _():
        greet((g - 2, me))

    ends = (p == 0).astype(jnp.int32) + (p == chips - 1).astype(jnp.int32)
    pl.semaphore_wait(barrier, count + 2 - ends)

    def send(src, dst, send_sem, recv_sem, target):
        pltpu.make_async_remote_copy(
            src_ref=src, dst_ref=dst, send_sem=send_sem, recv_sem=recv_sem,
            device_id=target, device_id_type=MESH,
        ).start()

    def wait(ref, sem):
        pltpu.make_async_copy(ref, ref, sem).wait()

    own = (wq, wo, kvs)
    whole = (q_all, o_all, kvs_all)
    parity = (0, 1, 0)
    size = wq.shape[0]
    up_size = upc.shape[1]
    up_half = up_size * count // 2

    def spot(a, z, col):
        if a < 3:
            at = ((z * 2 + c) * count + col) * size
            return whole[a].at[pl.ds(pl.multiple_of(at, 16), size)]
        at = (z * 2 + c) * up_half * 2 + (a - 3) * up_half
        return up_all.at[pl.ds(pl.multiple_of(at, 16), up_half)]

    def along(a, way, hop, src, z):
        step = 1 - 2 * way
        send(src, spot(a, z, me), zs.at[a, way, hop], zr.at[a, way, hop], (g + 2 * step, me))

    def across(a, src, z, q):
        for m in cube_tree(count, parity[a], q):
            send(
                src, spot(a, z, lax.bitwise_xor(me, q)), ps.at[a], pr.at[a, z, q ^ m],
                (g, lax.bitwise_xor(me, m)),
            )

    def aside(a, src, z, q):
        send(src, spot(a, z, lax.bitwise_xor(me, q)), bs.at[a], br.at[a], (g + 1 - 2 * c, me))

    def may_send(way, hop):
        if way == 0:
            return (p >= hop - 1) & (p < chips - 1)
        return (p + hop - 1 <= chips - 1) & (p > 0)

    def may_take(way, hop):
        return p >= hop if way == 0 else p + hop <= chips - 1

    up_rows = lambda col: up_all.at[pl.ds(pl.multiple_of((g * count + col) * up_size, 16), up_size)]
    for q in near_first(count):
        to = lax.bitwise_xor(me, q)
        send(upc.at[to], up_rows(me), us, ur.at[q], (g, to))
    mine = [pltpu.make_async_copy(upc.at[me], up_rows(me), loc.at[3])]
    for a in range(3):
        mine.append(pltpu.make_async_copy(own[a], spot(a, p, me), loc.at[a]))
    for copy in mine:
        copy.start()

    def first(a, src):
        for way in range(2):
            pl.when(may_send(way, 1))(functools.partial(along, a, way, 1, src, p))
        aside(a, src, p, 0)

    for a in range(3):
        first(a, own[a])
        across(a, own[a], p, 0)
    mine[0].wait()
    for q in near_first(count):
        wait(up_rows(me), ur.at[q])
    for a in (3, 4):
        first(a, spot(a, p, me))

    def plane(z):
        for q in near_first(count):
            for a in range(3):
                ref = spot(a, z, lax.bitwise_xor(me, q))
                wait(ref, pr.at[a, z, q])
                across(a, ref, z, q)
                aside(a, ref, z, q)

    def planes(hop):
        if hop == 0:
            plane(p)
            return
        for way in range(2):
            z = p - hop if way == 0 else p + hop
            pl.when(may_take(way, hop))(functools.partial(plane, z))

    def arrive(a, hop):
        for way in range(2):

            @pl.when(may_take(way, hop))
            def _():
                z = p - hop if way == 0 else p + hop
                ref = spot(a, z, me)
                wait(ref, zr.at[a, way, hop])
                if hop + 1 < chips:
                    pl.when(may_send(way, hop + 1))(
                        functools.partial(along, a, way, hop + 1, ref, z)
                    )
                if a < 3:
                    across(a, ref, z, 0)
                aside(a, ref, z, 0)

    for hop in range(1, chips):
        for a in range(3):
            arrive(a, hop)
        planes(hop - 1)
        for a in (3, 4):
            arrive(a, hop)
    planes(chips - 1)

    for copy in mine[1:]:
        copy.wait()
    for a in range(5):
        for way in range(2):
            for hop in range(1, chips):
                pl.when(may_send(way, hop))(
                    functools.partial(wait, spot(a, p, me), zs.at[a, way, hop])
                )
    for a in range(3):
        wait(whole[a].at[pl.ds(0, chips * (count - 1) * size)], ps.at[a])
        wait(whole[a].at[pl.ds(0, chips * count * size)], bs.at[a])
        wait(whole[a].at[pl.ds(0, chips * count * size)], br.at[a])
    for a in (3, 4):
        wait(up_all.at[pl.ds(0, chips * up_half)], bs.at[a])
        wait(up_all.at[pl.ds(0, chips * up_half)], br.at[a])
    wait(up_all.at[pl.ds(0, (count - 1) * up_size)], us)


def gather_all(groups, count, wq, wo, kvs, upc):
    chips = groups // 2
    n = groups * count
    any_ = pl.BlockSpec(memory_space=pl.ANY)
    dma = pltpu.SemaphoreType.DMA
    tall = lambda x: jax.ShapeDtypeStruct((n * x.shape[0], x.shape[1]), x.dtype)
    return pl.pallas_call(
        functools.partial(gather_kernel, groups, count),
        out_shape=(
            tall(wq), tall(wo), tall(kvs),
            jax.ShapeDtypeStruct((n * upc.shape[1], upc.shape[2]), upc.dtype),
        ),
        in_specs=[any_] * 4,
        out_specs=(any_,) * 4,
        scratch_shapes=[
            dma((5, 2, chips)), dma((5, 2, chips)), dma((3,)), dma((3, chips, count)),
            dma((5,)), dma((5,)), dma, dma((count,)), dma((4,)),
        ],
        compiler_params=pltpu.CompilerParams(collective_id=1, has_side_effects=True),
        cost_estimate=pl.CostEstimate(flops=0, bytes_accessed=100_000_000, transcendentals=0),
        name="gather_all",
    )(wq, wo, kvs, upc)


def reduce_kernel(groups, count, subs, plain, *refs):
    n = len(subs)
    take = iter(refs)
    many = lambda: [next(take) for _ in range(n)]
    terms, final, land = many(), many(), many()
    part, held, outer, mid, load = many(), many(), many(), many(), many()
    sib, ld, sent, came, zs, z_in, z_mid, os, z_fin, xs, xr, loc, ss = take
    chips = groups // 2
    g, me = lax.axis_index("grp"), lax.axis_index("shard")
    p, c = lax.div(g, 2), lax.rem(g, 2)
    low = p < chips // 2
    inn = jnp.where(low, g + 2, g - 2)
    out = jnp.where(low, g - 2, g + 2)
    end = (p == 0) | (p == chips - 1)
    middle = (p == chips // 2 - 1) | (p == chips // 2)
    other = g + 1 - 2 * c

    barrier = pltpu.get_barrier_semaphore()

    def greet(target):
        pl.semaphore_signal(barrier, inc=1, device_id=target, device_id_type=MESH)

    greet((other, me))
    greet((inn, me))
    for q in range(1, count):
        greet((g, lax.bitwise_xor(me, q)))

    @pl.when(jnp.logical_not(end))
    def _():
        greet((out, me))

    pl.semaphore_wait(barrier, count + 2 - end.astype(jnp.int32))

    def send(src, dst, send_sem, recv_sem, target):
        pltpu.make_async_remote_copy(
            src_ref=src, dst_ref=dst, send_sem=send_sem, recv_sem=recv_sem,
            device_id=target, device_id_type=MESH,
        ).start()

    def wait(ref, sem):
        pltpu.make_async_copy(ref, ref, sem).wait()

    def add(dst, *more):
        rows = dst.shape[0]

        @pl.loop(0, rows // 16)
        def _(i):
            at = pl.ds(pl.multiple_of(i * 16, 16), 16)
            total = dst[at].astype(F32)
            for ref in more:
                total = total + ref[at].astype(F32)
            dst[at] = total.astype(BF)

    size = [terms[m].shape[2] // subs[m] for m in range(n)]
    cut = lambda m, j: pl.ds(j * size[m], size[m])

    for m in range(n):
        for q in near_first(count) + [0]:
            send(
                terms[m].at[lax.bitwise_xor(me, q), 1 - c], land[m].at[q], ss.at[m], sib.at[m, q],
                (other, me),
            )

    pair_tasks = []
    for m in range(n):
        pair_tasks.append([(m, j, q) for j in range(subs[m]) for q in near_first(count) + [0]])
    flat = [task for tasks in pair_tasks for task in tasks]

    def place(m, j, q):
        if q:
            return part[m].at[q - 1, cut(m, j)]
        return held[m].at[me, cut(m, j)]

    def loads(k):
        m, j, q = flat[k]
        slot = k % 2
        return (
            pltpu.make_async_copy(
                terms[m].at[lax.bitwise_xor(me, q), c, cut(m, j)], place(m, j, q), ld.at[slot, 0]
            ),
            pltpu.make_async_copy(land[m].at[q, cut(m, j)], load[m].at[slot], ld.at[slot, 1]),
        )

    def begin(k):
        m, j, q = flat[k]
        if j == 0:
            wait(land[m].at[q], sib.at[m, q])
        for copy in loads(k):
            copy.start()

    def pair(k):
        m, j, q = flat[k]
        if k == 0:
            begin(0)
        if k + 1 < len(flat):
            begin(k + 1)
        for copy in loads(k):
            copy.wait()
        ref = place(m, j, q)
        add(ref, load[m].at[k % 2])
        if q:
            send(ref, held[m].at[me, cut(m, j)], sent.at[m], came.at[m, j, q], (g, lax.bitwise_xor(me, q)))

    units = []
    for m in range(n):
        for j in range(subs[m]):
            units += [(m, j, q) for q in range(count)] if plain[m] else [(m, j, 0)]

    def value(u):
        m, j, q = units[u]
        return held[m].at[lax.bitwise_xor(me, q), cut(m, j)]

    def result(u, half):
        m, j, q = units[u]
        return final[m].at[half, lax.bitwise_xor(me, q) if plain[m] else 0, cut(m, j)]

    def inward(u):
        m, j, q = units[u]
        ref = value(u)
        if plain[m]:
            if q:
                wait(ref, came.at[m, j, q])
        else:
            others = [held[m].at[lax.bitwise_xor(me, r), cut(m, j)] for r in near_first(count)]
            for r, other_ref in zip(near_first(count), others):
                wait(other_ref, came.at[m, j, r])
            add(ref, *others)

        @pl.when(jnp.logical_not(end))
        def _():
            wait(outer[m].at[q, cut(m, j)], z_in.at[u])
            add(ref, outer[m].at[q, cut(m, j)])

        @pl.when(middle)
        def _():
            send(ref, mid[m].at[q, cut(m, j)], zs.at[u], z_mid.at[u], (inn, me))

        @pl.when(jnp.logical_not(middle))
        def _():
            send(ref, outer[m].at[q, cut(m, j)], zs.at[u], z_in.at[u], (inn, me))

    def centre(u):
        m, j, q = units[u]

        @pl.when(middle)
        def _():
            ref = value(u)
            wait(ref, zs.at[u])
            wait(mid[m].at[q, cut(m, j)], z_mid.at[u])
            add(ref, mid[m].at[q, cut(m, j)])
            pl.when(jnp.logical_not(end))(
                lambda: send(ref, result(u, c), os.at[u], z_fin.at[u], (out, me))
            )
            send(ref, result(u, c), xs.at[u], xr.at[u], (other, me))
            pltpu.make_async_copy(ref, result(u, c), loc.at[u]).start()

    def outward(u):
        @pl.when(jnp.logical_not(middle))
        def _():
            ref = result(u, c)
            wait(ref, z_fin.at[u])
            pl.when(jnp.logical_not(end))(
                lambda: send(ref, ref, os.at[u], z_fin.at[u], (out, me))
            )
            send(ref, ref, xs.at[u], xr.at[u], (other, me))

    done = 0
    for _ in pair_tasks[0]:
        pair(done)
        done += 1
    for step in range(len(units) + LAG_OUT):
        for _ in range(3):
            if done < len(flat):
                pair(done)
                done += 1
        if step < len(units):
            inward(step)
        if 0 <= step - LAG_MID < len(units):
            centre(step - LAG_MID)
        if 0 <= step - LAG_OUT < len(units):
            outward(step - LAG_OUT)

    for m in range(n):
        wait(land[m], ss.at[m])
        for q in range(count - 1):
            wait(part[m].at[q], sent.at[m])
    for u in range(len(units)):
        wait(result(u, 1 - c), xr.at[u])
        wait(result(u, c), xs.at[u])
        pl.when(jnp.logical_not(end))(functools.partial(wait, result(u, c), os.at[u]))
        pl.when(middle)(functools.partial(wait, result(u, c), loc.at[u]))
        pl.when(jnp.logical_not(middle))(functools.partial(wait, value(u), zs.at[u]))


def reduce_all(groups, count, terms, plain, subs):
    n = len(terms)
    any_ = pl.BlockSpec(memory_space=pl.ANY)
    dma = pltpu.SemaphoreType.DMA
    shape = lambda x, a, b: tuple(d for d in (a, b) if d) + x.shape[2:]
    out = [jax.ShapeDtypeStruct(shape(x, 2, count if f else 1), BF) for x, f in zip(terms, plain)]
    land = [jax.ShapeDtypeStruct(shape(x, count, 0), BF) for x in terms]
    part = [pltpu.VMEM(shape(x, count - 1, 0), BF) for x in terms]
    held = [pltpu.VMEM(shape(x, count, 0), BF) for x in terms]
    line = [pltpu.VMEM(shape(x, count if f else 1, 0), BF) for x, f in zip(terms, plain)]
    load = [pltpu.VMEM((2, x.shape[2] // s, x.shape[3]), BF) for x, s in zip(terms, subs)]
    units = sum(s * (count if f else 1) for s, f in zip(subs, plain))
    got = pl.pallas_call(
        functools.partial(reduce_kernel, groups, count, subs, plain),
        out_shape=tuple(out + land),
        in_specs=[any_] * n,
        out_specs=(any_,) * (2 * n),
        scratch_shapes=part + held + line + line + load + [
            dma((n, count)), dma((2, 2)), dma((n,)), dma((n, max(subs), count)),
            dma((units,)), dma((units,)), dma((units,)), dma((units,)), dma((units,)),
            dma((units,)), dma((units,)), dma((units,)), dma((n,)),
        ],
        compiler_params=pltpu.CompilerParams(
            collective_id=2, has_side_effects=True, vmem_limit_bytes=60 * 1024 * 1024
        ),
        cost_estimate=pl.CostEstimate(flops=0, bytes_accessed=200_000_000, transcendentals=0),
        name="reduce_all",
    )(*terms)
    return got[:n]


def spread_kernel(block, x_ref, o_ref):
    _, count, rows, hidden = x_ref.shape
    for source in range(count):
        for k in range(hidden // block):
            o_ref[:, pl.ds((k * count + source) * block, block)] = x_ref[
                0, source, :, pl.ds(k * block, block)
            ].astype(F32)


def spread(values, block):
    _, count, rows, hidden = values.shape
    step = rows // 4
    return pl.pallas_call(
        functools.partial(spread_kernel, block),
        out_shape=jax.ShapeDtypeStruct((2 * rows, count * hidden), F32),
        grid=(2, rows // step),
        in_specs=[pl.BlockSpec((1, count, step, hidden), lambda h, i: (h, 0, i, 0))],
        out_specs=pl.BlockSpec((step, count * hidden), lambda h, i: (h * (rows // step) + i, 0)),
        name="spread",
    )(values)


def shards(
    groups,
    count,
    tokens,
    cotangent,
    lengths,
    dealing,
    first_gain,
    first_shift,
    query_weight,
    query_bias,
    keyval_weight,
    value_bias,
    out_weight,
    out_bias,
    second_gain,
    second_shift,
    up_weight,
    up_bias,
    down_weight,
    down_bias,
):
    both = ("grp", "shard")
    micro, length, width = tokens.shape
    group_rows = dealing.shape[0]
    group = lax.axis_index("grp")
    me = lax.axis_index("shard")
    half = micro // 2
    block = down_weight.shape[0]
    hidden = block * groups
    rows = micro * length

    local_deal = dealing - group * group_rows
    steps = jnp.arange(group_rows, dtype=jnp.int32)
    inverse = jnp.sum(jnp.where(local_deal[:, None] == steps[None, :], steps[:, None], 0), axis=0)
    pick = lambda table, at: lax.dynamic_index_in_dim(table, at, 0, keepdims=False)

    small = (
        first_gain, first_shift, query_bias, value_bias, out_bias,
        second_gain, second_shift, up_bias, down_bias,
    )
    up_rows = up_weight.shape[0]
    beside = jnp.concatenate(small)
    beside = jnp.pad(beside, (0, up_rows * 128 - beside.shape[0])).reshape(up_rows, 128)
    keyval_wide = jnp.concatenate([keyval_weight, beside], axis=1)
    up_cut = up_weight.reshape(up_rows, groups, count, block).transpose(2, 0, 1, 3)
    up_cut = up_cut.reshape(count, up_rows, hidden)
    weight_query, weight_out, keyval_all, weight_up = gather_all(
        groups, count, query_weight, out_weight, keyval_wide, up_cut
    )
    weight_query, weight_out, keyval_all, weight_up, down_weight, cotangent = lax.optimization_barrier(
        (weight_query, weight_out, keyval_all, weight_up, down_weight, cotangent)
    )
    weight_down = lax.all_gather(down_weight, "grp", axis=0, tiled=True)
    weight_keyval = keyval_all[:, : 2 * HD]
    packed = keyval_all[:, 2 * HD :].reshape(groups * count, up_rows * 128)
    wide = []
    at = 0
    for item in small:
        wide.append(packed[:, at : at + item.shape[0]].astype(F32))
        at += item.shape[0]
    up_part = pick(wide[7].reshape(groups, count, block).swapaxes(0, 1), me).reshape(hidden)
    gain_one, shift_one, bias_query, bias_value, bias_out, gain_two, shift_two, _, bias_down = [
        item.reshape(-1) for item in wide
    ]

    def gather_rows(values, place_of):
        held = cube_gather((values[:half], values[half:]), count, "shard")
        out = jnp.zeros((group_rows, length, width), values.dtype)
        for q in range(count):
            for k in range(2):
                for i in range(half):
                    row = (me ^ q) * micro + k * half + i
                    out = lax.dynamic_update_slice(out, held[k][q][i][None], (place_of(row), 0, 0))
        return out.reshape(group_rows * length, width)

    def scatter_rows(values, place_of):
        blocks = []
        for k in range(2):
            terms = {}
            for q in range(count):
                terms[q] = jnp.stack(
                    [pick(values, place_of((me ^ q) * micro + k * half + i)) for i in range(half)]
                )
            blocks.append(terms)
        return jnp.concatenate(cube_scatter(blocks, count, "shard"))

    dealt_place = lambda row: pick(inverse, row)
    same_place = lambda row: row

    cot_rows = gather_rows(cotangent, same_place).reshape(group_rows, length, width)
    dealt_live = jnp.stack([live(pick(lengths, local_deal[j]), length) for j in range(group_rows)])
    grad_down = (cot_rows.astype(F32) * dealt_live[:, :, None]).astype(BF)
    own_live = jnp.stack([pick(dealt_live, me * micro + m) for m in range(micro)])

    scale = HD**-0.5
    own_lengths = [pick(lengths, me * micro + m) for m in range(micro)]
    inputs = tokens.astype(F32).reshape(rows, width)
    unit_one, rate_one = normalize(inputs)
    normed_one = (unit_one * gain_one + shift_one).astype(BF)
    queries = (mm(normed_one, weight_query) + bias_query).astype(BF)
    value_pad = jnp.concatenate([jnp.zeros((HD,), F32), bias_value])
    keyvals = (mm(normed_one, weight_keyval) + value_pad).astype(BF)
    kept = []
    attended = []
    for m in range(micro):
        mask = jnp.repeat(allowed_pairs(own_lengths[m], length), HEADS, axis=0)
        query_rows = queries[m * length : (m + 1) * length].reshape(length * HEADS, HD)
        key_rows = keyvals[m * length : (m + 1) * length, :HD]
        value_rows = keyvals[m * length : (m + 1) * length, HD:]
        scores = jnp.where(mask, mm_nt(query_rows, key_rows) * scale, NEGATIVE)
        top = jnp.max(scores, axis=1, keepdims=True)
        powers = jnp.exp(scores - top)
        totals = jnp.sum(powers, axis=1, keepdims=True)
        probs = powers / totals
        probs_low = probs.astype(BF)
        attended.append(mm(probs_low, value_rows).reshape(length, width).astype(BF))
        kept.append((mask, query_rows, key_rows, value_rows, top + jnp.log(totals), probs_low))
    attended = jnp.concatenate(attended)
    middle = inputs + mm(attended, weight_out) + bias_out
    unit_two, rate_two = normalize(middle)
    normed_two_own = (unit_two * gain_two + shift_two).astype(BF)

    normed_two = gather_rows(normed_two_own.reshape(micro, length, width), dealt_place)
    hidden_pre = mm(normed_two, weight_up) + up_part
    gelu_tanh = partial(jax.nn.gelu, approximate=True)
    activated_wide, gelu_pull = jax.vjp(gelu_tanh, hidden_pre)
    activated = activated_wide.astype(BF)
    grad_down = grad_down.reshape(group_rows * length, width)
    grad_hidden = gelu_pull(mm_nt(grad_down, weight_down))[0].astype(BF)
    grad_two = mm_nt(grad_hidden, weight_up).astype(BF).reshape(group_rows, length, width)
    grad_normed_two = scatter_rows(grad_two, dealt_place).astype(F32).reshape(rows, width)
    down_grad = mm_tn(activated, grad_down).astype(BF)
    up_grad = mm_tn(normed_two, grad_hidden).astype(BF)

    result = mm(activated, weight_down).astype(BF).reshape(group_rows, length, width)
    middle_rows = middle.reshape(micro, length, width)
    for m in range(micro):
        at = dealt_place(me * micro + m)
        row = (pick(result, at).astype(F32) + middle_rows[m]).astype(BF)
        result = lax.dynamic_update_slice(result, row[None], (at, 0, 0))
    result = scatter_rows(result, same_place).astype(F32)
    block_output = ((result + bias_down) * own_live[:, :, None]).astype(BF)

    own_cot = jnp.stack([pick(cot_rows, dealt_place(me * micro + m)) for m in range(micro)])
    given_live = jnp.stack([live(own_lengths[m], length) for m in range(micro)])
    grad_out = (own_cot.astype(F32) * given_live[:, :, None]).reshape(rows, width)
    down_bias_grad = jnp.sum(grad_out.astype(BF).astype(F32), axis=0)
    back_two, gain_two_grad, shift_two_grad = norm_back(grad_normed_two, unit_two, rate_two, gain_two)
    grad_middle = back_two + grad_out
    grad_branch = grad_middle.astype(BF)
    out_bias_grad = jnp.sum(grad_branch.astype(F32), axis=0)
    out_grad = mm_tn(attended, grad_branch).astype(BF)
    grad_attended = mm_nt(grad_branch, weight_out).astype(BF)
    grad_queries = []
    grad_keyvals = []
    for m in range(micro):
        mask, query_rows, key_rows, value_rows, log_total, probs_low = kept[m]
        grad_rows = grad_attended[m * length : (m + 1) * length].reshape(length * HEADS, HD)
        again = jnp.where(mask, mm_nt(query_rows, key_rows) * scale, NEGATIVE)
        probs = jnp.exp(again - log_total)
        grad_probs = mm_nt(grad_rows, value_rows)
        centre = jnp.sum(probs * grad_probs, axis=1, keepdims=True)
        grad_scores = (probs * (grad_probs - centre)).astype(BF)
        grad_queries.append((mm(grad_scores, key_rows) * scale).reshape(length, width).astype(BF))
        grad_keys = mm_tn(grad_scores, query_rows) * scale
        grad_values = mm_tn(probs_low, grad_rows)
        grad_keyvals.append(jnp.concatenate([grad_keys, grad_values], axis=1).astype(BF))
    grad_queries = jnp.concatenate(grad_queries)
    grad_keyvals = jnp.concatenate(grad_keyvals)
    query_grad = mm_tn(normed_one, grad_queries).astype(BF)
    keyval_grad = mm_tn(normed_one, grad_keyvals).astype(BF)
    grad_normed_one = mm_nt(grad_queries, weight_query) + mm_nt(grad_keyvals, weight_keyval)
    back_one, gain_one_grad, shift_one_grad = norm_back(grad_normed_one, unit_one, rate_one, gain_one)
    input_grad = (back_one + grad_middle).astype(BF).reshape(micro, length, width)

    up_bias_part = jnp.sum(grad_hidden.astype(F32), axis=0).reshape(groups, 1, block)
    value_bias_grad = jnp.sum(grad_keyvals[:, HD:].astype(F32), axis=0)
    query_bias_grad = jnp.sum(grad_queries.astype(F32), axis=0)
    spot = (jnp.arange(count, dtype=jnp.int32) == me)[None, :, None]
    up_bias_grad = jnp.where(spot, up_bias_part, 0.0).reshape(-1)
    vectors = (
        gain_one_grad, shift_one_grad, query_bias_grad, value_bias_grad, out_bias_grad,
        gain_two_grad, shift_two_grad, up_bias_grad, down_bias_grad,
    )
    line = jnp.concatenate([item.reshape(count, -1) for item in vectors], axis=1).astype(BF)
    unit = 2 * 16 * 2 * HD
    more = -(-line.shape[1] // unit)
    line = jnp.pad(line, ((0, 0), (0, more * unit - line.shape[1])))
    line = line.reshape(count, 2, more * 16, 2 * HD)

    cut = lambda x: x.reshape(count, 2, x.shape[0] // count // 2, x.shape[1])
    terms = [cut(x) for x in (down_grad, up_grad, out_grad, query_grad, keyval_grad)]
    terms[4] = jnp.concatenate([terms[4], line], axis=2)
    down_full, up_full, out_full, query_full, last = reduce_all(
        groups, count, terms, (True, True, False, False, False), (2, 2, 2, 2, 1)
    )
    down_full = down_full.reshape(-1, width).astype(F32)
    up_full = spread(up_full, block)
    out_full = out_full.reshape(-1, width).astype(F32)
    query_full = query_full.reshape(-1, width).astype(F32)
    tall = width // count // 2
    keyval_full = last[:, 0, :tall].reshape(2 * tall, 2 * HD).astype(F32)
    summed = last[:, 0, tall:].reshape(-1).astype(F32)
    parts = []
    at = 0
    for item in vectors:
        size = item.shape[0] // count
        parts.append(summed[at : at + size])
        at += size

    return (
        block_output, input_grad, parts[0], parts[1], query_full, parts[2], keyval_full, parts[3],
        out_full, parts[4], parts[5], parts[6], up_full, parts[7], down_full, parts[8],
    )


def solution(mesh):
    rows = P(("grp", "shard"), None, None)
    flat = P(("grp", "shard"))
    tall = P(("grp", "shard"), None)
    vector, matrix = P("shard"), P("shard", None)
    return jax.shard_map(
        partial(shards, mesh.shape["grp"], mesh.shape["shard"]),
        mesh=mesh,
        in_specs=(
            rows, rows, P("grp", None), P("grp"), flat, flat, tall, flat, tall, flat,
            tall, flat, flat, flat, tall, flat, tall, flat,
        ),
        out_specs=(
            rows, rows, vector, vector, matrix, vector, matrix, vector,
            matrix, vector, vector, vector, matrix, vector, matrix, vector,
        ),
        check_vma=False,
    )
```

```python
from functools import partial

import jax
import jax.numpy as jnp
from jax import lax
from jax.experimental import pallas as pl
from jax.experimental.pallas import tpu as pltpu
from jax.sharding import PartitionSpec as P

HEADS = 16
HD = 128
EPS = 1e-05
NEGATIVE = -1e30
BF = jnp.bfloat16
F32 = jnp.float32
MESH = pl.DeviceIdType.MESH
LAG_MID = 2
LAG_OUT = 4
NORM_STEP = 4
RING = 6


def mm(left, right):
    return jnp.dot(left, right, preferred_element_type=F32)


def mm_tn(left, right):
    return lax.dot_general(left, right, (((0,), (0,)), ((), ())), preferred_element_type=F32)


def mm_nt(left, right):
    return lax.dot_general(left, right, (((1,), (1,)), ((), ())), preferred_element_type=F32)


def normalize(values):
    centre = jnp.mean(values, axis=-1, keepdims=True)
    offset = values - centre
    spread = jnp.mean(offset * offset, axis=-1, keepdims=True)
    rate = lax.rsqrt(spread + EPS)
    return offset * rate, rate


def row_ends(lengths_row):
    docs = lengths_row.shape[0]
    at = jnp.arange(docs, dtype=jnp.int32)
    return jnp.sum(jnp.where(at[None, :] <= at[:, None], lengths_row[None, :], 0), axis=1)


def live(lengths_row, length):
    places = jnp.arange(length, dtype=jnp.int32)
    return (places < jnp.sum(lengths_row)).astype(F32)


def allowed_pairs(lengths_row, length):
    ends = row_ends(lengths_row)
    places = jnp.arange(length, dtype=jnp.int32)
    segment = jnp.sum((places[:, None] >= ends[None, :]).astype(jnp.int32), axis=1)
    return (segment[:, None] == segment[None, :]) & (places[None, :] <= places[:, None])


def flips(count, mask):
    return [(i, i ^ mask) for i in range(count)]


def cube_orders(count):
    order = list(range(count.bit_length() - 1))
    return order, order[::-1]


def cube_gather(halves, count, axis):
    orders = cube_orders(count)
    held = [{0: half} for half in halves]
    for step in range(len(orders[0])):
        for k in range(2):
            mask = 1 << orders[k][step]
            keys = sorted(held[k])
            pack = jnp.stack([held[k][q] for q in keys])
            got = lax.ppermute(pack, axis, flips(count, mask))
            for i, q in enumerate(keys):
                held[k][q ^ mask] = got[i]
    return held


def near_first(count):
    return sorted(range(1, count), key=lambda q: (bin(q).count("1"), q))


def cube_tree(count, parity, q):
    order = list(range(count.bit_length() - 1))
    if parity:
        order = order[::-1]
    at = max([i for i, d in enumerate(order) if q >> d & 1], default=-1)
    return [1 << d for d in order[at + 1 :]]


def near_first(count):
    return sorted(range(1, count), key=lambda q: (bin(q).count("1"), q))


def gather_kernel(
    groups, count, wq, wo, kvs, upc, q_all, o_all, kvs_all, up_all,
    zs, zr, ps, pr, bs, br, us, ur, loc,
):
    chips = groups // 2
    g, me = lax.axis_index("grp"), lax.axis_index("shard")
    p, c = lax.div(g, 2), lax.rem(g, 2)

    barrier = pltpu.get_barrier_semaphore()

    def greet(target):
        pl.semaphore_signal(barrier, inc=1, device_id=target, device_id_type=MESH)

    greet((g + 1 - 2 * c, me))
    for q in range(1, count):
        greet((g, lax.bitwise_xor(me, q)))

    @pl.when(p < chips - 1)
    def _():
        greet((g + 2, me))

    @pl.when(p > 0)
    def _():
        greet((g - 2, me))

    ends = (p == 0).astype(jnp.int32) + (p == chips - 1).astype(jnp.int32)
    pl.semaphore_wait(barrier, count + 2 - ends)

    def send(src, dst, send_sem, recv_sem, target):
        pltpu.make_async_remote_copy(
            src_ref=src, dst_ref=dst, send_sem=send_sem, recv_sem=recv_sem,
            device_id=target, device_id_type=MESH,
        ).start()

    def wait(ref, sem):
        pltpu.make_async_copy(ref, ref, sem).wait()

    own = (wq, wo, kvs)
    whole = (q_all, o_all, kvs_all)
    parity = (0, 1, 0)
    size = wq.shape[0]
    up_size = upc.shape[1]
    up_half = up_size * count // 2

    def spot(a, z, col):
        if a < 3:
            at = ((z * 2 + c) * count + col) * size
            return whole[a].at[pl.ds(pl.multiple_of(at, 16), size)]
        at = (z * 2 + c) * up_half * 2 + (a - 3) * up_half
        return up_all.at[pl.ds(pl.multiple_of(at, 16), up_half)]

    def along(a, way, hop, src, z):
        step = 1 - 2 * way
        send(src, spot(a, z, me), zs.at[a, way, hop], zr.at[a, way, hop], (g + 2 * step, me))

    def across(a, src, z, q):
        for m in cube_tree(count, parity[a], q):
            send(
                src, spot(a, z, lax.bitwise_xor(me, q)), ps.at[a], pr.at[a, z, q ^ m],
                (g, lax.bitwise_xor(me, m)),
            )

    def aside(a, src, z, q):
        send(src, spot(a, z, lax.bitwise_xor(me, q)), bs.at[a], br.at[a], (g + 1 - 2 * c, me))

    def may_send(way, hop):
        if way == 0:
            return (p >= hop - 1) & (p < chips - 1)
        return (p + hop - 1 <= chips - 1) & (p > 0)

    def may_take(way, hop):
        return p >= hop if way == 0 else p + hop <= chips - 1

    up_rows = lambda col: up_all.at[pl.ds(pl.multiple_of((g * count + col) * up_size, 16), up_size)]
    for q in near_first(count):
        to = lax.bitwise_xor(me, q)
        send(upc.at[to], up_rows(me), us, ur.at[q], (g, to))
    mine = [pltpu.make_async_copy(upc.at[me], up_rows(me), loc.at[3])]
    for a in range(3):
        mine.append(pltpu.make_async_copy(own[a], spot(a, p, me), loc.at[a]))
    for copy in mine:
        copy.start()

    def first(a, src):
        for way in range(2):
            pl.when(may_send(way, 1))(partial(along, a, way, 1, src, p))
        aside(a, src, p, 0)

    for a in range(3):
        first(a, own[a])
        across(a, own[a], p, 0)
    mine[0].wait()
    for q in near_first(count):
        wait(up_rows(me), ur.at[q])
    for a in (3, 4):
        first(a, spot(a, p, me))

    def plane(z):
        for q in near_first(count):
            for a in range(3):
                ref = spot(a, z, lax.bitwise_xor(me, q))
                wait(ref, pr.at[a, z, q])
                across(a, ref, z, q)
                aside(a, ref, z, q)

    def planes(hop):
        if hop == 0:
            plane(p)
            return
        for way in range(2):
            z = p - hop if way == 0 else p + hop
            pl.when(may_take(way, hop))(partial(plane, z))

    def arrive(a, hop):
        for way in range(2):

            @pl.when(may_take(way, hop))
            def _():
                z = p - hop if way == 0 else p + hop
                ref = spot(a, z, me)
                wait(ref, zr.at[a, way, hop])
                if hop + 1 < chips:
                    pl.when(may_send(way, hop + 1))(
                        partial(along, a, way, hop + 1, ref, z)
                    )
                if a < 3:
                    across(a, ref, z, 0)
                aside(a, ref, z, 0)

    for hop in range(1, chips):
        for a in range(3):
            arrive(a, hop)
        planes(hop - 1)
        for a in (3, 4):
            arrive(a, hop)
    planes(chips - 1)

    for copy in mine[1:]:
        copy.wait()
    for a in range(5):
        for way in range(2):
            for hop in range(1, chips):
                pl.when(may_send(way, hop))(
                    partial(wait, spot(a, p, me), zs.at[a, way, hop])
                )
    for a in range(3):
        wait(whole[a].at[pl.ds(0, chips * (count - 1) * size)], ps.at[a])
        wait(whole[a].at[pl.ds(0, chips * count * size)], bs.at[a])
        wait(whole[a].at[pl.ds(0, chips * count * size)], br.at[a])
    for a in (3, 4):
        wait(up_all.at[pl.ds(0, chips * up_half)], bs.at[a])
        wait(up_all.at[pl.ds(0, chips * up_half)], br.at[a])
    wait(up_all.at[pl.ds(0, (count - 1) * up_size)], us)


def gather_all(groups, count, wq, wo, kvs, upc):
    chips = groups // 2
    n = groups * count
    any_ = pl.BlockSpec(memory_space=pl.ANY)
    dma = pltpu.SemaphoreType.DMA
    tall = lambda x: jax.ShapeDtypeStruct((n * x.shape[0], x.shape[1]), x.dtype)
    return pl.pallas_call(
        partial(gather_kernel, groups, count),
        out_shape=(
            tall(wq), tall(wo), tall(kvs),
            jax.ShapeDtypeStruct((n * upc.shape[1], upc.shape[2]), upc.dtype),
        ),
        in_specs=[any_] * 4,
        out_specs=(any_,) * 4,
        scratch_shapes=[
            dma((5, 2, chips)), dma((5, 2, chips)), dma((3,)), dma((3, chips, count)),
            dma((5,)), dma((5,)), dma, dma((count,)), dma((4,)),
        ],
        compiler_params=pltpu.CompilerParams(collective_id=1, has_side_effects=True),
        cost_estimate=pl.CostEstimate(flops=0, bytes_accessed=100_000_000, transcendentals=0),
        name="gather_all",
    )(wq, wo, kvs, upc)


def back_kernel(groups, count, subs, plain, sizes, share, *refs):
    n = len(subs)
    take = iter(refs)
    many = lambda k: [next(take) for _ in range(k)]
    down_term, up_term, slices, wq, wo, middle_far = many(6)
    grad_out, attended, queries, keyvals, normed, tokens, bias, gains, wkv, early = many(10)
    final, land = many(n), many(n)
    input_grad = next(take)
    own_part = {m: next(take) for m in range(n) if share[m] == m}
    part = [own_part[share[m]] for m in range(n)]
    held = many(n)
    ring_of = sorted(set(sizes))
    load, outer, mid = many(len(ring_of)), many(len(ring_of)), many(len(ring_of))
    load = [load[ring_of.index(size)] for size in sizes]
    arrived, middle, grad_mid, branch, grad_q, tiles, stage, stage_kv, grad_kv, sums = many(10)
    sib, ld, sent, came, zs, z_in, z_mid, os, z_fin, xs, xr, loc, ss, gs, gr, ws, ms, free_in, free_mid = take
    chips = groups // 2
    g, me = lax.axis_index("grp"), lax.axis_index("shard")
    p, c = lax.div(g, 2), lax.rem(g, 2)
    low = p < chips // 2
    inn = jnp.where(low, g + 2, g - 2)
    out = jnp.where(low, g - 2, g + 2)
    end = (p == 0) | (p == chips - 1)
    middle_chip = (p == chips // 2 - 1) | (p == chips // 2)
    other = g + 1 - 2 * c
    near = near_first(count)

    barrier = pltpu.get_barrier_semaphore()

    def greet(target):
        pl.semaphore_signal(barrier, inc=1, device_id=target, device_id_type=MESH)

    greet((other, me))
    greet((inn, me))
    for q in range(1, count):
        greet((g, lax.bitwise_xor(me, q)))

    @pl.when(jnp.logical_not(end))
    def _():
        greet((out, me))

    pl.semaphore_wait(barrier, count + 2 - end.astype(jnp.int32))

    def send(src, dst, send_sem, recv_sem, target):
        pltpu.make_async_remote_copy(
            src_ref=src, dst_ref=dst, send_sem=send_sem, recv_sem=recv_sem,
            device_id=target, device_id_type=MESH,
        ).start()

    def wait(ref, sem):
        pltpu.make_async_copy(ref, ref, sem).wait()

    def add(dst, *more):
        @pl.loop(0, dst.shape[0] // 16)
        def _(i):
            at = pl.ds(pl.multiple_of(i * 16, 16), 16)
            total = dst[at].astype(F32)
            for ref in more:
                total = total + ref[at].astype(F32)
            dst[at] = total.astype(BF)

    cut = lambda m, j: pl.ds(j * sizes[m][0], sizes[m][0])
    away = lambda q: lax.bitwise_xor(me, q)

    given = (down_term, up_term)
    for m in range(2):
        for q in near + [0]:
            send(given[m].at[away(q), 1 - c], land[m].at[q], ss.at[m, q], sib.at[m, q], (other, me))
    own_slice = pltpu.make_async_copy(slices.at[me], arrived.at[0], gr.at[0])
    own_slice.start()
    middle_copy = pltpu.make_async_copy(middle_far, middle, ms)
    middle_copy.start()

    def send_slices():
        for q in near:
            send(slices.at[away(q)], arrived.at[q], gs.at[q], gr.at[q], (g, away(q)))

    pair_tasks = [[(m, j, q) for j in range(subs[m]) for q in near + [0]] for m in range(n)]
    flat = [task for tasks in pair_tasks for task in tasks]

    def spot(m, q):
        return part[m].at[q - 1] if q else held[m].at[me]

    def loads(k):
        m, j, q = flat[k]
        slot = k % 2
        copies = [pltpu.make_async_copy(land[m].at[q, cut(m, j)], load[m].at[slot], ld.at[slot, 1])]
        if m < 2:
            place = spot(m, q).at[cut(m, j)]
            copies.append(pltpu.make_async_copy(given[m].at[away(q), c, cut(m, j)], place, ld.at[slot, 0]))
        return copies

    def begin(k):
        m, j, q = flat[k]
        if j == 0:
            wait(land[m].at[q], sib.at[m, q])
        for copy in loads(k):
            copy.start()

    def pair(k):
        m, j, q = flat[k]
        if k == 0 or flat[k - 1][0] != m:
            begin(k)
        if k + 1 < len(flat) and flat[k + 1][0] == m:
            begin(k + 1)
        for copy in loads(k):
            copy.wait()
        ref = spot(m, q).at[cut(m, j)]
        add(ref, load[m].at[k % 2])
        if q:
            send(ref, held[m].at[me, cut(m, j)], sent.at[m], came.at[m, j, q], (g, away(q)))

    units = []
    for m in range(n):
        for j in range(subs[m]):
            units += [(m, j, q) for q in range(count)] if plain[m] else [(m, j, 0)]
    rings = [ring_of.index(sizes[m]) for m, j, q in units]
    index = [rings[:u].count(rings[u]) for u in range(len(units))]
    total_in = [rings.count(r) for r in range(len(ring_of))]
    slot_of = lambda u: index[u] % outer[rings[u]].shape[0]
    reused = lambda u: index[u] >= outer[rings[u]].shape[0]
    again = lambda u: index[u] + outer[rings[u]].shape[0] < total_in[rings[u]]

    def value(u):
        m, j, q = units[u]
        return held[m].at[away(q), cut(m, j)]

    def result(u, half):
        m, j, q = units[u]
        return final[m].at[half, away(q) if plain[m] else 0, cut(m, j)]

    def inward(u):
        m, j, q = units[u]
        ref = value(u)
        if plain[m]:
            if q:
                wait(ref, came.at[m, j, q])
        else:
            others = [held[m].at[away(r), cut(m, j)] for r in near]
            for r, other_ref in zip(near, others):
                wait(other_ref, came.at[m, j, r])
            add(ref, *others)
        box, slot = rings[u], slot_of(u)

        @pl.when(jnp.logical_not(end))
        def _():
            wait(outer[box].at[slot], z_in.at[u])
            add(ref, outer[box].at[slot])
            if again(u):
                pl.semaphore_signal(free_in.at[box, slot], inc=1, device_id=(out, me), device_id_type=MESH)

        @pl.when(middle_chip)
        def _():
            if reused(u):
                pl.semaphore_wait(free_mid.at[box, slot], 1)
            send(ref, mid[box].at[slot], zs.at[u], z_mid.at[u], (inn, me))

        @pl.when(jnp.logical_not(middle_chip))
        def _():
            if reused(u):
                pl.semaphore_wait(free_in.at[box, slot], 1)
            send(ref, outer[box].at[slot], zs.at[u], z_in.at[u], (inn, me))

    def centre(u):
        box, slot = rings[u], slot_of(u)

        @pl.when(middle_chip)
        def _():
            ref = value(u)
            wait(ref, zs.at[u])
            wait(mid[box].at[slot], z_mid.at[u])
            add(ref, mid[box].at[slot])
            if again(u):
                pl.semaphore_signal(free_mid.at[box, slot], inc=1, device_id=(inn, me), device_id_type=MESH)
            pl.when(jnp.logical_not(end))(
                lambda: send(ref, result(u, c), os.at[u], z_fin.at[u], (out, me))
            )
            send(ref, result(u, c), xs.at[u], xr.at[u], (other, me))
            pltpu.make_async_copy(ref, result(u, c), loc.at[u]).start()

    def outward(u):
        @pl.when(jnp.logical_not(middle_chip))
        def _():
            ref = result(u, c)
            wait(ref, z_fin.at[u])
            pl.when(jnp.logical_not(end))(
                lambda: send(ref, ref, os.at[u], z_fin.at[u], (out, me))
            )
            send(ref, ref, xs.at[u], xr.at[u], (other, me))

    rows, width = attended.shape
    length = bias.shape[1]
    scale = HD**-0.5
    band = 32
    column = lambda at, size: pl.ds(pl.multiple_of(at, 128), size)

    def moments(x):
        centre_ = jnp.mean(x, axis=1, keepdims=True)
        offset = x - centre_
        rate = lax.rsqrt(jnp.mean(offset * offset, axis=1, keepdims=True) + EPS)
        return offset * rate, rate

    def clear():
        sums[...] = jnp.zeros_like(sums)
        grad_kv[...] = jnp.zeros_like(grad_kv)

    def tally(k, x):
        sums[k : k + 1, :] += jnp.sum(x, axis=0, keepdims=True)

    def second_norm(lo, hi):
        gain = gains[1:2, :]

        @pl.loop(lo, hi)
        def _(i):
            at = pl.ds(pl.multiple_of(i * band, band), band)
            grad = arrived[0, at, :].astype(F32)
            for q in range(1, count):
                grad = grad + arrived[q, at, :].astype(F32)
            unit, rate = moments(middle[at, :])
            tally(0, grad * unit)
            tally(1, grad)
            e = grad * gain
            back = rate * (
                e - jnp.mean(e, axis=1, keepdims=True) - unit * jnp.mean(e * unit, axis=1, keepdims=True)
            )
            whole = back + grad_out[at, :].astype(F32)
            grad_mid[at, :] = whole
            short = whole.astype(BF)
            branch[at, :] = short
            tally(2, short.astype(F32))

    def first_norm(lo, hi):
        gain = gains[0:1, :]

        @pl.loop(lo, hi)
        def _(i):
            at = pl.ds(pl.multiple_of(i * band, band), band)
            grad = middle[at, :]
            unit, rate = moments(tokens[at, :].astype(F32))
            tally(3, grad * unit)
            tally(4, grad)
            e = grad * gain
            back = rate * (
                e - jnp.mean(e, axis=1, keepdims=True) - unit * jnp.mean(e * unit, axis=1, keepdims=True)
            )
            input_grad[at, :] = (back + grad_mid[at, :]).astype(BF)
            tally(5, grad_q[at, :].astype(F32))

    part_cols = min(512, width)

    def outer_product(dst, left, start, size, right):
        lhs = left[:, column(start, size)]

        @pl.loop(0, right.shape[1] // min(part_cols, right.shape[1]))
        def _(k):
            cols = column(k * min(part_cols, right.shape[1]), min(part_cols, right.shape[1]))
            dst[:, cols] = lax.dot_general(
                lhs, right[:, cols], (((0,), (0,)), ((), ())), preferred_element_type=F32
            ).astype(BF)

    staged = []

    def weight_terms(m, left, right, some):
        size = width // count // 2
        for q in some:
            k = len(staged)
            if k >= 2:
                wait(stage.at[k % 2], ss.at[staged[k - 2][0], staged[k - 2][1]])
            outer_product(stage.at[k % 2], left, (away(q) * 2 + 1 - c) * size, size, right)
            send(stage.at[k % 2], land[m].at[q], ss.at[m, q], sib.at[m, q], (other, me))
            staged.append((m, q))
            outer_product(spot(m, q), left, (away(q) * 2 + c) * size, size, right)

    tile_rows = tiles.shape[1]
    tile_count = width // tile_rows

    def weight_tile(source, i):
        at = pl.multiple_of(i * tile_rows, tile_rows)
        slot = lax.rem(i, 2)
        return pltpu.make_async_copy(source.at[pl.ds(at, tile_rows)], tiles.at[slot], ws.at[slot])

    def attention_tiles(lo, hi):
        @pl.loop(lo, hi)
        def _(i):
            pl.when(i + 1 < tile_count)(lambda: weight_tile(wo, i + 1).start())
            weight_tile(wo, i).wait()
            cols = column(i * tile_rows, tile_rows)
            grad_att = lax.dot_general(
                branch[...], tiles[lax.rem(i, 2)], (((1,), (1,)), ((), ())), preferred_element_type=F32
            ).astype(BF)
            query = queries[:, cols]
            heads = tile_rows // HD
            fold = lambda x: jnp.concatenate([x[:, h * HD : (h + 1) * HD] for h in range(heads)], axis=0)
            for m in range(rows // length):
                at = pl.ds(m * length, length)
                q = fold(query[m * length : (m + 1) * length])
                ga = fold(grad_att[m * length : (m + 1) * length])
                k, v = keyvals[at, :HD], keyvals[at, HD:]
                shut = jnp.concatenate([bias[at, :]] * heads, axis=0)
                s = lax.dot_general(q, k, (((1,), (1,)), ((), ())), preferred_element_type=F32) * scale + shut
                e = jnp.exp(s - jnp.max(s, axis=1, keepdims=True))
                probs = e / jnp.sum(e, axis=1, keepdims=True)
                gp = lax.dot_general(ga, v, (((1,), (1,)), ((), ())), preferred_element_type=F32)
                ds = (probs * (gp - jnp.sum(probs * gp, axis=1, keepdims=True))).astype(BF)
                dq = (jnp.dot(ds, k, preferred_element_type=F32) * scale).astype(BF)
                for h in range(heads):
                    grad_q[at, column(i * tile_rows + h * HD, HD)] = dq[h * length : (h + 1) * length]
                tn = (((0,), (0,)), ((), ()))
                dk = lax.dot_general(ds, q, tn, preferred_element_type=F32) * scale
                dv = lax.dot_general(probs.astype(BF), ga, tn, preferred_element_type=F32)
                grad_kv[at, :HD] += dk
                grad_kv[at, HD:] += dv

    def query_tiles(lo, hi):
        low_kv = grad_kv[...].astype(BF)

        @pl.loop(lo, hi)
        def _(i):
            pl.when(i + 1 < tile_count)(lambda: weight_tile(wq, i + 1).start())
            weight_tile(wq, i).wait()
            cols = column(i * tile_rows, tile_rows)
            nt = (((1,), (1,)), ((), ()))
            middle[:, cols] = lax.dot_general(
                grad_q[...], tiles[lax.rem(i, 2)], nt, preferred_element_type=F32
            ) + lax.dot_general(
                low_kv, wkv[pl.ds(pl.multiple_of(i * tile_rows, tile_rows), tile_rows)], nt,
                preferred_element_type=F32,
            )

    def keyval_terms():
        low_kv = grad_kv[...].astype(BF)
        size = width // count // 2
        last = n - 1
        line = jnp.sum(low_kv[:, HD:].astype(F32), axis=0, keepdims=True)
        for k in range(width // size):
            sums[6:7, k * size : k * size + HD] = line
        for q in near + [0]:
            for ref, which in ((stage_kv.at[q], 1 - c), (spot(last, q), c)):
                start = (away(q) * 2 + which) * size
                ref[pl.ds(0, size), :] = lax.dot_general(
                    normed[:, column(start, size)], low_kv, (((0,), (0,)), ((), ())),
                    preferred_element_type=F32,
                ).astype(BF)
                ref[pl.ds(size, 16), :] = jnp.zeros((16, 2 * HD), BF)
                ref[pl.ds(size, 16), :size] = sums[:, column(start, size)].astype(BF)
                ref[pl.ds(size + 16, early.shape[2]), :] = early[away(q), which]
            send(stage_kv.at[q], land[last].at[q], ss.at[last, q], sib.at[last, q], (other, me))

    def reuse(m):
        if share[m] != m:
            wait(part[m], sent.at[share[m]])

    bands = rows // band
    plan = {}

    def at_step(step, *work):
        plan.setdefault(step, []).extend(work)

    P_ = partial
    starts = [sum(len(t) for t in pair_tasks[:m]) for m in range(n)]
    pairs_ = lambda m, lo, hi: [P_(pair, starts[m] + k) for k in range(lo, min(hi, len(pair_tasks[m])))]
    per = len(pair_tasks[1])
    for s in range(4):
        at_step(s, *pairs_(1, s * per // 4, (s + 1) * per // 4))

    def got_slices():
        clear()
        middle_copy.wait()
        own_slice.wait()
        for q in near:
            wait(arrived.at[q], gr.at[q])

    order = near + [0]
    half = len(order) // 2
    at_step(NORM_STEP, got_slices, P_(second_norm, 0, bands // 2))
    at_step(NORM_STEP + 1, P_(second_norm, bands // 2, bands), lambda: weight_tile(wo, 0).start(), P_(reuse, 2))
    at_step(NORM_STEP + 2, P_(weight_terms, 2, attended, branch, order[:half]))
    at_step(NORM_STEP + 3, P_(weight_terms, 2, attended, branch, order[half:]))
    for k in range(4):
        at_step(NORM_STEP + 4 + k, P_(attention_tiles, k * tile_count // 4, (k + 1) * tile_count // 4))
    per = len(pair_tasks[2])
    at_step(NORM_STEP + 5, *pairs_(2, 0, per // 2))
    at_step(NORM_STEP + 6, *pairs_(2, per // 2, per))
    at_step(NORM_STEP + 7, lambda: weight_tile(wq, 0).start(), P_(reuse, 3))
    at_step(NORM_STEP + 8, P_(weight_terms, 3, normed, grad_q, order[:half]))
    at_step(NORM_STEP + 9, P_(weight_terms, 3, normed, grad_q, order[half:]))
    at_step(NORM_STEP + 10, P_(query_tiles, 0, tile_count // 2), *pairs_(3, 0, per // 2))
    at_step(NORM_STEP + 11, P_(query_tiles, tile_count // 2, tile_count), *pairs_(3, per // 2, per))
    at_step(NORM_STEP + 12, P_(first_norm, 0, bands // 2))
    at_step(NORM_STEP + 13, P_(first_norm, bands // 2, bands), keyval_terms)
    at_step(NORM_STEP + 14, *pairs_(4, 0, 99))

    per = len(pair_tasks[0])
    for work in pairs_(0, 0, per // 2):
        work()
    send_slices()
    for work in pairs_(0, per // 2, per):
        work()
    steps = max(len(units) + LAG_OUT, max(plan) + 1)
    for step in range(steps):
        if step < len(units):
            inward(step)
        if 0 <= step - LAG_MID < len(units):
            centre(step - LAG_MID)
        if 0 <= step - LAG_OUT < len(units):
            outward(step - LAG_OUT)
        for work in plan.get(step, ()):
            work()

    for m in range(n):
        if m not in share[m + 1 :]:
            wait(part[m], sent.at[m])
        for q in near + [0]:
            if m < 2 or m == n - 1 or (m, q) in staged[-2:]:
                wait(land[m].at[q], ss.at[m, q])
    for q in near:
        wait(arrived.at[q], gs.at[q])
    for u in range(len(units)):
        wait(result(u, 1 - c), xr.at[u])
        wait(result(u, c), xs.at[u])
        pl.when(jnp.logical_not(end))(partial(wait, result(u, c), os.at[u]))
        pl.when(middle_chip)(partial(wait, result(u, c), loc.at[u]))
        pl.when(jnp.logical_not(middle_chip))(partial(wait, value(u), zs.at[u]))


def back_all(groups, count, given, far, near_by, early):
    rows, width = near_by[0].shape
    size = width // count // 2
    low = (size + 16 + early.shape[2], 2 * HD)
    shapes = [x.shape[2:] for x in given] + [(size, width), (size, width), low]
    plain, subs = (True, True, False, False, False), (2, 2, 2, 2, 1)
    n = len(shapes)
    sizes = [(s[0] // k, s[1]) for s, k in zip(shapes, subs)]
    share = list(range(n))
    for m in (2, 3):
        if shapes[m] == shapes[m - 2]:
            share[m] = m - 2
    rings = sorted(set(sizes))
    units = sum(s * (count if f else 1) for s, f in zip(subs, plain))
    slots = [min(RING, sum(s * (count if f else 1) for s, f, z in zip(subs, plain, sizes) if z == r)) for r in rings]
    any_, vmem = pl.BlockSpec(memory_space=pl.ANY), pl.BlockSpec(memory_space=pltpu.VMEM)
    dma, regular = pltpu.SemaphoreType.DMA, pltpu.SemaphoreType.REGULAR
    out = [jax.ShapeDtypeStruct((2, count if f else 1) + s, BF) for s, f in zip(shapes, plain)]
    out += [jax.ShapeDtypeStruct((count,) + s, BF) for s in shapes]
    tile = 2 * HD
    scratch = [pltpu.VMEM((count - 1,) + shapes[m], BF) for m in range(n) if share[m] == m]
    scratch += [pltpu.VMEM((count,) + s, BF) for s in shapes]
    scratch += [pltpu.VMEM((2,) + r, BF) for r in rings]
    scratch += [pltpu.VMEM((k,) + r, BF) for k, r in zip(slots, rings)] * 2
    scratch += [
        pltpu.VMEM((count, rows, width), BF), pltpu.VMEM((rows, width), F32), pltpu.VMEM((rows, width), F32),
        pltpu.VMEM((rows, width), BF), pltpu.VMEM((rows, width), BF), pltpu.VMEM((2, tile, width), BF),
        pltpu.VMEM((2, size, width), BF), pltpu.VMEM((count,) + low, BF), pltpu.VMEM((rows, 2 * HD), F32),
        pltpu.VMEM((16, width), F32),
        dma((n, count)), dma((2, 2)), dma((n,)), dma((n, max(subs), count)), dma((units,)), dma((units,)),
        dma((units,)), dma((units,)), dma((units,)), dma((units,)), dma((units,)), dma((units,)),
        dma((n, count)), dma((count,)), dma((count,)), dma((2,)), dma,
        regular((len(rings), max(slots))), regular((len(rings), max(slots))),
    ]
    got = pl.pallas_call(
        partial(back_kernel, groups, count, subs, plain, sizes, share),
        out_shape=tuple(out) + (jax.ShapeDtypeStruct((rows, width), BF),),
        in_specs=[any_] * 6 + [vmem] * 10,
        out_specs=(any_,) * (2 * n) + (vmem,),
        scratch_shapes=scratch,
        compiler_params=pltpu.CompilerParams(
            collective_id=2, has_side_effects=True, vmem_limit_bytes=60 * 1024 * 1024
        ),
        cost_estimate=pl.CostEstimate(flops=0, bytes_accessed=200_000_000, transcendentals=0),
        name="back_all",
    )(*given, *far, *near_by, early)
    return got[:n], got[-1]


def spread_kernel(block, x_ref, o_ref):
    _, count, rows, hidden = x_ref.shape
    for source in range(count):
        for k in range(hidden // block):
            o_ref[:, pl.ds((k * count + source) * block, block)] = x_ref[
                0, source, :, pl.ds(k * block, block)
            ].astype(F32)


def spread(values, block):
    _, count, rows, hidden = values.shape
    step = rows // 4
    return pl.pallas_call(
        partial(spread_kernel, block),
        out_shape=jax.ShapeDtypeStruct((2 * rows, count * hidden), F32),
        grid=(2, rows // step),
        in_specs=[pl.BlockSpec((1, count, step, hidden), lambda h, i: (h, 0, i, 0))],
        out_specs=pl.BlockSpec((step, count * hidden), lambda h, i: (h * (rows // step) + i, 0)),
        name="spread",
    )(values)


def shards(
    groups,
    count,
    tokens,
    cotangent,
    lengths,
    dealing,
    first_gain,
    first_shift,
    query_weight,
    query_bias,
    keyval_weight,
    value_bias,
    out_weight,
    out_bias,
    second_gain,
    second_shift,
    up_weight,
    up_bias,
    down_weight,
    down_bias,
):
    both = ("grp", "shard")
    micro, length, width = tokens.shape
    group_rows = dealing.shape[0]
    group = lax.axis_index("grp")
    me = lax.axis_index("shard")
    half = micro // 2
    block = down_weight.shape[0]
    hidden = block * groups
    rows = micro * length

    local_deal = dealing - group * group_rows
    steps = jnp.arange(group_rows, dtype=jnp.int32)
    inverse = jnp.sum(jnp.where(local_deal[:, None] == steps[None, :], steps[:, None], 0), axis=0)
    pick = lambda table, at: lax.dynamic_index_in_dim(table, at, 0, keepdims=False)

    small = (
        first_gain, first_shift, query_bias, value_bias, out_bias,
        second_gain, second_shift, up_bias, down_bias,
    )
    up_rows = up_weight.shape[0]
    beside = jnp.concatenate(small)
    beside = jnp.pad(beside, (0, up_rows * 128 - beside.shape[0])).reshape(up_rows, 128)
    keyval_wide = jnp.concatenate([keyval_weight, beside], axis=1)
    up_cut = up_weight.reshape(up_rows, groups, count, block).transpose(2, 0, 1, 3)
    up_cut = up_cut.reshape(count, up_rows, hidden)
    weight_query, weight_out, keyval_all, weight_up = gather_all(
        groups, count, query_weight, out_weight, keyval_wide, up_cut
    )
    weight_query, weight_out, keyval_all, weight_up, down_weight, cotangent = lax.optimization_barrier(
        (weight_query, weight_out, keyval_all, weight_up, down_weight, cotangent)
    )
    weight_down = lax.all_gather(down_weight, "grp", axis=0, tiled=True)
    weight_keyval = keyval_all[:, : 2 * HD]
    packed = keyval_all[:, 2 * HD :].reshape(groups * count, up_rows * 128)
    wide = []
    at = 0
    for item in small:
        wide.append(packed[:, at : at + item.shape[0]].astype(F32))
        at += item.shape[0]
    up_part = pick(wide[7].reshape(groups, count, block).swapaxes(0, 1), me).reshape(hidden)
    gain_one, shift_one, bias_query, bias_value, bias_out, gain_two, shift_two, _, bias_down = [
        item.reshape(-1) for item in wide
    ]

    def gather_rows(values, place_of):
        held = cube_gather((values[:half], values[half:]), count, "shard")
        out = jnp.zeros((group_rows, length, width), values.dtype)
        for q in range(count):
            for k in range(2):
                for i in range(half):
                    row = (me ^ q) * micro + k * half + i
                    out = lax.dynamic_update_slice(out, held[k][q][i][None], (place_of(row), 0, 0))
        return out.reshape(group_rows * length, width)

    dealt_place = lambda row: pick(inverse, row)
    same_place = lambda row: row

    cot_rows = gather_rows(cotangent, same_place).reshape(group_rows, length, width)
    dealt_live = jnp.stack([live(pick(lengths, local_deal[j]), length) for j in range(group_rows)])
    grad_down = (cot_rows.astype(F32) * dealt_live[:, :, None]).astype(BF)
    own_live = jnp.stack([pick(dealt_live, me * micro + m) for m in range(micro)])

    scale = HD**-0.5
    own_lengths = [pick(lengths, me * micro + m) for m in range(micro)]
    inputs = tokens.astype(F32).reshape(rows, width)
    unit_one, rate_one = normalize(inputs)
    normed_one = (unit_one * gain_one + shift_one).astype(BF)
    queries = (mm(normed_one, weight_query) + bias_query).astype(BF)
    value_pad = jnp.concatenate([jnp.zeros((HD,), F32), bias_value])
    keyvals = (mm(normed_one, weight_keyval) + value_pad).astype(BF)
    attended = []
    for m in range(micro):
        mask = jnp.repeat(allowed_pairs(own_lengths[m], length), HEADS, axis=0)
        query_rows = queries[m * length : (m + 1) * length].reshape(length * HEADS, HD)
        key_rows = keyvals[m * length : (m + 1) * length, :HD]
        value_rows = keyvals[m * length : (m + 1) * length, HD:]
        scores = jnp.where(mask, mm_nt(query_rows, key_rows) * scale, NEGATIVE)
        top = jnp.max(scores, axis=1, keepdims=True)
        powers = jnp.exp(scores - top)
        totals = jnp.sum(powers, axis=1, keepdims=True)
        probs = powers / totals
        probs_low = probs.astype(BF)
        attended.append(mm(probs_low, value_rows).reshape(length, width).astype(BF))
    attended = jnp.concatenate(attended)
    middle = inputs + mm(attended, weight_out) + bias_out
    unit_two, rate_two = normalize(middle)
    normed_two_own = (unit_two * gain_two + shift_two).astype(BF)

    normed_two = gather_rows(normed_two_own.reshape(micro, length, width), dealt_place)
    hidden_pre = mm(normed_two, weight_up) + up_part
    gelu_tanh = partial(jax.nn.gelu, approximate=True)
    activated_wide, gelu_pull = jax.vjp(gelu_tanh, hidden_pre)
    activated = activated_wide.astype(BF)
    grad_down = grad_down.reshape(group_rows * length, width)
    grad_hidden = gelu_pull(mm_nt(grad_down, weight_down))[0].astype(BF)
    grad_two = mm_nt(grad_hidden, weight_up).astype(BF).reshape(group_rows, length, width)
    slices = jnp.stack([pick(grad_two, inverse[r]) for r in range(group_rows)]).reshape(count, rows, width)
    down_grad = mm_tn(activated, grad_down).astype(BF)
    up_grad = mm_tn(normed_two, grad_hidden).astype(BF)

    result = mm(activated, weight_down).astype(BF).reshape(group_rows, length, width)
    middle_rows = middle.reshape(micro, length, width)
    for m in range(micro):
        at = dealt_place(me * micro + m)
        row = (pick(result, at).astype(F32) + middle_rows[m]).astype(BF)
        result = lax.dynamic_update_slice(result, row[None], (at, 0, 0))
    result = lax.psum_scatter(
        result.reshape(group_rows * length, width), "shard", scatter_dimension=0, tiled=True
    )
    result = result.reshape(micro, length, width).astype(F32)
    block_output = ((result + bias_down) * own_live[:, :, None]).astype(BF)

    own_cot = jnp.stack([pick(cot_rows, dealt_place(me * micro + m)) for m in range(micro)])
    given_live = jnp.stack([live(own_lengths[m], length) for m in range(micro)])
    grad_out = (own_cot.astype(F32) * given_live[:, :, None]).reshape(rows, width).astype(BF)
    per = groups // count
    up_bias_part = jnp.sum(grad_hidden.astype(F32), axis=0).reshape(count, per, 1, block)
    spot = (jnp.arange(count, dtype=jnp.int32) == me)[None, None, :, None]
    up_bias_part = jnp.where(spot, up_bias_part, 0.0).reshape(count, 2, -1)
    down_bias_part = jnp.sum(grad_out.astype(F32), axis=0).reshape(count, 2, -1)
    early = jnp.concatenate([up_bias_part, down_bias_part], axis=2).astype(BF)
    fill = -early.shape[2] % (16 * 2 * HD)
    early = jnp.pad(early, ((0, 0), (0, 0), (0, fill))).reshape(count, 2, -1, 2 * HD)

    bias = jnp.concatenate(
        [jnp.where(allowed_pairs(own_lengths[m], length), 0.0, NEGATIVE) for m in range(micro)]
    )
    gains = jnp.pad(jnp.stack([gain_one, gain_two]), ((0, 6), (0, 0)))
    cut = lambda x: x.reshape(count, 2, x.shape[0] // count // 2, x.shape[1])
    near_by = (
        grad_out, attended, queries, keyvals, normed_one, tokens.reshape(rows, width), bias, gains, weight_keyval,
    )
    full, input_grad = back_all(
        groups, count, (cut(down_grad), cut(up_grad)),
        (slices, weight_query, weight_out, middle), near_by, early,
    )
    input_grad = input_grad.reshape(micro, length, width)

    down_full = full[0].reshape(-1, width).astype(F32)
    up_full = spread(full[1], block)
    out_full = full[2].reshape(-1, width).astype(F32)
    query_full = full[3].reshape(-1, width).astype(F32)
    size = width // count // 2
    last = full[4][:, 0]
    keyval_full = last[:, :size].reshape(2 * size, 2 * HD).astype(F32)
    sums = last[:, size : size + 16, :size].swapaxes(0, 1).reshape(16, 2 * size).astype(F32)
    gain_two_grad, shift_two_grad, out_bias_grad, gain_one_grad, shift_one_grad, query_bias_grad = sums[:6]
    short = value_bias.shape[0] * groups
    value_bias_grad = lax.dynamic_slice(sums[6, :HD], (me * short,), (short,))
    tail = last[:, size + 16 :].reshape(2, -1).astype(F32)
    up_bias_grad = tail[:, : hidden // 2].reshape(-1)
    down_bias_grad = tail[:, hidden // 2 : hidden // 2 + size].reshape(-1)

    return (
        block_output, input_grad, gain_one_grad, shift_one_grad, query_full, query_bias_grad, keyval_full,
        value_bias_grad, out_full, out_bias_grad, gain_two_grad, shift_two_grad, up_full, up_bias_grad,
        down_full, down_bias_grad,
    )


def solution(mesh):
    rows = P(("grp", "shard"), None, None)
    flat = P(("grp", "shard"))
    tall = P(("grp", "shard"), None)
    vector, matrix = P("shard"), P("shard", None)
    return jax.shard_map(
        partial(shards, mesh.shape["grp"], mesh.shape["shard"]),
        mesh=mesh,
        in_specs=(
            rows, rows, P("grp", None), P("grp"), flat, flat, tall, flat, tall, flat,
            tall, flat, flat, flat, tall, flat, tall, flat,
        ),
        out_specs=(
            rows, rows, vector, vector, matrix, vector, matrix, vector,
            matrix, vector, vector, vector, matrix, vector, matrix, vector,
        ),
        check_vma=False,
    )
```

```python
from functools import partial

import jax
import jax.numpy as jnp
from jax import lax
from jax.experimental import pallas as pl
from jax.experimental.pallas import tpu as pltpu
from jax.sharding import PartitionSpec as P

HEADS = 16
HD = 128
EPS = 1e-05
NEGATIVE = -1e30
BF = jnp.bfloat16
F32 = jnp.float32
MESH = pl.DeviceIdType.MESH
LAG_MID = 2
LAG_OUT = 4
NORM_STEP = 5
AHEAD = 4
SLICE_STEP = 1
RING = 6


def mm(left, right):
    return jnp.dot(left, right, preferred_element_type=F32)


def mm_tn(left, right):
    return lax.dot_general(left, right, (((0,), (0,)), ((), ())), preferred_element_type=F32)


def mm_nt(left, right):
    return lax.dot_general(left, right, (((1,), (1,)), ((), ())), preferred_element_type=F32)


def near_first(count):
    return sorted(range(1, count), key=lambda q: (bin(q).count("1"), q))


def cube_tree(count, parity, q):
    order = list(range(count.bit_length() - 1))
    if parity:
        order = order[::-1]
    at = max([i for i, d in enumerate(order) if q >> d & 1], default=-1)
    return [1 << d for d in order[at + 1 :]]


def near_first(count):
    return sorted(range(1, count), key=lambda q: (bin(q).count("1"), q))


def gather_kernel(
    groups, count, wq, wo, wkv, small, upc, q_all, o_all, kv_all, small_all, up_all,
    zs, zr, ps, pr, bs, br, us, ur, loc,
):
    chips = groups // 2
    g, me = lax.axis_index("grp"), lax.axis_index("shard")
    p, c = lax.div(g, 2), lax.rem(g, 2)

    barrier = pltpu.get_barrier_semaphore()

    def greet(target):
        pl.semaphore_signal(barrier, inc=1, device_id=target, device_id_type=MESH)

    greet((g + 1 - 2 * c, me))
    for q in range(1, count):
        greet((g, lax.bitwise_xor(me, q)))

    @pl.when(p < chips - 1)
    def _():
        greet((g + 2, me))

    @pl.when(p > 0)
    def _():
        greet((g - 2, me))

    ends = (p == 0).astype(jnp.int32) + (p == chips - 1).astype(jnp.int32)
    pl.semaphore_wait(barrier, count + 2 - ends)

    def send(src, dst, send_sem, recv_sem, target):
        pltpu.make_async_remote_copy(
            src_ref=src, dst_ref=dst, send_sem=send_sem, recv_sem=recv_sem,
            device_id=target, device_id_type=MESH,
        ).start()

    def wait(ref, sem):
        pltpu.make_async_copy(ref, ref, sem).wait()

    own = (wq, wo, wkv, small)
    whole = (q_all, o_all, kv_all, small_all)
    parity = (0, 1, 0, 1)
    size = [x.shape[0] for x in own]
    full = len(own)
    cuts = (full, full + 1)
    up_size = upc.shape[1]
    up_half = up_size * count // 2

    def spot(a, z, col):
        if a < full:
            at = ((z * 2 + c) * count + col) * size[a]
            return whole[a].at[pl.ds(pl.multiple_of(at, 16), size[a])]
        at = (z * 2 + c) * up_half * 2 + (a - full) * up_half
        return up_all.at[pl.ds(pl.multiple_of(at, 16), up_half)]

    def along(a, way, hop, src, z):
        step = 1 - 2 * way
        send(src, spot(a, z, me), zs.at[a, way, hop], zr.at[a, way, hop], (g + 2 * step, me))

    def across(a, src, z, q):
        for m in cube_tree(count, parity[a], q):
            send(
                src, spot(a, z, lax.bitwise_xor(me, q)), ps.at[a], pr.at[a, z, q ^ m],
                (g, lax.bitwise_xor(me, m)),
            )

    def aside(a, src, z, q):
        send(src, spot(a, z, lax.bitwise_xor(me, q)), bs.at[a], br.at[a], (g + 1 - 2 * c, me))

    def may_send(way, hop):
        if way == 0:
            return (p >= hop - 1) & (p < chips - 1)
        return (p + hop - 1 <= chips - 1) & (p > 0)

    def may_take(way, hop):
        return p >= hop if way == 0 else p + hop <= chips - 1

    up_rows = lambda col: up_all.at[pl.ds(pl.multiple_of((g * count + col) * up_size, 16), up_size)]
    for q in near_first(count):
        to = lax.bitwise_xor(me, q)
        send(upc.at[to], up_rows(me), us, ur.at[q], (g, to))
    mine = [pltpu.make_async_copy(upc.at[me], up_rows(me), loc.at[full])]
    for a in range(full):
        mine.append(pltpu.make_async_copy(own[a], spot(a, p, me), loc.at[a]))
    for copy in mine:
        copy.start()

    def first(a, src):
        for way in range(2):
            pl.when(may_send(way, 1))(partial(along, a, way, 1, src, p))
        aside(a, src, p, 0)

    for a in range(full):
        first(a, own[a])
        across(a, own[a], p, 0)
    mine[0].wait()
    for q in near_first(count):
        wait(up_rows(me), ur.at[q])
    for a in cuts:
        first(a, spot(a, p, me))

    def plane(z):
        for q in near_first(count):
            for a in range(full):
                ref = spot(a, z, lax.bitwise_xor(me, q))
                wait(ref, pr.at[a, z, q])
                across(a, ref, z, q)
                aside(a, ref, z, q)

    def planes(hop):
        if hop == 0:
            plane(p)
            return
        for way in range(2):
            z = p - hop if way == 0 else p + hop
            pl.when(may_take(way, hop))(partial(plane, z))

    def arrive(a, hop):
        for way in range(2):

            @pl.when(may_take(way, hop))
            def _():
                z = p - hop if way == 0 else p + hop
                ref = spot(a, z, me)
                wait(ref, zr.at[a, way, hop])
                if hop + 1 < chips:
                    pl.when(may_send(way, hop + 1))(
                        partial(along, a, way, hop + 1, ref, z)
                    )
                if a < full:
                    across(a, ref, z, 0)
                aside(a, ref, z, 0)

    for hop in range(1, chips):
        for a in range(full):
            arrive(a, hop)
        planes(hop - 1)
        for a in cuts:
            arrive(a, hop)
    planes(chips - 1)

    for copy in mine[1:]:
        copy.wait()
    for a in range(full + 2):
        for way in range(2):
            for hop in range(1, chips):
                pl.when(may_send(way, hop))(
                    partial(wait, spot(a, p, me), zs.at[a, way, hop])
                )
    for a in range(full):
        wait(whole[a].at[pl.ds(0, chips * (count - 1) * size[a])], ps.at[a])
        wait(whole[a].at[pl.ds(0, chips * count * size[a])], bs.at[a])
        wait(whole[a].at[pl.ds(0, chips * count * size[a])], br.at[a])
    for a in cuts:
        wait(up_all.at[pl.ds(0, chips * up_half)], bs.at[a])
        wait(up_all.at[pl.ds(0, chips * up_half)], br.at[a])
    wait(up_all.at[pl.ds(0, (count - 1) * up_size)], us)


def gather_all(groups, count, wq, wo, wkv, small, upc):
    chips = groups // 2
    n = groups * count
    any_ = pl.BlockSpec(memory_space=pl.ANY)
    dma = pltpu.SemaphoreType.DMA
    tall = lambda x: jax.ShapeDtypeStruct((n * x.shape[0], x.shape[1]), x.dtype)
    return pl.pallas_call(
        partial(gather_kernel, groups, count),
        out_shape=(
            tall(wq), tall(wo), tall(wkv), tall(small),
            jax.ShapeDtypeStruct((n * upc.shape[1], upc.shape[2]), upc.dtype),
        ),
        in_specs=[any_] * 5,
        out_specs=(any_,) * 5,
        scratch_shapes=[
            dma((6, 2, chips)), dma((6, 2, chips)), dma((4,)), dma((4, chips, count)),
            dma((6,)), dma((6,)), dma, dma((count,)), dma((5,)),
        ],
        compiler_params=pltpu.CompilerParams(collective_id=1, has_side_effects=True),
        cost_estimate=pl.CostEstimate(flops=0, bytes_accessed=100_000_000, transcendentals=0),
        name="gather_all",
    )(wq, wo, wkv, small, upc)


def attend_kernel(
    groups, count, tokens, small_all, lengths, cot, wq, wo, wkv,
    near_all, cot_all, normed, queries, keyvals, attended, middle, vectors, up_part, bias,
    wq_v, wo_v, wkv_v, second, ws, ns, nr, cs, cr, loc,
):
    g, me = lax.axis_index("grp"), lax.axis_index("shard")
    barrier = pltpu.get_barrier_semaphore()
    nearest = [1 << d for d in range(count.bit_length() - 1)]
    for m in nearest:
        pl.semaphore_signal(
            barrier, inc=1, device_id=(g, lax.bitwise_xor(me, m)), device_id_type=MESH
        )
    pl.semaphore_wait(barrier, len(nearest))

    loads = [
        pltpu.make_async_copy(a, b, ws.at[i])
        for i, (a, b) in enumerate(((wkv, wkv_v), (wq, wq_v), (wo, wo_v)))
    ]
    for load in loads:
        load.start()

    rows, width = tokens.shape
    length = bias.shape[1]
    half = rows // 2
    near = near_first(count)
    place = lambda ref, k, col: ref.at[pl.ds(pl.multiple_of(col * rows + k * half, 16), half)]

    def send(src, dst, send_sem, recv_sem, m):
        pltpu.make_async_remote_copy(
            src_ref=src, dst_ref=dst, send_sem=send_sem, recv_sem=recv_sem,
            device_id=(g, lax.bitwise_xor(me, m)), device_id_type=MESH,
        ).start()

    def wait(ref, sem):
        pltpu.make_async_copy(ref, ref, sem).wait()

    def pass_on(ref, src, k, q, sends, gets):
        for m in cube_tree(count, k, q):
            send(src, place(ref, k, lax.bitwise_xor(me, q)), sends.at[k], gets.at[k, q ^ m], m)

    def take_all(ref, sends, gets):
        for q in near:
            for k in range(2):
                got = place(ref, k, lax.bitwise_xor(me, q))
                wait(got, gets.at[k, q])
                pass_on(ref, got, k, q, sends, gets)

    for k in range(2):
        pass_on(cot_all, cot.at[pl.ds(k * half, half)], k, 0, cs, cr)
    own_cot = pltpu.make_async_copy(cot, cot_all.at[pl.ds(pl.multiple_of(me * rows, 16), rows)], loc.at[0])
    own_cot.start()

    lot = small_all.shape[0] // (groups * count)
    piece = width // (groups * count)
    join = 128 // piece
    for k in range(width // 128):
        parts = [
            small_all[(k * join + i) * lot : (k * join + i) * lot + 16, :piece].astype(F32) for i in range(join)
        ]
        vectors[:, k * 128 : (k + 1) * 128] = jnp.concatenate(parts, axis=1)
    total = small_all[0:16, :].astype(F32)
    for d in range(1, groups * count):
        total = total + small_all[d * lot : d * lot + 16, :].astype(F32)
    vectors[7:8, :128] = total[7:8, :]
    pieces = []
    for k in range(groups):
        at = pl.multiple_of((k * count + me) * lot, 16)
        mine = small_all[pl.ds(at, 16), :].astype(F32)
        pieces += [mine[8 + r : 9 + r, :piece] for r in range(up_part.shape[1] // groups // piece)]
    for k in range(up_part.shape[1] // 128):
        up_part[:, k * 128 : (k + 1) * 128] = jnp.concatenate(pieces[k * join : (k + 1) * join], axis=1)

    band = 32
    spots = [lax.broadcasted_iota(jnp.int32, (length, length), d) for d in range(2)]
    for m in range(rows // length):
        segments = [jnp.zeros((length, length), jnp.int32)] * 2
        stop = 0
        for k in range(lengths.shape[1]):
            stop = stop + lengths[me * (rows // length) + m, k]
            segments = [a + (spot >= stop).astype(jnp.int32) for a, spot in zip(segments, spots)]
        allowed = (segments[0] == segments[1]) & (spots[1] <= spots[0])
        bias[m * length : (m + 1) * length, :] = jnp.where(allowed, 0.0, NEGATIVE)

    def norm(x, gain, shift):
        offset = x - jnp.mean(x, axis=1, keepdims=True)
        rate = lax.rsqrt(jnp.mean(offset * offset, axis=1, keepdims=True) + EPS)
        return (offset * rate * gain + shift).astype(BF)

    @pl.loop(0, rows // band)
    def _(i):
        at = pl.ds(pl.multiple_of(i * band, band), band)
        normed[at, :] = norm(tokens[at, :].astype(F32), vectors[0:1, :], vectors[1:2, :])

    loads[0].wait()
    kv = jnp.dot(normed[...], wkv_v[...], preferred_element_type=F32)
    keyvals[:, :HD] = kv[:, :HD].astype(BF)
    keyvals[:, HD:] = (kv[:, HD:] + vectors[7:8, :HD]).astype(BF)
    loads[1].wait()
    tile = 2 * HD
    scale = HD**-0.5
    fold = lambda x: jnp.concatenate([x[:, h * HD : (h + 1) * HD] for h in range(tile // HD)], axis=0)

    @pl.loop(0, width // tile)
    def _(i):
        cols = pl.ds(pl.multiple_of(i * tile, tile), tile)
        query = jnp.dot(normed[...], wq_v[:, cols], preferred_element_type=F32)
        query = (query + vectors[2:3, cols]).astype(BF)
        queries[:, cols] = query
        for m in range(rows // length):
            at = pl.ds(m * length, length)
            q = fold(query[m * length : (m + 1) * length])
            k, v = keyvals[at, :HD], keyvals[at, HD:]
            shut = jnp.concatenate([bias[at, :]] * (tile // HD), axis=0)
            s = lax.dot_general(q, k, (((1,), (1,)), ((), ())), preferred_element_type=F32) * scale + shut
            e = jnp.exp(s - jnp.max(s, axis=1, keepdims=True))
            probs = (e / jnp.sum(e, axis=1, keepdims=True)).astype(BF)
            got = jnp.dot(probs, v, preferred_element_type=F32).astype(BF)
            for h in range(tile // HD):
                attended[at, pl.ds(pl.multiple_of(i * tile + h * HD, HD), HD)] = got[
                    h * length : (h + 1) * length
                ]

    loads[2].wait()
    wide = min(512, width)

    @pl.loop(0, width // wide)
    def _(i):
        cols = pl.ds(pl.multiple_of(i * wide, wide), wide)
        branch = jnp.dot(attended[...], wo_v[:, cols], preferred_element_type=F32)
        middle[:, cols] = tokens[:, cols].astype(F32) + branch + vectors[3:4, cols]

    take_all(cot_all, cs, cr)
    for k in range(2):

        @pl.loop(k * half // band, (k + 1) * half // band)
        def _(i):
            at = pl.ds(pl.multiple_of(i * band, band), band)
            second[at, :] = norm(middle[at, :], vectors[4:5, :], vectors[5:6, :])

        pass_on(near_all, second.at[pl.ds(k * half, half)], k, 0, ns, nr)
    own = pltpu.make_async_copy(second, near_all.at[pl.ds(pl.multiple_of(me * rows, 16), rows)], loc.at[1])
    own.start()
    take_all(near_all, ns, nr)
    own_cot.wait()
    own.wait()
    for k in range(2):
        wait(cot_all.at[pl.ds(0, (count - 1) * half)], cs.at[k])
        wait(near_all.at[pl.ds(0, (count - 1) * half)], ns.at[k])


def attend(groups, count, tokens, small_all, lengths, cot, wq, wo, wkv, hidden, length):
    rows, width = tokens.shape
    any_, vmem = pl.BlockSpec(memory_space=pl.ANY), pl.BlockSpec(memory_space=pltpu.VMEM)
    dma = pltpu.SemaphoreType.DMA
    shape = jax.ShapeDtypeStruct
    return pl.pallas_call(
        partial(attend_kernel, groups, count),
        out_shape=(
            shape((count * rows, width), BF), shape((count * rows, width), BF), shape((rows, width), BF),
            shape((rows, width), BF), shape((rows, 2 * HD), BF), shape((rows, width), BF),
            shape((rows, width), F32), shape((16, width), F32), shape((1, hidden), F32),
            shape((rows, length), F32),
        ),
        in_specs=[vmem, vmem, pl.BlockSpec(memory_space=pltpu.SMEM), any_, any_, any_, any_],
        out_specs=(any_, any_) + (vmem,) * 8,
        scratch_shapes=[
            pltpu.VMEM(wq.shape, BF), pltpu.VMEM(wo.shape, BF), pltpu.VMEM(wkv.shape, BF),
            pltpu.VMEM((rows, width), BF), dma((3,)), dma((2,)), dma((2, count)), dma((2,)),
            dma((2, count)), dma((2,)),
        ],
        compiler_params=pltpu.CompilerParams(
            collective_id=3, has_side_effects=True, vmem_limit_bytes=48 * 1024 * 1024
        ),
        cost_estimate=pl.CostEstimate(flops=5_000_000_000, bytes_accessed=100_000_000, transcendentals=0),
        name="attend",
    )(tokens, small_all, lengths, cot, wq, wo, wkv)


def back_kernel(groups, count, subs, plain, sizes, share, *refs):
    n = len(subs)
    take = iter(refs)
    many = lambda k: [next(take) for _ in range(k)]
    down_term, up_term, slices, wq, wo, middle_far, down_rows = many(7)
    attended, queries, keyvals, normed, tokens, bias, gains, wkv, early = many(9)
    final, land = many(n), many(n)
    input_grad = next(take)
    own_part = {m: next(take) for m in range(n) if share[m] == m}
    part = [own_part[share[m]] for m in range(n)]
    held = many(n)
    ring_of = sorted(set(sizes))
    load, outer, mid = many(len(ring_of)), many(len(ring_of)), many(len(ring_of))
    load = [load[ring_of.index(size)] for size in sizes]
    arrived, middle, grad_out, grad_mid, branch, grad_q, tiles, stage, stage_kv, grad_kv, sums = many(11)
    sib, ld, sent, came, zs, z_in, z_mid, os, z_fin, xs, xr, loc, ss, gs, gr, ws, ms, free_in, free_mid = take
    chips = groups // 2
    g, me = lax.axis_index("grp"), lax.axis_index("shard")
    p, c = lax.div(g, 2), lax.rem(g, 2)
    low = p < chips // 2
    inn = jnp.where(low, g + 2, g - 2)
    out = jnp.where(low, g - 2, g + 2)
    end = (p == 0) | (p == chips - 1)
    middle_chip = (p == chips // 2 - 1) | (p == chips // 2)
    other = g + 1 - 2 * c
    near = near_first(count)

    barrier = pltpu.get_barrier_semaphore()

    def greet(target):
        pl.semaphore_signal(barrier, inc=1, device_id=target, device_id_type=MESH)

    greet((other, me))
    greet((inn, me))
    for q in range(1, count):
        greet((g, lax.bitwise_xor(me, q)))

    @pl.when(jnp.logical_not(end))
    def _():
        greet((out, me))

    pl.semaphore_wait(barrier, count + 2 - end.astype(jnp.int32))

    def send(src, dst, send_sem, recv_sem, target):
        pltpu.make_async_remote_copy(
            src_ref=src, dst_ref=dst, send_sem=send_sem, recv_sem=recv_sem,
            device_id=target, device_id_type=MESH,
        ).start()

    def wait(ref, sem):
        pltpu.make_async_copy(ref, ref, sem).wait()

    def add(dst, *more):
        @pl.loop(0, dst.shape[0] // 16)
        def _(i):
            at = pl.ds(pl.multiple_of(i * 16, 16), 16)
            total = dst[at].astype(F32)
            for ref in more:
                total = total + ref[at].astype(F32)
            dst[at] = total.astype(BF)

    cut = lambda m, j: pl.ds(j * sizes[m][0], sizes[m][0])
    away = lambda q: lax.bitwise_xor(me, q)

    given = (down_term, up_term)
    for m in range(2):
        for q in [0] + near:
            send(given[m].at[away(q), 1 - c], land[m].at[q], ss.at[m, q], sib.at[m, q], (other, me))
    own_slice = pltpu.make_async_copy(slices.at[me], arrived.at[0], gr.at[0])
    own_slice.start()
    span = pl.ds(pl.multiple_of(me * attended.shape[0], 16), attended.shape[0])
    own_copies = [
        pltpu.make_async_copy(middle_far, middle, ms.at[0]),
        pltpu.make_async_copy(down_rows.at[span], grad_out, ms.at[1]),
    ]
    for copy in own_copies:
        copy.start()

    def send_slices():
        for q in near:
            send(slices.at[away(q)], arrived.at[q], gs.at[q], gr.at[q], (g, away(q)))

    pair_tasks = [
        [(m, j, q) for j in range(subs[m]) for q in ([0] + near if plain[m] else near + [0])]
        for m in range(n)
    ]
    flat = [task for tasks in pair_tasks for task in tasks]

    def spot(m, q):
        return part[m].at[q - 1] if q else held[m].at[me]

    def loads(k):
        m, j, q = flat[k]
        slot = k % 2
        copies = [pltpu.make_async_copy(land[m].at[q, cut(m, j)], load[m].at[slot], ld.at[slot, 1])]
        if m < 2:
            place = spot(m, q).at[cut(m, j)]
            copies.append(pltpu.make_async_copy(given[m].at[away(q), c, cut(m, j)], place, ld.at[slot, 0]))
        return copies

    def begin(k):
        m, j, q = flat[k]
        if j == 0:
            wait(land[m].at[q], sib.at[m, q])
        for copy in loads(k):
            copy.start()

    def pair(k):
        m, j, q = flat[k]
        if k == 0 or flat[k - 1][0] != m:
            begin(k)
        if k + 1 < len(flat) and flat[k + 1][0] == m:
            begin(k + 1)
        for copy in loads(k):
            copy.wait()
        ref = spot(m, q).at[cut(m, j)]
        add(ref, load[m].at[k % 2])
        if q:
            send(ref, held[m].at[me, cut(m, j)], sent.at[m], came.at[m, j, q], (g, away(q)))

    units = []
    for m in range(n):
        for j in range(subs[m]):
            units += [(m, j, q) for q in [0] + near] if plain[m] else [(m, j, 0)]
    rings = [ring_of.index(sizes[m]) for m, j, q in units]
    index = [rings[:u].count(rings[u]) for u in range(len(units))]
    total_in = [rings.count(r) for r in range(len(ring_of))]
    slot_of = lambda u: index[u] % outer[rings[u]].shape[0]
    reused = lambda u: index[u] >= outer[rings[u]].shape[0]
    again = lambda u: index[u] + outer[rings[u]].shape[0] < total_in[rings[u]]

    def value(u):
        m, j, q = units[u]
        return held[m].at[away(q), cut(m, j)]

    def result(u, half):
        m, j, q = units[u]
        return final[m].at[half, away(q) if plain[m] else 0, cut(m, j)]

    def inward(u):
        m, j, q = units[u]
        ref = value(u)
        if plain[m]:
            if q:
                wait(ref, came.at[m, j, q])
        else:
            others = [held[m].at[away(r), cut(m, j)] for r in near]
            for r, other_ref in zip(near, others):
                wait(other_ref, came.at[m, j, r])
            add(ref, *others)
        box, slot = rings[u], slot_of(u)

        @pl.when(jnp.logical_not(end))
        def _():
            wait(outer[box].at[slot], z_in.at[u])
            add(ref, outer[box].at[slot])
            if again(u):
                pl.semaphore_signal(free_in.at[box, slot], inc=1, device_id=(out, me), device_id_type=MESH)

        @pl.when(middle_chip)
        def _():
            if reused(u):
                pl.semaphore_wait(free_mid.at[box, slot], 1)
            send(ref, mid[box].at[slot], zs.at[u], z_mid.at[u], (inn, me))

        @pl.when(jnp.logical_not(middle_chip))
        def _():
            if reused(u):
                pl.semaphore_wait(free_in.at[box, slot], 1)
            send(ref, outer[box].at[slot], zs.at[u], z_in.at[u], (inn, me))

    def centre(u):
        box, slot = rings[u], slot_of(u)

        @pl.when(middle_chip)
        def _():
            ref = value(u)
            wait(ref, zs.at[u])
            wait(mid[box].at[slot], z_mid.at[u])
            add(ref, mid[box].at[slot])
            if again(u):
                pl.semaphore_signal(free_mid.at[box, slot], inc=1, device_id=(inn, me), device_id_type=MESH)
            pl.when(jnp.logical_not(end))(
                lambda: send(ref, result(u, c), os.at[u], z_fin.at[u], (out, me))
            )
            send(ref, result(u, c), xs.at[u], xr.at[u], (other, me))
            pltpu.make_async_copy(ref, result(u, c), loc.at[u]).start()

    def outward(u):
        @pl.when(jnp.logical_not(middle_chip))
        def _():
            ref = result(u, c)
            wait(ref, z_fin.at[u])
            pl.when(jnp.logical_not(end))(
                lambda: send(ref, ref, os.at[u], z_fin.at[u], (out, me))
            )
            send(ref, ref, xs.at[u], xr.at[u], (other, me))

    rows, width = attended.shape
    length = bias.shape[1]
    scale = HD**-0.5
    band = 32
    column = lambda at, size: pl.ds(pl.multiple_of(at, 128), size)

    def moments(x):
        centre_ = jnp.mean(x, axis=1, keepdims=True)
        offset = x - centre_
        rate = lax.rsqrt(jnp.mean(offset * offset, axis=1, keepdims=True) + EPS)
        return offset * rate, rate

    def clear():
        sums[...] = jnp.zeros_like(sums)
        grad_kv[...] = jnp.zeros_like(grad_kv)

    def tally(k, x):
        sums[k : k + 1, :] += jnp.sum(x, axis=0, keepdims=True)

    def second_norm(lo, hi):
        gain = gains[4:5, :]

        @pl.loop(lo, hi)
        def _(i):
            at = pl.ds(pl.multiple_of(i * band, band), band)
            grad = arrived[0, at, :].astype(F32)
            for q in range(1, count):
                grad = grad + arrived[q, at, :].astype(F32)
            unit, rate = moments(middle[at, :])
            tally(0, grad * unit)
            tally(1, grad)
            e = grad * gain
            back = rate * (
                e - jnp.mean(e, axis=1, keepdims=True) - unit * jnp.mean(e * unit, axis=1, keepdims=True)
            )
            away_grad = grad_out[at, :].astype(F32)
            tally(7, away_grad)
            whole = back + away_grad
            grad_mid[at, :] = whole
            short = whole.astype(BF)
            branch[at, :] = short
            tally(2, short.astype(F32))

    def first_norm(lo, hi):
        gain = gains[0:1, :]

        @pl.loop(lo, hi)
        def _(i):
            at = pl.ds(pl.multiple_of(i * band, band), band)
            grad = middle[at, :]
            unit, rate = moments(tokens[at, :].astype(F32))
            tally(3, grad * unit)
            tally(4, grad)
            e = grad * gain
            back = rate * (
                e - jnp.mean(e, axis=1, keepdims=True) - unit * jnp.mean(e * unit, axis=1, keepdims=True)
            )
            input_grad[at, :] = (back + grad_mid[at, :]).astype(BF)
            tally(5, grad_q[at, :].astype(F32))

    part_cols = min(512, width)

    def outer_product(dst, left, start, size, right):
        lhs = left[:, column(start, size)]

        @pl.loop(0, right.shape[1] // min(part_cols, right.shape[1]))
        def _(k):
            cols = column(k * min(part_cols, right.shape[1]), min(part_cols, right.shape[1]))
            dst[:, cols] = lax.dot_general(
                lhs, right[:, cols], (((0,), (0,)), ((), ())), preferred_element_type=F32
            ).astype(BF)

    staged = []

    def weight_terms(m, left, right, some):
        size = width // count // 2
        for q in some:
            k = len(staged)
            if k >= 2:
                wait(stage.at[k % 2], ss.at[staged[k - 2][0], staged[k - 2][1]])
            outer_product(stage.at[k % 2], left, (away(q) * 2 + 1 - c) * size, size, right)
            send(stage.at[k % 2], land[m].at[q], ss.at[m, q], sib.at[m, q], (other, me))
            staged.append((m, q))
            outer_product(spot(m, q), left, (away(q) * 2 + c) * size, size, right)

    tile_rows = tiles.shape[1]
    tile_count = width // tile_rows

    def weight_tile(source, i):
        at = pl.multiple_of(i * tile_rows, tile_rows)
        slot = lax.rem(i, 2)
        return pltpu.make_async_copy(source.at[pl.ds(at, tile_rows)], tiles.at[slot], ws.at[slot])

    def attention_tiles(lo, hi):
        @pl.loop(lo, hi)
        def _(i):
            pl.when(i + 1 < tile_count)(lambda: weight_tile(wo, i + 1).start())
            weight_tile(wo, i).wait()
            cols = column(i * tile_rows, tile_rows)
            grad_att = lax.dot_general(
                branch[...], tiles[lax.rem(i, 2)], (((1,), (1,)), ((), ())), preferred_element_type=F32
            ).astype(BF)
            query = queries[:, cols]
            heads = tile_rows // HD
            fold = lambda x: jnp.concatenate([x[:, h * HD : (h + 1) * HD] for h in range(heads)], axis=0)
            for m in range(rows // length):
                at = pl.ds(m * length, length)
                q = fold(query[m * length : (m + 1) * length])
                ga = fold(grad_att[m * length : (m + 1) * length])
                k, v = keyvals[at, :HD], keyvals[at, HD:]
                shut = jnp.concatenate([bias[at, :]] * heads, axis=0)
                s = lax.dot_general(q, k, (((1,), (1,)), ((), ())), preferred_element_type=F32) * scale + shut
                e = jnp.exp(s - jnp.max(s, axis=1, keepdims=True))
                probs = e / jnp.sum(e, axis=1, keepdims=True)
                gp = lax.dot_general(ga, v, (((1,), (1,)), ((), ())), preferred_element_type=F32)
                ds = (probs * (gp - jnp.sum(probs * gp, axis=1, keepdims=True))).astype(BF)
                dq = (jnp.dot(ds, k, preferred_element_type=F32) * scale).astype(BF)
                for h in range(heads):
                    grad_q[at, column(i * tile_rows + h * HD, HD)] = dq[h * length : (h + 1) * length]
                tn = (((0,), (0,)), ((), ()))
                dk = lax.dot_general(ds, q, tn, preferred_element_type=F32) * scale
                dv = lax.dot_general(probs.astype(BF), ga, tn, preferred_element_type=F32)
                grad_kv[at, :HD] += dk
                grad_kv[at, HD:] += dv

    def query_tiles(lo, hi):
        low_kv = grad_kv[...].astype(BF)

        @pl.loop(lo, hi)
        def _(i):
            pl.when(i + 1 < tile_count)(lambda: weight_tile(wq, i + 1).start())
            weight_tile(wq, i).wait()
            cols = column(i * tile_rows, tile_rows)
            nt = (((1,), (1,)), ((), ()))
            middle[:, cols] = lax.dot_general(
                grad_q[...], tiles[lax.rem(i, 2)], nt, preferred_element_type=F32
            ) + lax.dot_general(
                low_kv, wkv[pl.ds(pl.multiple_of(i * tile_rows, tile_rows), tile_rows)], nt,
                preferred_element_type=F32,
            )

    def keyval_terms():
        low_kv = grad_kv[...].astype(BF)
        size = width // count // 2
        last = n - 1
        line = jnp.sum(low_kv[:, HD:].astype(F32), axis=0, keepdims=True)
        for k in range(width // size):
            sums[6:7, k * size : k * size + HD] = line
        for q in near + [0]:
            for ref, which in ((stage_kv.at[q], 1 - c), (spot(last, q), c)):
                start = (away(q) * 2 + which) * size
                ref[pl.ds(0, size), :] = lax.dot_general(
                    normed[:, column(start, size)], low_kv, (((0,), (0,)), ((), ())),
                    preferred_element_type=F32,
                ).astype(BF)
                ref[pl.ds(size, 16), :] = jnp.zeros((16, 2 * HD), BF)
                ref[pl.ds(size, 16), :size] = sums[:, column(start, size)].astype(BF)
                ref[pl.ds(size + 16, early.shape[2]), :] = early[away(q), which]
            send(stage_kv.at[q], land[last].at[q], ss.at[last, q], sib.at[last, q], (other, me))

    def reuse(m):
        if share[m] != m:
            wait(part[m], sent.at[share[m]])

    bands = rows // band
    plan = {}

    def at_step(step, *work):
        plan.setdefault(step, []).extend(work)

    P_ = partial
    starts = [sum(len(t) for t in pair_tasks[:m]) for m in range(n)]
    pairs_ = lambda m, lo, hi: [P_(pair, starts[m] + k) for k in range(lo, min(hi, len(pair_tasks[m])))]
    first = [*pairs_(0, 0, 99), *pairs_(1, 0, 99)]
    for s, work in enumerate(first[AHEAD:]):
        at_step(s // 2, work)
    at_step(SLICE_STEP, send_slices)

    def got_slices():
        clear()
        for copy in own_copies:
            copy.wait()
        own_slice.wait()
        for q in near:
            wait(arrived.at[q], gr.at[q])

    order = near + [0]
    half = len(order) // 2
    at_step(NORM_STEP, got_slices, P_(second_norm, 0, bands // 2))
    at_step(NORM_STEP + 1, P_(second_norm, bands // 2, bands), lambda: weight_tile(wo, 0).start(), P_(reuse, 2))
    at_step(NORM_STEP + 2, P_(weight_terms, 2, attended, branch, order[:half]))
    at_step(NORM_STEP + 3, P_(weight_terms, 2, attended, branch, order[half:]))
    for k in range(4):
        at_step(NORM_STEP + 4 + k, P_(attention_tiles, k * tile_count // 4, (k + 1) * tile_count // 4))
    per = len(pair_tasks[2])
    at_step(NORM_STEP + 5, *pairs_(2, 0, per // 2))
    at_step(NORM_STEP + 6, *pairs_(2, per // 2, per))
    at_step(NORM_STEP + 7, lambda: weight_tile(wq, 0).start(), P_(reuse, 3))
    at_step(NORM_STEP + 8, P_(weight_terms, 3, normed, grad_q, order[:half]))
    at_step(NORM_STEP + 9, P_(weight_terms, 3, normed, grad_q, order[half:]))
    at_step(NORM_STEP + 10, P_(query_tiles, 0, tile_count // 2), *pairs_(3, 0, per // 2))
    at_step(NORM_STEP + 11, P_(query_tiles, tile_count // 2, tile_count), *pairs_(3, per // 2, per))
    at_step(NORM_STEP + 12, P_(first_norm, 0, bands // 2))
    at_step(NORM_STEP + 13, P_(first_norm, bands // 2, bands), keyval_terms)
    at_step(NORM_STEP + 14, *pairs_(4, 0, 99))

    for work in first[:AHEAD]:
        work()
    steps = max(len(units) + LAG_OUT, max(plan) + 1)
    for step in range(steps):
        if step < len(units):
            inward(step)
        if 0 <= step - LAG_MID < len(units):
            centre(step - LAG_MID)
        if 0 <= step - LAG_OUT < len(units):
            outward(step - LAG_OUT)
        for work in plan.get(step, ()):
            work()

    for m in range(n):
        if m not in share[m + 1 :]:
            wait(part[m], sent.at[m])
        for q in near + [0]:
            if m < 2 or m == n - 1 or (m, q) in staged[-2:]:
                wait(land[m].at[q], ss.at[m, q])
    for q in near:
        wait(arrived.at[q], gs.at[q])
    for u in range(len(units)):
        wait(result(u, 1 - c), xr.at[u])
        wait(result(u, c), xs.at[u])
        pl.when(jnp.logical_not(end))(partial(wait, result(u, c), os.at[u]))
        pl.when(middle_chip)(partial(wait, result(u, c), loc.at[u]))
        pl.when(jnp.logical_not(middle_chip))(partial(wait, value(u), zs.at[u]))


def back_all(groups, count, given, far, near_by, early):
    rows, width = near_by[0].shape
    size = width // count // 2
    low = (size + 16 + early.shape[2], 2 * HD)
    shapes = [x.shape[2:] for x in given] + [(size, width), (size, width), low]
    plain, subs = (True, True, False, False, False), (2, 2, 2, 2, 1)
    n = len(shapes)
    sizes = [(s[0] // k, s[1]) for s, k in zip(shapes, subs)]
    share = list(range(n))
    for m in (2, 3):
        if shapes[m] == shapes[m - 2]:
            share[m] = m - 2
    rings = sorted(set(sizes))
    units = sum(s * (count if f else 1) for s, f in zip(subs, plain))
    slots = [min(RING, sum(s * (count if f else 1) for s, f, z in zip(subs, plain, sizes) if z == r)) for r in rings]
    any_, vmem = pl.BlockSpec(memory_space=pl.ANY), pl.BlockSpec(memory_space=pltpu.VMEM)
    dma, regular = pltpu.SemaphoreType.DMA, pltpu.SemaphoreType.REGULAR
    out = [jax.ShapeDtypeStruct((2, count if f else 1) + s, BF) for s, f in zip(shapes, plain)]
    out += [jax.ShapeDtypeStruct((count,) + s, BF) for s in shapes]
    tile = 2 * HD
    scratch = [pltpu.VMEM((count - 1,) + shapes[m], BF) for m in range(n) if share[m] == m]
    scratch += [pltpu.VMEM((count,) + s, BF) for s in shapes]
    scratch += [pltpu.VMEM((2,) + r, BF) for r in rings]
    scratch += [pltpu.VMEM((k,) + r, BF) for k, r in zip(slots, rings)] * 2
    scratch += [
        pltpu.VMEM((count, rows, width), BF), pltpu.VMEM((rows, width), F32), pltpu.VMEM((rows, width), BF),
        pltpu.VMEM((rows, width), F32),
        pltpu.VMEM((rows, width), BF), pltpu.VMEM((rows, width), BF), pltpu.VMEM((2, tile, width), BF),
        pltpu.VMEM((2, size, width), BF), pltpu.VMEM((count,) + low, BF), pltpu.VMEM((rows, 2 * HD), F32),
        pltpu.VMEM((16, width), F32),
        dma((n, count)), dma((2, 2)), dma((n,)), dma((n, max(subs), count)), dma((units,)), dma((units,)),
        dma((units,)), dma((units,)), dma((units,)), dma((units,)), dma((units,)), dma((units,)),
        dma((n, count)), dma((count,)), dma((count,)), dma((2,)), dma((2,)),
        regular((len(rings), max(slots))), regular((len(rings), max(slots))),
    ]
    got = pl.pallas_call(
        partial(back_kernel, groups, count, subs, plain, sizes, share),
        out_shape=tuple(out) + (jax.ShapeDtypeStruct((rows, width), BF),),
        in_specs=[any_] * 7 + [vmem] * 9,
        out_specs=(any_,) * (2 * n) + (vmem,),
        scratch_shapes=scratch,
        compiler_params=pltpu.CompilerParams(
            collective_id=2, has_side_effects=True, vmem_limit_bytes=60 * 1024 * 1024
        ),
        cost_estimate=pl.CostEstimate(flops=0, bytes_accessed=200_000_000, transcendentals=0),
        name="back_all",
    )(*given, *far, *near_by, early)
    return got[:n], got[-1]


def widen_kernel(block, size, down, up, out, query, low, o_down, o_up, o_out, o_query, o_low, *lines):
    o_down[...] = down[...].astype(F32)
    o_out[...] = out[...].astype(F32)
    o_query[...] = query[...].astype(F32)
    _, count, rows, hidden = up.shape
    for source in range(count):
        for k in range(hidden // block):
            o_up[:, pl.ds((k * count + source) * block, block)] = up[0, source, :, pl.ds(k * block, block)].astype(F32)

    @pl.when(pl.program_id(0) == 0)
    def _():
        for half in range(2):
            o_low[half * size : (half + 1) * size, :] = low[half, :size, :].astype(F32)
            sums = low[half, size : size + 16, :size].astype(F32)
            for v in range(8):
                lines[v][:, half * size : (half + 1) * size] = sums[v : v + 1, :]
            tail = low[half, size + 16 :, :].astype(F32)
            wide = tail.shape[1]
            for r in range(hidden // 2 // wide):
                start = half * hidden // 2 + r * wide
                lines[8][:, start : start + wide] = tail[r : r + 1, :]


def widen(full, block):
    down, up, out, query, low = full
    flat = lambda x: x.reshape(-1, x.shape[-1])
    down, out, query, low = flat(down), flat(out), flat(query), low[:, 0]
    _, count, rows, hidden = up.shape
    steps = 16
    step = 2 * rows // steps
    size = out.shape[0] // 2
    row = lambda x: pl.BlockSpec((x.shape[0] // steps, x.shape[1]), lambda i: (i, 0))
    still = lambda *shape: pl.BlockSpec(shape, lambda i: (0,) * len(shape))
    shape = lambda *dims: jax.ShapeDtypeStruct(dims, F32)
    vectors = [(1, 2 * size)] * 8 + [(1, hidden)]
    return pl.pallas_call(
        partial(widen_kernel, block, size),
        out_shape=(
            shape(*down.shape), shape(2 * rows, count * hidden), shape(*out.shape), shape(*query.shape),
            shape(2 * size, low.shape[2]),
        ) + tuple(shape(*v) for v in vectors),
        grid=(steps,),
        in_specs=[
            row(down), pl.BlockSpec((1, count, step, hidden), lambda i: (i // (steps // 2), 0, i % (steps // 2), 0)),
            row(out), row(query), still(*low.shape),
        ],
        out_specs=(
            row(down), pl.BlockSpec((step, count * hidden), lambda i: (i, 0)), row(out), row(query),
            still(2 * size, low.shape[2]),
        ) + tuple(still(*v) for v in vectors),
        name="widen",
    )(down, up, out, query, low)


def used(lengths, row):
    total = lengths[row, 0]
    for k in range(1, lengths.shape[1]):
        total = total + lengths[row, k]
    return total


def masked(x, lengths, row):
    places = lax.broadcasted_iota(jnp.int32, x.shape, 0)
    return jnp.where(places < used(lengths, row), x, 0.0)


def take_kernel(order, lengths, x, out):
    out[0] = masked(x[0].astype(F32), lengths, pl.program_id(0)).astype(BF)


def take_rows(values, order, lengths):
    _, length, width = values.shape
    spec = lambda f: pl.BlockSpec((1, length, width), f)
    return pl.pallas_call(
        take_kernel,
        out_shape=jax.ShapeDtypeStruct(values.shape, BF),
        grid_spec=pltpu.PrefetchScalarGridSpec(
            num_scalar_prefetch=2,
            grid=(values.shape[0],),
            in_specs=[spec(lambda r, order, lengths: (order[r], 0, 0))],
            out_specs=spec(lambda r, order, lengths: (r, 0, 0)),
        ),
        name="take_rows",
    )(order, lengths, values)


def finish_kernel(deal, lengths, place, x, middle, table, out):
    row = deal[pl.program_id(0)]
    micro = middle.shape[0]
    term = x[0].astype(F32)
    own = lax.div(row, micro) == place[0]

    @pl.when(own)
    def _():
        whole = term + middle[lax.rem(row, micro)] + table[6:7, :]
        out[0] = masked(whole, lengths, row).astype(BF)

    @pl.when(jnp.logical_not(own))
    def _():
        out[0] = masked(term, lengths, row).astype(BF)


def finish_rows(values, deal, lengths, me, middle, table):
    _, length, width = values.shape
    spec = lambda f: pl.BlockSpec((1, length, width), f)
    return pl.pallas_call(
        finish_kernel,
        out_shape=jax.ShapeDtypeStruct(values.shape, BF),
        grid_spec=pltpu.PrefetchScalarGridSpec(
            num_scalar_prefetch=3,
            grid=(values.shape[0],),
            in_specs=[
                spec(lambda j, deal, lengths, me: (deal[j], 0, 0)),
                pl.BlockSpec(middle.shape, lambda j, deal, lengths, me: (0, 0, 0)),
                pl.BlockSpec(table.shape, lambda j, deal, lengths, me: (0, 0)),
            ],
            out_specs=spec(lambda j, deal, lengths, me: (j, 0, 0)),
        ),
        name="finish_rows",
    )(deal, lengths, me.reshape(1), values, middle, table)


def cut_kernel(groups, count, block, x, out):
    for to in range(count):
        for k in range(groups):
            out[to, :, k * block : (k + 1) * block] = x[:, (k * count + to) * block : (k * count + to + 1) * block]


def shards(
    groups,
    count,
    tokens,
    cotangent,
    lengths,
    dealing,
    first_gain,
    first_shift,
    query_weight,
    query_bias,
    keyval_weight,
    value_bias,
    out_weight,
    out_bias,
    second_gain,
    second_shift,
    up_weight,
    up_bias,
    down_weight,
    down_bias,
):
    both = ("grp", "shard")
    micro, length, width = tokens.shape
    group_rows = dealing.shape[0]
    group = lax.axis_index("grp")
    me = lax.axis_index("shard")
    half = micro // 2
    block = down_weight.shape[0]
    hidden = block * groups
    rows = micro * length

    deal = dealing - group * group_rows
    steps = jnp.arange(group_rows, dtype=jnp.int32)
    inverse = jnp.sum(jnp.where(deal[:, None] == steps[None, :], steps[:, None], 0), axis=0)

    line = lambda x: jnp.pad(x, (0, 128 - x.shape[0]))
    piece = first_gain.shape[0]
    device = group * count + me
    value_line = lax.dynamic_update_slice(
        jnp.zeros((128,), BF), value_bias, (device * value_bias.shape[0],)
    )
    small = [first_gain, first_shift, query_bias, out_bias, second_gain, second_shift, down_bias]
    small = [line(x) for x in small] + [value_line]
    small += [line(up_bias[k * piece : (k + 1) * piece]) for k in range(block // piece)]
    small = jnp.stack(small + [jnp.zeros((128,), BF)] * (16 - len(small)))
    up_rows = up_weight.shape[0]
    up_cut = pl.pallas_call(
        partial(cut_kernel, groups, count, block),
        out_shape=jax.ShapeDtypeStruct((count, up_rows, hidden), BF),
        name="cut",
    )(up_weight)
    weight_query, weight_out, weight_keyval, small_all, weight_up = gather_all(
        groups, count, query_weight, out_weight, keyval_weight, small, up_cut
    )
    weight_query, weight_out, weight_up, down_weight = lax.optimization_barrier(
        (weight_query, weight_out, weight_up, down_weight)
    )
    weight_down = lax.all_gather(down_weight, "grp", axis=0, tiled=True)

    flat_tokens = tokens.reshape(rows, width)
    (
        normed_two, cot_rows, normed_one, queries, keyvals, attended, middle, table, up_part, bias,
    ) = attend(
        groups, count, flat_tokens, small_all, lengths, cotangent.reshape(rows, width),
        weight_query, weight_out, weight_keyval, hidden, length,
    )
    grad_down = take_rows(cot_rows.reshape(group_rows, length, width), inverse, lengths)
    grad_down = grad_down.reshape(group_rows * length, width)

    hidden_pre = mm(normed_two, weight_up) + up_part
    gelu_tanh = partial(jax.nn.gelu, approximate=True)
    activated_wide, gelu_pull = jax.vjp(gelu_tanh, hidden_pre)
    activated = activated_wide.astype(BF)
    grad_hidden = gelu_pull(mm_nt(grad_down, weight_down))[0].astype(BF)
    slices = mm_nt(grad_hidden, weight_up).astype(BF).reshape(count, rows, width)
    down_grad = mm_tn(activated, grad_down).astype(BF)
    up_grad = mm_tn(normed_two, grad_hidden).astype(BF)

    result = mm(activated, weight_down).astype(BF).reshape(group_rows, length, width)
    result = finish_rows(result, deal, lengths, me, middle.reshape(micro, length, width), table)
    block_output = lax.psum_scatter(
        result.reshape(group_rows * length, width), "shard", scatter_dimension=0, tiled=True
    ).reshape(micro, length, width)

    per = groups // count
    up_bias_part = jnp.sum(grad_hidden.astype(F32), axis=0).reshape(count, per, 1, block)
    spot = (jnp.arange(count, dtype=jnp.int32) == me)[None, None, :, None]
    up_bias_part = jnp.where(spot, up_bias_part, 0.0).reshape(count, 2, -1)
    early = up_bias_part.astype(BF)
    fill = -early.shape[2] % (16 * 2 * HD)
    early = jnp.pad(early, ((0, 0), (0, 0), (0, fill))).reshape(count, 2, -1, 2 * HD)

    cut = lambda x: x.reshape(count, 2, x.shape[0] // count // 2, x.shape[1])
    near_by = (
        attended, queries, keyvals, normed_one, flat_tokens, bias, table, weight_keyval,
    )
    full, input_grad = back_all(
        groups, count, (cut(down_grad), cut(up_grad)),
        (slices, weight_query, weight_out, middle, grad_down), near_by, early,
    )
    input_grad = input_grad.reshape(micro, length, width)

    down_full, up_full, out_full, query_full, keyval_full, *lines = widen(full, block)
    lines = [line.reshape(-1) for line in lines]
    gain_two_grad, shift_two_grad, out_bias_grad, gain_one_grad, shift_one_grad, query_bias_grad = lines[:6]
    short = value_bias.shape[0] * groups
    value_bias_grad = lax.dynamic_slice(lines[6], (me * short,), (short,))
    down_bias_grad, up_bias_grad = lines[7:]

    return (
        block_output, input_grad, gain_one_grad, shift_one_grad, query_full, query_bias_grad, keyval_full,
        value_bias_grad, out_full, out_bias_grad, gain_two_grad, shift_two_grad, up_full, up_bias_grad,
        down_full, down_bias_grad,
    )


def solution(mesh):
    rows = P(("grp", "shard"), None, None)
    flat = P(("grp", "shard"))
    tall = P(("grp", "shard"), None)
    vector, matrix = P("shard"), P("shard", None)
    return jax.shard_map(
        partial(shards, mesh.shape["grp"], mesh.shape["shard"]),
        mesh=mesh,
        in_specs=(
            rows, rows, P("grp", None), P("grp"), flat, flat, tall, flat, tall, flat,
            tall, flat, flat, flat, tall, flat, tall, flat,
        ),
        out_specs=(
            rows, rows, vector, vector, matrix, vector, matrix, vector,
            matrix, vector, vector, vector, matrix, vector, matrix, vector,
        ),
        check_vma=False,
    )
```

```python
from functools import partial

import jax
import jax.numpy as jnp
from jax import lax
from jax.experimental import pallas as pl
from jax.experimental.pallas import tpu as pltpu
from jax.sharding import PartitionSpec as P

HEADS = 16
HD = 128
EPS = 1e-05
NEGATIVE = -1e30
BF = jnp.bfloat16
F32 = jnp.float32
MESH = pl.DeviceIdType.MESH
LAG_MID = 2
LAG_OUT = 6
BUDGET = 8.0
TILE_COST = 4.0
NORM_STEP = 15
RING = 6


def mm(left, right):
    return jnp.dot(left, right, preferred_element_type=F32)


def cube_tree(count, parity, q):
    order = list(range(count.bit_length() - 1))
    if parity:
        order = order[::-1]
    at = max([i for i, d in enumerate(order) if q >> d & 1], default=-1)
    return [1 << d for d in order[at + 1 :]]


def near_first(count):
    return sorted(range(1, count), key=lambda q: (bin(q).count("1"), q))


def gather_kernel(
    groups, count, wq, wo, wkv, small, upc, q_all, o_all, kv_all, small_all, up_all,
    zs, zr, ps, pr, bs, br, us, ur, loc,
):
    chips = groups // 2
    g, me = lax.axis_index("grp"), lax.axis_index("shard")
    p, c = lax.div(g, 2), lax.rem(g, 2)

    barrier = pltpu.get_barrier_semaphore()

    def greet(target):
        pl.semaphore_signal(barrier, inc=1, device_id=target, device_id_type=MESH)

    greet((g + 1 - 2 * c, me))
    for q in range(1, count):
        greet((g, lax.bitwise_xor(me, q)))

    @pl.when(p < chips - 1)
    def _():
        greet((g + 2, me))

    @pl.when(p > 0)
    def _():
        greet((g - 2, me))

    ends = (p == 0).astype(jnp.int32) + (p == chips - 1).astype(jnp.int32)
    pl.semaphore_wait(barrier, count + 2 - ends)

    def send(src, dst, send_sem, recv_sem, target):
        pltpu.make_async_remote_copy(
            src_ref=src, dst_ref=dst, send_sem=send_sem, recv_sem=recv_sem,
            device_id=target, device_id_type=MESH,
        ).start()

    def wait(ref, sem):
        pltpu.make_async_copy(ref, ref, sem).wait()

    own = (wq, wo, wkv, small)
    whole = (q_all, o_all, kv_all, small_all)
    parity = (0, 1, 0, 1)
    size = [x.shape[0] for x in own]
    full = len(own)
    cuts = (full, full + 1)
    up_size = upc.shape[1]
    up_half = up_size * count // 2

    def spot(a, z, col):
        if a < full:
            at = ((z * 2 + c) * count + col) * size[a]
            return whole[a].at[pl.ds(pl.multiple_of(at, 16), size[a])]
        at = (z * 2 + c) * up_half * 2 + (a - full) * up_half
        return up_all.at[pl.ds(pl.multiple_of(at, 16), up_half)]

    def along(a, way, hop, src, z):
        step = 1 - 2 * way
        send(src, spot(a, z, me), zs.at[a, way, hop], zr.at[a, way, hop], (g + 2 * step, me))

    def across(a, src, z, q):
        for m in cube_tree(count, parity[a], q):
            send(
                src, spot(a, z, lax.bitwise_xor(me, q)), ps.at[a], pr.at[a, z, q ^ m],
                (g, lax.bitwise_xor(me, m)),
            )

    def aside(a, src, z, q):
        send(src, spot(a, z, lax.bitwise_xor(me, q)), bs.at[a], br.at[a], (g + 1 - 2 * c, me))

    def may_send(way, hop):
        if way == 0:
            return (p >= hop - 1) & (p < chips - 1)
        return (p + hop - 1 <= chips - 1) & (p > 0)

    def may_take(way, hop):
        return p >= hop if way == 0 else p + hop <= chips - 1

    up_rows = lambda col: up_all.at[pl.ds(pl.multiple_of((g * count + col) * up_size, 16), up_size)]
    for q in near_first(count):
        to = lax.bitwise_xor(me, q)
        send(upc.at[to], up_rows(me), us, ur.at[q], (g, to))
    mine = [pltpu.make_async_copy(upc.at[me], up_rows(me), loc.at[full])]
    for a in range(full):
        mine.append(pltpu.make_async_copy(own[a], spot(a, p, me), loc.at[a]))
    for copy in mine:
        copy.start()

    def first(a, src):
        for way in range(2):
            pl.when(may_send(way, 1))(partial(along, a, way, 1, src, p))
        aside(a, src, p, 0)

    for a in range(full):
        first(a, own[a])
        across(a, own[a], p, 0)
    mine[0].wait()
    for q in near_first(count):
        wait(up_rows(me), ur.at[q])
    for a in cuts:
        first(a, spot(a, p, me))

    def plane(z):
        for q in near_first(count):
            for a in range(full):
                ref = spot(a, z, lax.bitwise_xor(me, q))
                wait(ref, pr.at[a, z, q])
                across(a, ref, z, q)
                aside(a, ref, z, q)

    def planes(hop):
        if hop == 0:
            plane(p)
            return
        for way in range(2):
            z = p - hop if way == 0 else p + hop
            pl.when(may_take(way, hop))(partial(plane, z))

    def arrive(a, hop):
        for way in range(2):

            @pl.when(may_take(way, hop))
            def _():
                z = p - hop if way == 0 else p + hop
                ref = spot(a, z, me)
                wait(ref, zr.at[a, way, hop])
                if hop + 1 < chips:
                    pl.when(may_send(way, hop + 1))(
                        partial(along, a, way, hop + 1, ref, z)
                    )
                if a < full:
                    across(a, ref, z, 0)
                aside(a, ref, z, 0)

    for hop in range(1, chips):
        for a in range(full):
            arrive(a, hop)
        planes(hop - 1)
        for a in cuts:
            arrive(a, hop)
    planes(chips - 1)

    for copy in mine[1:]:
        copy.wait()
    for a in range(full + 2):
        for way in range(2):
            for hop in range(1, chips):
                pl.when(may_send(way, hop))(
                    partial(wait, spot(a, p, me), zs.at[a, way, hop])
                )
    for a in range(full):
        wait(whole[a].at[pl.ds(0, chips * (count - 1) * size[a])], ps.at[a])
        wait(whole[a].at[pl.ds(0, chips * count * size[a])], bs.at[a])
        wait(whole[a].at[pl.ds(0, chips * count * size[a])], br.at[a])
    for a in cuts:
        wait(up_all.at[pl.ds(0, chips * up_half)], bs.at[a])
        wait(up_all.at[pl.ds(0, chips * up_half)], br.at[a])
    wait(up_all.at[pl.ds(0, (count - 1) * up_size)], us)


def gather_all(groups, count, wq, wo, wkv, small, upc):
    chips = groups // 2
    n = groups * count
    any_ = pl.BlockSpec(memory_space=pl.ANY)
    dma = pltpu.SemaphoreType.DMA
    tall = lambda x: jax.ShapeDtypeStruct((n * x.shape[0], x.shape[1]), x.dtype)
    return pl.pallas_call(
        partial(gather_kernel, groups, count),
        out_shape=(
            tall(wq), tall(wo), tall(wkv), tall(small),
            jax.ShapeDtypeStruct((n * upc.shape[1], upc.shape[2]), upc.dtype),
        ),
        in_specs=[any_] * 5,
        out_specs=(any_,) * 5,
        scratch_shapes=[
            dma((6, 2, chips)), dma((6, 2, chips)), dma((4,)), dma((4, chips, count)),
            dma((6,)), dma((6,)), dma, dma((count,)), dma((5,)),
        ],
        compiler_params=pltpu.CompilerParams(collective_id=1, has_side_effects=True),
        cost_estimate=pl.CostEstimate(flops=0, bytes_accessed=100_000_000, transcendentals=0),
        name="gather_all",
    )(wq, wo, wkv, small, upc)


def attend_kernel(
    groups, count, tokens, small_all, lengths, cot, wq, wo, wkv,
    near_all, cot_all, normed, queries, keyvals, attended, middle, vectors, up_part, bias,
    wq_v, wo_v, wkv_v, second, ws, ns, nr, cs, cr, loc,
):
    g, me = lax.axis_index("grp"), lax.axis_index("shard")
    barrier = pltpu.get_barrier_semaphore()
    nearest = [1 << d for d in range(count.bit_length() - 1)]
    for m in nearest:
        pl.semaphore_signal(
            barrier, inc=1, device_id=(g, lax.bitwise_xor(me, m)), device_id_type=MESH
        )
    pl.semaphore_wait(barrier, len(nearest))

    loads = [
        pltpu.make_async_copy(a, b, ws.at[i])
        for i, (a, b) in enumerate(((wkv, wkv_v), (wq, wq_v), (wo, wo_v)))
    ]
    for load in loads:
        load.start()

    rows, width = tokens.shape
    length = bias.shape[1]
    half = rows // 2
    near = near_first(count)
    place = lambda ref, k, col: ref.at[pl.ds(pl.multiple_of(col * rows + k * half, 16), half)]

    def send(src, dst, send_sem, recv_sem, m):
        pltpu.make_async_remote_copy(
            src_ref=src, dst_ref=dst, send_sem=send_sem, recv_sem=recv_sem,
            device_id=(g, lax.bitwise_xor(me, m)), device_id_type=MESH,
        ).start()

    def wait(ref, sem):
        pltpu.make_async_copy(ref, ref, sem).wait()

    def pass_on(ref, src, k, q, sends, gets):
        for m in cube_tree(count, k, q):
            send(src, place(ref, k, lax.bitwise_xor(me, q)), sends.at[k], gets.at[k, q ^ m], m)

    def take_all(ref, sends, gets):
        for q in near:
            for k in range(2):
                got = place(ref, k, lax.bitwise_xor(me, q))
                wait(got, gets.at[k, q])
                pass_on(ref, got, k, q, sends, gets)

    for k in range(2):
        pass_on(cot_all, cot.at[pl.ds(k * half, half)], k, 0, cs, cr)
    own_cot = pltpu.make_async_copy(cot, cot_all.at[pl.ds(pl.multiple_of(me * rows, 16), rows)], loc.at[0])
    own_cot.start()

    lot = small_all.shape[0] // (groups * count)
    piece = width // (groups * count)
    join = 128 // piece
    for k in range(width // 128):
        parts = [
            small_all[(k * join + i) * lot : (k * join + i) * lot + 16, :piece].astype(F32) for i in range(join)
        ]
        vectors[:, k * 128 : (k + 1) * 128] = jnp.concatenate(parts, axis=1)
    total = small_all[0:16, :].astype(F32)
    for d in range(1, groups * count):
        total = total + small_all[d * lot : d * lot + 16, :].astype(F32)
    vectors[7:8, :128] = total[7:8, :]
    pieces = []
    for k in range(groups):
        at = pl.multiple_of((k * count + me) * lot, 16)
        mine = small_all[pl.ds(at, 16), :].astype(F32)
        pieces += [mine[8 + r : 9 + r, :piece] for r in range(up_part.shape[1] // groups // piece)]
    for k in range(up_part.shape[1] // 128):
        up_part[:, k * 128 : (k + 1) * 128] = jnp.concatenate(pieces[k * join : (k + 1) * join], axis=1)

    band = 32
    spots = [lax.broadcasted_iota(jnp.int32, (length, length), d) for d in range(2)]
    for m in range(rows // length):
        segments = [jnp.zeros((length, length), jnp.int32)] * 2
        stop = 0
        for k in range(lengths.shape[1]):
            stop = stop + lengths[me * (rows // length) + m, k]
            segments = [a + (spot >= stop).astype(jnp.int32) for a, spot in zip(segments, spots)]
        allowed = (segments[0] == segments[1]) & (spots[1] <= spots[0])
        bias[m * length : (m + 1) * length, :] = jnp.where(allowed, 0.0, NEGATIVE)

    def norm(x, gain, shift):
        offset = x - jnp.mean(x, axis=1, keepdims=True)
        rate = lax.rsqrt(jnp.mean(offset * offset, axis=1, keepdims=True) + EPS)
        return (offset * rate * gain + shift).astype(BF)

    @pl.loop(0, rows // band)
    def _(i):
        at = pl.ds(pl.multiple_of(i * band, band), band)
        normed[at, :] = norm(tokens[at, :].astype(F32), vectors[0:1, :], vectors[1:2, :])

    loads[0].wait()
    kv = jnp.dot(normed[...], wkv_v[...], preferred_element_type=F32)
    keyvals[:, :HD] = kv[:, :HD].astype(BF)
    keyvals[:, HD:] = (kv[:, HD:] + vectors[7:8, :HD]).astype(BF)
    loads[1].wait()
    tile = 2 * HD
    scale = HD**-0.5
    fold = lambda x: jnp.concatenate([x[:, h * HD : (h + 1) * HD] for h in range(tile // HD)], axis=0)

    @pl.loop(0, width // tile)
    def _(i):
        cols = pl.ds(pl.multiple_of(i * tile, tile), tile)
        query = jnp.dot(normed[...], wq_v[:, cols], preferred_element_type=F32)
        query = (query + vectors[2:3, cols]).astype(BF)
        queries[:, cols] = query
        for m in range(rows // length):
            at = pl.ds(m * length, length)
            q = fold(query[m * length : (m + 1) * length])
            k, v = keyvals[at, :HD], keyvals[at, HD:]
            shut = jnp.concatenate([bias[at, :]] * (tile // HD), axis=0)
            s = lax.dot_general(q, k, (((1,), (1,)), ((), ())), preferred_element_type=F32) * scale + shut
            e = jnp.exp(s - jnp.max(s, axis=1, keepdims=True))
            probs = (e / jnp.sum(e, axis=1, keepdims=True)).astype(BF)
            got = jnp.dot(probs, v, preferred_element_type=F32).astype(BF)
            for h in range(tile // HD):
                attended[at, pl.ds(pl.multiple_of(i * tile + h * HD, HD), HD)] = got[
                    h * length : (h + 1) * length
                ]

    loads[2].wait()
    wide = min(512, width)

    @pl.loop(0, width // wide)
    def _(i):
        cols = pl.ds(pl.multiple_of(i * wide, wide), wide)
        branch = jnp.dot(attended[...], wo_v[:, cols], preferred_element_type=F32)
        middle[:, cols] = tokens[:, cols].astype(F32) + branch + vectors[3:4, cols]

    take_all(cot_all, cs, cr)
    for k in range(2):

        @pl.loop(k * half // band, (k + 1) * half // band)
        def _(i):
            at = pl.ds(pl.multiple_of(i * band, band), band)
            second[at, :] = norm(middle[at, :], vectors[4:5, :], vectors[5:6, :])

        pass_on(near_all, second.at[pl.ds(k * half, half)], k, 0, ns, nr)
    own = pltpu.make_async_copy(second, near_all.at[pl.ds(pl.multiple_of(me * rows, 16), rows)], loc.at[1])
    own.start()
    take_all(near_all, ns, nr)
    own_cot.wait()
    own.wait()
    for k in range(2):
        wait(cot_all.at[pl.ds(0, (count - 1) * half)], cs.at[k])
        wait(near_all.at[pl.ds(0, (count - 1) * half)], ns.at[k])


def attend(groups, count, tokens, small_all, lengths, cot, wq, wo, wkv, hidden, length):
    rows, width = tokens.shape
    any_, vmem = pl.BlockSpec(memory_space=pl.ANY), pl.BlockSpec(memory_space=pltpu.VMEM)
    dma = pltpu.SemaphoreType.DMA
    shape = jax.ShapeDtypeStruct
    return pl.pallas_call(
        partial(attend_kernel, groups, count),
        out_shape=(
            shape((count * rows, width), BF), shape((count * rows, width), BF), shape((rows, width), BF),
            shape((rows, width), BF), shape((rows, 2 * HD), BF), shape((rows, width), BF),
            shape((rows, width), F32), shape((16, width), F32), shape((1, hidden), F32),
            shape((rows, length), F32),
        ),
        in_specs=[vmem, vmem, pl.BlockSpec(memory_space=pltpu.SMEM), any_, any_, any_, any_],
        out_specs=(any_, any_) + (vmem,) * 8,
        scratch_shapes=[
            pltpu.VMEM(wq.shape, BF), pltpu.VMEM(wo.shape, BF), pltpu.VMEM(wkv.shape, BF),
            pltpu.VMEM((rows, width), BF), dma((3,)), dma((2,)), dma((2, count)), dma((2,)),
            dma((2, count)), dma((2,)),
        ],
        compiler_params=pltpu.CompilerParams(
            collective_id=3, has_side_effects=True, vmem_limit_bytes=48 * 1024 * 1024
        ),
        cost_estimate=pl.CostEstimate(flops=5_000_000_000, bytes_accessed=100_000_000, transcendentals=0),
        name="attend",
    )(tokens, small_all, lengths, cot, wq, wo, wkv)


def back_kernel(groups, count, subs, plain, sizes, share, *refs):
    n = len(subs)
    take = iter(refs)
    many = lambda k: [next(take) for _ in range(k)]
    act, slope, down_rows, wdn, normed_two, wup, wq, wo, middle_far = many(9)
    far_rows = many(4)
    keyvals, bias, gains, wkv = many(4)
    final, land = many(n), many(n)
    slices = next(take)
    input_grad = next(take)
    own_part = {m: next(take) for m in range(n) if share[m] == m}
    part = [own_part[share[m]] for m in range(n)]
    held = many(n)
    ring_of = sorted(set(sizes))
    load, outer, mid = many(len(ring_of)), many(len(ring_of)), many(len(ring_of))
    load = [load[ring_of.index(size)] for size in sizes]
    down_all, grad_hidden, strips, slices_stage, middle, grad_out, grad_mid, branch, grad_q, tiles, stage, stage_kv, grad_kv, sums, up_sums = many(15)
    attended, queries, normed, tokens = many(4)
    sib, ld, sent, came, zs, z_in, z_mid, os, z_fin, xs, xr, loc, ss, gs, gr, ws, ms, ts, ps, free_in, free_mid, ready = take
    chips = groups // 2
    g, me = lax.axis_index("grp"), lax.axis_index("shard")
    p, c = lax.div(g, 2), lax.rem(g, 2)
    low = p < chips // 2
    inn = jnp.where(low, g + 2, g - 2)
    out = jnp.where(low, g - 2, g + 2)
    end = (p == 0) | (p == chips - 1)
    middle_chip = (p == chips // 2 - 1) | (p == chips // 2)
    other = g + 1 - 2 * c
    near = near_first(count)

    barrier = pltpu.get_barrier_semaphore()

    def greet(target):
        pl.semaphore_signal(barrier, inc=1, device_id=target, device_id_type=MESH)

    greet((other, me))
    greet((inn, me))
    for q in range(1, count):
        greet((g, lax.bitwise_xor(me, q)))

    @pl.when(jnp.logical_not(end))
    def _():
        greet((out, me))

    pl.semaphore_wait(barrier, count + 2 - end.astype(jnp.int32))

    def send(src, dst, send_sem, recv_sem, target):
        pltpu.make_async_remote_copy(
            src_ref=src, dst_ref=dst, send_sem=send_sem, recv_sem=recv_sem,
            device_id=target, device_id_type=MESH,
        ).start()

    def wait(ref, sem):
        pltpu.make_async_copy(ref, ref, sem).wait()

    def add(dst, *more):
        @pl.loop(0, dst.shape[0] // 16)
        def _(i):
            at = pl.ds(pl.multiple_of(i * 16, 16), 16)
            total = dst[at].astype(F32)
            for ref in more:
                total = total + ref[at].astype(F32)
            dst[at] = total.astype(BF)

    cut = lambda m, j: pl.ds(j * sizes[m][0], sizes[m][0])
    away = lambda q: lax.bitwise_xor(me, q)

    rows, width = attended.shape
    hidden = grad_hidden.shape[1]
    everyone = down_all.shape[0]
    arrived = lambda q: down_all.at[pl.ds(q * rows, rows)]
    whole_down = pltpu.make_async_copy(down_rows, down_all, ms.at[6])
    whole_down.start()
    span = pl.ds(pl.multiple_of(me * attended.shape[0], 16), attended.shape[0])
    own_copies = [
        pltpu.make_async_copy(middle_far, middle, ms.at[0]),
        pltpu.make_async_copy(down_rows.at[span], grad_out, ms.at[1]),
    ]
    for i, (a, b) in enumerate(zip(far_rows, (attended, queries, normed, tokens))):
        own_copies.append(pltpu.make_async_copy(a, b, ms.at[2 + i]))
    for copy in own_copies:
        copy.start()

    def send_slices():
        pl.semaphore_wait(ready, count - 1)
        part_of = lambda col: slices.at[pl.ds(pl.multiple_of(col * rows, 16), rows)]
        for q in near:
            send(part_of(away(q)), arrived(q), gs.at[q], gr.at[q], (g, away(q)))
        pltpu.make_async_copy(part_of(me), arrived(0), gr.at[0]).start()


    pair_tasks = [
        [(m, j, q) for q in [0] + near for j in range(subs[m])]
        if plain[m]
        else [(m, j, q) for j in range(subs[m]) for q in near + [0]]
        for m in range(n)
    ]
    flat = [task for tasks in pair_tasks for task in tasks]

    begun, paired_set = set(), set()

    def spot(m, q):
        return part[m].at[q - 1] if q else held[m].at[me]

    def loads(k):
        m, j, q = flat[k]
        slot = k % 2
        return [pltpu.make_async_copy(land[m].at[q, cut(m, j)], load[m].at[slot], ld.at[slot])]

    def begin(k):
        m, j, q = flat[k]
        if j == 0:
            wait(land[m].at[q], sib.at[m, q])
        begun.add(k)
        for copy in loads(k):
            copy.start()

    def pair(k):
        m, j, q = flat[k]
        paired_set.add(k)
        if k not in begun:
            begin(k)
        if k + 1 < len(flat) and flat[k + 1][0] == m and (flat[k + 1][1] > j or not plain[m]):
            begin(k + 1)
        for copy in loads(k):
            copy.wait()
        ref = spot(m, q).at[cut(m, j)]
        add(ref, load[m].at[k % 2])
        if q:
            send(ref, held[m].at[me, cut(m, j)], sent.at[m], came.at[m, j, q], (g, away(q)))

    units = []
    for m in range(n):
        units += [(m, j, q) for q in ([0] + near if plain[m] else [0]) for j in range(subs[m])]
    rings = [ring_of.index(sizes[m]) for m, j, q in units]
    index = [rings[:u].count(rings[u]) for u in range(len(units))]
    total_in = [rings.count(r) for r in range(len(ring_of))]
    slot_of = lambda u: index[u] % outer[rings[u]].shape[0]
    reused = lambda u: index[u] >= outer[rings[u]].shape[0]
    again = lambda u: index[u] + outer[rings[u]].shape[0] < total_in[rings[u]]

    def value(u):
        m, j, q = units[u]
        return held[m].at[away(q), cut(m, j)]

    def result(u, half):
        m, j, q = units[u]
        return final[m].at[half, away(q) if plain[m] else 0, cut(m, j)]

    def inward(u):
        m, j, q = units[u]
        ref = value(u)
        if plain[m]:
            if q:
                wait(ref, came.at[m, j, q])
        else:
            others = [held[m].at[away(r), cut(m, j)] for r in near]
            for r, other_ref in zip(near, others):
                wait(other_ref, came.at[m, j, r])
            add(ref, *others)
        box, slot = rings[u], slot_of(u)

        @pl.when(jnp.logical_not(end))
        def _():
            wait(outer[box].at[slot], z_in.at[u])
            add(ref, outer[box].at[slot])
            if again(u):
                pl.semaphore_signal(free_in.at[box, slot], inc=1, device_id=(out, me), device_id_type=MESH)

        @pl.when(middle_chip)
        def _():
            if reused(u):
                pl.semaphore_wait(free_mid.at[box, slot], 1)
            send(ref, mid[box].at[slot], zs.at[u], z_mid.at[u], (inn, me))

        @pl.when(jnp.logical_not(middle_chip))
        def _():
            if reused(u):
                pl.semaphore_wait(free_in.at[box, slot], 1)
            send(ref, outer[box].at[slot], zs.at[u], z_in.at[u], (inn, me))

    def centre(u):
        box, slot = rings[u], slot_of(u)

        @pl.when(middle_chip)
        def _():
            ref = value(u)
            wait(ref, zs.at[u])
            wait(mid[box].at[slot], z_mid.at[u])
            add(ref, mid[box].at[slot])
            if again(u):
                pl.semaphore_signal(free_mid.at[box, slot], inc=1, device_id=(inn, me), device_id_type=MESH)
            pl.when(jnp.logical_not(end))(
                lambda: send(ref, result(u, c), os.at[u], z_fin.at[u], (out, me))
            )
            send(ref, result(u, c), xs.at[u], xr.at[u], (other, me))
            pltpu.make_async_copy(ref, result(u, c), loc.at[u]).start()

    def outward(u):
        @pl.when(jnp.logical_not(middle_chip))
        def _():
            ref = result(u, c)
            wait(ref, z_fin.at[u])
            pl.when(jnp.logical_not(end))(
                lambda: send(ref, ref, os.at[u], z_fin.at[u], (out, me))
            )
            send(ref, ref, xs.at[u], xr.at[u], (other, me))

    length = bias.shape[1]
    scale = HD**-0.5
    band = 32
    column = lambda at, size: pl.ds(pl.multiple_of(at, 128), size)

    def moments(x):
        centre_ = jnp.mean(x, axis=1, keepdims=True)
        offset = x - centre_
        rate = lax.rsqrt(jnp.mean(offset * offset, axis=1, keepdims=True) + EPS)
        return offset * rate, rate

    def clear():
        sums[...] = jnp.zeros_like(sums)
        grad_kv[...] = jnp.zeros_like(grad_kv)

    def tally(k, x):
        sums[k : k + 1, :] += jnp.sum(x, axis=0, keepdims=True)

    def second_norm(lo, hi):
        gain = gains[4:5, :]

        @pl.loop(lo, hi)
        def _(i):
            at = pl.ds(pl.multiple_of(i * band, band), band)
            grad = jnp.zeros((band, width), F32)
            for q in range(count):
                grad = grad + down_all[pl.ds(pl.multiple_of(q * rows + i * band, band), band), :].astype(F32)
            unit, rate = moments(middle[at, :])
            tally(0, grad * unit)
            tally(1, grad)
            e = grad * gain
            back = rate * (
                e - jnp.mean(e, axis=1, keepdims=True) - unit * jnp.mean(e * unit, axis=1, keepdims=True)
            )
            away_grad = grad_out[at, :].astype(F32)
            tally(7, away_grad)
            whole = back + away_grad
            grad_mid[at, :] = whole
            short = whole.astype(BF)
            branch[at, :] = short
            tally(2, short.astype(F32))

    def first_norm(lo, hi):
        gain = gains[0:1, :]

        @pl.loop(lo, hi)
        def _(i):
            at = pl.ds(pl.multiple_of(i * band, band), band)
            grad = middle[at, :]
            unit, rate = moments(tokens[at, :].astype(F32))
            tally(3, grad * unit)
            tally(4, grad)
            e = grad * gain
            back = rate * (
                e - jnp.mean(e, axis=1, keepdims=True) - unit * jnp.mean(e * unit, axis=1, keepdims=True)
            )
            input_grad[at, :] = (back + grad_mid[at, :]).astype(BF)
            tally(5, grad_q[at, :].astype(F32))

    part_cols = min(512, width)

    def outer_product(dst, left, start, size, right):
        lhs = left[:, start : start + size] if isinstance(start, int) else left[:, column(start, size)]

        @pl.loop(0, right.shape[1] // min(part_cols, right.shape[1]))
        def _(k):
            cols = column(k * min(part_cols, right.shape[1]), min(part_cols, right.shape[1]))
            dst[:, cols] = lax.dot_general(
                lhs, right[:, cols], (((0,), (0,)), ((), ())), preferred_element_type=F32
            ).astype(BF)

    staged = []

    def stage_slot(m, q, size):
        k = len(staged)
        if k >= 2:
            before = staged[k - 2]
            wait(stage.at[k % 2, pl.ds(0, sizes[before[0]][0] * subs[before[0]]), : sizes[before[0]][1]], ss.at[before[0], before[1]])
        staged.append((m, q))
        return stage.at[k % 2, pl.ds(0, size), : sizes[m][1]]

    def weight_terms(m, left, right, some):
        size = width // count // 2
        for q in some:
            slot = stage_slot(m, q, size)
            outer_product(slot, left, (away(q) * 2 + 1 - c) * size, size, right)
            send(slot, land[m].at[q], ss.at[m, q], sib.at[m, q], (other, me))
            outer_product(spot(m, q), left, (away(q) * 2 + c) * size, size, right)

    strip_jobs = []

    def strip(source, start, size):
        strip_jobs.append((source, start, size))

    def strip_copy(k):
        source, start, size = strip_jobs[k]
        return pltpu.make_async_copy(
            source.at[:, column(start, size)], strips.at[k % 2, :, pl.ds(0, size)], ts.at[k % 2]
        )

    def use_strip(k):
        strip_copy(k).wait()
        return strips.at[k % 2]

    def next_strip(k):
        if k < len(strip_jobs):
            strip_copy(k).start()

    down_size = hidden // count // 2
    up_size = width // count // 2
    tile = tiles.shape[1]
    for q in [0] + near:
        strip(act, away(q) * 2 * down_size, 2 * down_size)
    for f in range(hidden // tile):
        strip(slope, f * tile, tile)
    for q in [0] + near:
        strip(normed_two, (away(q) * 2 + 1 - c) * up_size, up_size)
        strip(normed_two, (away(q) * 2 + c) * up_size, up_size)

    def down_terms(i):
        q = ([0] + near)[i]
        if i == 0:
            whole_down.wait()
        left = use_strip(i)
        slot = stage_slot(0, q, down_size)
        for k in range(2):

            @pl.when(c == k)
            def _():
                outer_product(slot, left, (1 - k) * down_size, down_size, down_all)

        send(slot, land[0].at[q], ss.at[0, q], sib.at[0, q], (other, me))
        for k in range(2):

            @pl.when(c == k)
            def _():
                outer_product(spot(0, q), left, k * down_size, down_size, down_all)

        next_strip(i + 2)

    block = hidden // (groups)

    def hidden_tile(f):
        k = count + f
        gate = use_strip(k)
        if f + 1 < hidden // tile:
            weight_rows(wdn, f + 1, width).start()
        weight_rows(wdn, f, width).wait()
        up_sums[pl.ds(f * (tile // block), tile // block), :] = jnp.zeros((tile // block, block), F32)

        @pl.loop(0, everyone // rows)
        def _(i):
            at = pl.ds(pl.multiple_of(i * rows, rows), rows)
            got = lax.dot_general(
                down_all[at, :], tiles[f % 2], (((1,), (1,)), ((), ())), preferred_element_type=F32
            )
            low_grad = (got * gate[at, :tile].astype(F32)).astype(BF)
            grad_hidden[at, f * tile : (f + 1) * tile] = low_grad
            total = jnp.sum(low_grad.astype(F32), axis=0, keepdims=True)
            for b in range(tile // block):
                k_ = f * (tile // block) + b
                up_sums[k_ : k_ + 1, :] += total[:, b * block : (b + 1) * block]

        next_strip(k + 2)
        if f + 1 == hidden // tile:
            for q in near:
                pl.semaphore_signal(ready, inc=1, device_id=(g, away(q)), device_id_type=MESH)

    def up_terms(i):
        q = ([0] + near)[i]
        k = count + hidden // tile + 2 * i
        slot = stage_slot(1, q, up_size)
        outer_product(slot, use_strip(k), 0, up_size, grad_hidden)
        next_strip(k + 2)
        send(slot, land[1].at[q], ss.at[1, q], sib.at[1, q], (other, me))
        outer_product(spot(1, q), use_strip(k + 1), 0, up_size, grad_hidden)
        next_strip(k + 3)

    def weight_rows(source, i, size):
        return pltpu.make_async_copy(
            source.at[pl.ds(i * tile, tile)], tiles.at[i % 2, :, pl.ds(0, size)], ws.at[i % 2]
        )

    def slice_out(d):
        return pltpu.make_async_copy(
            slices_stage.at[d % 2], slices.at[:, pl.ds(d * tile, tile)], ps.at[d % 2]
        )

    def slice_tile(d):
        if d + 1 < width // tile:
            weight_rows(wup, d + 1, hidden).start()
        weight_rows(wup, d, hidden).wait()
        if d >= 2:
            slice_out(d - 2).wait()

        @pl.loop(0, everyone // rows)
        def _(i):
            at = pl.ds(pl.multiple_of(i * rows, rows), rows)
            slices_stage[d % 2, at, :] = lax.dot_general(
                grad_hidden[at, :], tiles[d % 2, :, :hidden], (((1,), (1,)), ((), ())),
                preferred_element_type=F32,
            ).astype(BF)

        slice_out(d).start()
        if d + 1 == width // tile:
            slice_out(d - 1).wait()
            slice_out(d).wait()

    tile_rows = tiles.shape[1]
    tile_count = width // tile_rows

    def weight_tile(source, i):
        at = pl.multiple_of(i * tile_rows, tile_rows)
        slot = lax.rem(i, 2)
        return pltpu.make_async_copy(source.at[pl.ds(at, tile_rows)], tiles.at[slot], ws.at[slot])

    def attention_tiles(lo, hi):
        @pl.loop(lo, hi)
        def _(i):
            pl.when(i + 1 < tile_count)(lambda: weight_tile(wo, i + 1).start())
            weight_tile(wo, i).wait()
            cols = column(i * tile_rows, tile_rows)
            grad_att = lax.dot_general(
                branch[...], tiles[lax.rem(i, 2)], (((1,), (1,)), ((), ())), preferred_element_type=F32
            ).astype(BF)
            query = queries[:, cols]
            heads = tile_rows // HD
            fold = lambda x: jnp.concatenate([x[:, h * HD : (h + 1) * HD] for h in range(heads)], axis=0)
            for m in range(rows // length):
                at = pl.ds(m * length, length)
                q = fold(query[m * length : (m + 1) * length])
                ga = fold(grad_att[m * length : (m + 1) * length])
                k, v = keyvals[at, :HD], keyvals[at, HD:]
                shut = jnp.concatenate([bias[at, :]] * heads, axis=0)
                s = lax.dot_general(q, k, (((1,), (1,)), ((), ())), preferred_element_type=F32) * scale + shut
                e = jnp.exp(s - jnp.max(s, axis=1, keepdims=True))
                probs = e / jnp.sum(e, axis=1, keepdims=True)
                gp = lax.dot_general(ga, v, (((1,), (1,)), ((), ())), preferred_element_type=F32)
                ds = (probs * (gp - jnp.sum(probs * gp, axis=1, keepdims=True))).astype(BF)
                dq = (jnp.dot(ds, k, preferred_element_type=F32) * scale).astype(BF)
                for h in range(heads):
                    grad_q[at, column(i * tile_rows + h * HD, HD)] = dq[h * length : (h + 1) * length]
                tn = (((0,), (0,)), ((), ()))
                dk = lax.dot_general(ds, q, tn, preferred_element_type=F32) * scale
                dv = lax.dot_general(probs.astype(BF), ga, tn, preferred_element_type=F32)
                grad_kv[at, :HD] += dk
                grad_kv[at, HD:] += dv

    def query_tiles(lo, hi):
        low_kv = grad_kv[...].astype(BF)

        @pl.loop(lo, hi)
        def _(i):
            pl.when(i + 1 < tile_count)(lambda: weight_tile(wq, i + 1).start())
            weight_tile(wq, i).wait()
            cols = column(i * tile_rows, tile_rows)
            nt = (((1,), (1,)), ((), ()))
            middle[:, cols] = lax.dot_general(
                grad_q[...], tiles[lax.rem(i, 2)], nt, preferred_element_type=F32
            ) + lax.dot_general(
                low_kv, wkv[pl.ds(pl.multiple_of(i * tile_rows, tile_rows), tile_rows)], nt,
                preferred_element_type=F32,
            )

    def keyval_terms():
        low_kv = grad_kv[...].astype(BF)
        size = width // count // 2
        last = n - 1
        line = jnp.sum(low_kv[:, HD:].astype(F32), axis=0, keepdims=True)
        for k in range(width // size):
            sums[6:7, k * size : k * size + HD] = line
        for q in near + [0]:
            for ref, which in ((stage_kv.at[q], 1 - c), (spot(last, q), c)):
                start = (away(q) * 2 + which) * size
                ref[pl.ds(0, size), :] = lax.dot_general(
                    normed[:, column(start, size)], low_kv, (((0,), (0,)), ((), ())),
                    preferred_element_type=F32,
                ).astype(BF)
                ref[pl.ds(size, 16), :] = jnp.zeros((16, 2 * HD), BF)
                ref[pl.ds(size, 16), :size] = sums[:, column(start, size)].astype(BF)
                mine = up_sums[pl.ds(away(q) * 2 + which, 1), :]
                mine = jnp.concatenate([mine] * (2 * HD // block), axis=1)
                flat_at = lax.broadcasted_iota(jnp.int32, (16, 2 * HD), 0) * (2 * HD)
                flat_at = flat_at + lax.broadcasted_iota(jnp.int32, (16, 2 * HD), 1)
                own_place = lax.div(flat_at, block) == me
                ref[pl.ds(size + 16, 16), :] = jnp.where(own_place, mine, 0.0).astype(BF)
            send(stage_kv.at[q], land[last].at[q], ss.at[last, q], sib.at[last, q], (other, me))

    def reuse(m):
        if share[m] != m:
            wait(part[m], sent.at[share[m]])

    bands = rows // band
    plan = {}

    def at_step(step, *work):
        plan.setdefault(step, []).extend(work)

    P_ = partial
    starts = [sum(len(t) for t in pair_tasks[:m]) for m in range(n)]
    pairs_ = lambda m, lo, hi: [P_(pair, starts[m] + k) for k in range(lo, min(hi, len(pair_tasks[m])))]
    def got_slices():
        clear()
        for copy in own_copies:
            copy.wait()
        for q in [0] + near:
            wait(arrived(q), gr.at[q])

    order = near + [0]
    quarter = lambda k: (k * bands // 4, (k + 1) * bands // 4)
    tile_of = lambda k: (k * tile_count // 8, (k + 1) * tile_count // 8)
    subs_0, subs_1 = subs[0], subs[1]

    def begin_all():
        next_strip(0)
        next_strip(1)
        down_terms(0)
        for work in pairs_(0, 0, subs_0):
            work()

    queue = []
    for i in range(1, count):
        queue += [(3.5, P_(down_terms, i))] + [(0.3, x) for x in pairs_(0, i * subs_0, (i + 1) * subs_0)]
    queue += [(0.0, lambda: weight_rows(wdn, 0, width).start())]
    queue += [(12.0 / (hidden // tile), P_(hidden_tile, f)) for f in range(hidden // tile)]
    queue += [(0.0, lambda: weight_rows(wup, 0, hidden).start())]
    queue += [(1.5, P_(slice_tile, d)) for d in range(width // tile)]
    queue += [(0.0, send_slices)]
    for i in range(count):
        queue += [(3.5, P_(up_terms, i))] + [(0.3, x) for x in pairs_(1, i * subs_1, (i + 1) * subs_1)]
    later = [(0.0, got_slices)]
    later += [(2.5, P_(second_norm, *quarter(k))) for k in range(4)]
    later += [(0.0, lambda: weight_tile(wo, 0).start()), (0.0, P_(reuse, 2))]
    later += [(16.0 / count, P_(weight_terms, 2, attended, branch, [q])) for q in order]
    pairs_2, pairs_3 = pairs_(2, 0, 99), pairs_(3, 0, 99)
    share_of = lambda work, k: [(0.4, x) for x in work[k * len(work) // 4 : (k + 1) * len(work) // 4]]
    for k in range(8):
        later += [(TILE_COST, P_(attention_tiles, *tile_of(k)))]
        later += share_of(pairs_2, k) if k < 4 else []
    later += [(0.0, lambda: weight_tile(wq, 0).start()), (0.0, P_(reuse, 3))]
    later += [(16.0 / count, P_(weight_terms, 3, normed, grad_q, [q])) for q in order]
    for k in range(8):
        later += [(0.8, P_(query_tiles, *tile_of(k)))]
        later += share_of(pairs_3, k) if k < 4 else []
    later += [(2.5, P_(first_norm, *quarter(k))) for k in range(4)]
    later += [(4.0, keyval_terms)]
    later += [(1.0, work) for work in pairs_(4, 0, 99)]
    step, spent = 0, 0.0
    for some, start in ((queue, 0), (later, NORM_STEP)):
        if start > step:
            step, spent = start, 0.0
        for cost, work in some:
            if spent + cost > BUDGET and spent:
                spent, step = 0.0, step + 1
            spent += cost
            at_step(step, work)
    needs = {}
    for m, per_unit in ((0, 1), (1, 1), (2, count), (3, count), (4, count)):
        base_unit = [u for u in range(len(units)) if units[u][0] == m][0]
        for k, work in enumerate(pair_tasks[m]):
            needs.setdefault(base_unit + k // per_unit, []).append((m, k))
    begin_all()
    cursor = [0]
    steps = max(len(units) + LAG_OUT, max(plan) + 1)
    for step in range(steps):
        if step < len(units):
            while any(starts[m] + k not in paired_set for m, k in needs[step]):
                while not plan.get(cursor[0]):
                    cursor[0] += 1
                plan[cursor[0]].pop(0)()
            inward(step)
        if 0 <= step - LAG_MID < len(units):
            centre(step - LAG_MID)
        if 0 <= step - LAG_OUT < len(units):
            outward(step - LAG_OUT)
        for at in range(cursor[0], step + 1):
            for work in plan.pop(at, ()):
                work()
        cursor[0] = max(cursor[0], step + 1)

    for m in range(n):
        if m not in share[m + 1 :]:
            wait(part[m], sent.at[m])
        for q in near + [0]:
            if m == n - 1 or (m, q) in staged[-2:]:
                wait(land[m].at[q], ss.at[m, q])
    for q in near:
        wait(arrived(q), gs.at[q])
    for u in range(len(units)):
        wait(result(u, 1 - c), xr.at[u])
        wait(result(u, c), xs.at[u])
        pl.when(jnp.logical_not(end))(partial(wait, result(u, c), os.at[u]))
        pl.when(middle_chip)(partial(wait, result(u, c), loc.at[u]))
        pl.when(jnp.logical_not(middle_chip))(partial(wait, value(u), zs.at[u]))


def back_all(groups, count, far, own, near_by):
    rows, width = own[0].shape
    everyone, hidden = far[0].shape
    size = width // count // 2
    tile = 2 * HD
    low = (size + 32, 2 * HD)
    shapes = [(hidden // count // 2, width), (size, hidden), (size, width), (size, width), low]
    plain, subs = (True, True, False, False, False), (4, 4, 4, 4, 1)
    n = len(shapes)
    sizes = [(s[0] // k, s[1]) for s, k in zip(shapes, subs)]
    share = list(range(n))
    for m in (2, 3):
        share[m] = m - 2 if shapes[m] == shapes[m - 2] else 2
    rings = sorted(set(sizes))
    units = sum(s * (count if f else 1) for s, f in zip(subs, plain))
    slots = [min(RING, sum(s * (count if f else 1) for s, f, z in zip(subs, plain, sizes) if z == r)) for r in rings]
    any_, vmem = pl.BlockSpec(memory_space=pl.ANY), pl.BlockSpec(memory_space=pltpu.VMEM)
    dma, regular = pltpu.SemaphoreType.DMA, pltpu.SemaphoreType.REGULAR
    out = [jax.ShapeDtypeStruct((2, count if f else 1) + s, BF) for s, f in zip(shapes, plain)]
    out += [jax.ShapeDtypeStruct((count,) + s, BF) for s in shapes]
    scratch = [pltpu.VMEM((count - 1,) + shapes[m], BF) for m in range(n) if share[m] == m]
    scratch += [pltpu.VMEM((count,) + s, BF) for s in shapes]
    scratch += [pltpu.VMEM((2,) + r, BF) for r in rings]
    scratch += [pltpu.VMEM((k,) + r, BF) for k, r in zip(slots, rings)] * 2
    scratch += [
        pltpu.VMEM((everyone, width), BF), pltpu.VMEM((everyone, hidden), BF),
        pltpu.VMEM((2, everyone, max(2 * hidden // count // 2, tile)), BF), pltpu.VMEM((2, everyone, tile), BF),
        pltpu.VMEM((rows, width), F32), pltpu.VMEM((rows, width), BF), pltpu.VMEM((rows, width), F32),
        pltpu.VMEM((rows, width), BF), pltpu.VMEM((rows, width), BF), pltpu.VMEM((2, tile, width), BF),
        pltpu.VMEM((2, max(s[0] for s in shapes[:4]), width), BF), pltpu.VMEM((count,) + low, BF),
        pltpu.VMEM((rows, 2 * HD), F32),
        pltpu.VMEM((16, width), F32), pltpu.VMEM((max(16, groups), hidden // groups), F32),
        pltpu.VMEM((rows, width), BF), pltpu.VMEM((rows, width), BF), pltpu.VMEM((rows, width), BF),
        pltpu.VMEM((rows, width), BF),
        dma((n, count)), dma((2,)), dma((n,)), dma((n, max(subs), count)), dma((units,)), dma((units,)),
        dma((units,)), dma((units,)), dma((units,)), dma((units,)), dma((units,)), dma((units,)),
        dma((n, count)), dma((count,)), dma((count,)), dma((2,)), dma((7,)), dma((2,)), dma((2,)),
        regular((len(rings), max(slots))), regular((len(rings), max(slots))), regular,
    ]
    got = pl.pallas_call(
        partial(back_kernel, groups, count, subs, plain, sizes, share),
        out_shape=tuple(out) + (jax.ShapeDtypeStruct((everyone, width), BF), jax.ShapeDtypeStruct((rows, width), BF)),
        in_specs=[any_] * 13 + [vmem] * 4,
        out_specs=(any_,) * (2 * n + 1) + (vmem,),
        scratch_shapes=scratch,
        compiler_params=pltpu.CompilerParams(
            collective_id=2, has_side_effects=True, vmem_limit_bytes=60 * 1024 * 1024
        ),
        cost_estimate=pl.CostEstimate(flops=0, bytes_accessed=200_000_000, transcendentals=0),
        name="back_all",
    )(*far, *own, *near_by)
    return got[:n], got[-1]


def lift_kernel(rows, weight, bias, act, slope):
    u = jnp.dot(rows[...], weight[...], preferred_element_type=F32) + bias[...]
    root = 0.7978845608028654
    t = jnp.tanh(root * (u + 0.044715 * (u * u * u)))
    half = 0.5 * (1.0 + t)
    act[...] = (u * half).astype(BF)
    slope[...] = (half + 0.5 * u * (1.0 - t * t) * (root * (1.0 + 3 * 0.044715 * (u * u)))).astype(BF)


def lift(rows, weight, bias):
    n, hidden = rows.shape[0], weight.shape[1]
    tile = 2 * HD
    out = jax.ShapeDtypeStruct((n, hidden), BF)
    column = lambda k: pl.BlockSpec((k, tile), lambda i: (0, i))
    return pl.pallas_call(
        lift_kernel,
        out_shape=(out, out),
        grid=(hidden // tile,),
        in_specs=[pl.BlockSpec(rows.shape, lambda i: (0, 0)), column(weight.shape[0]), column(1)],
        out_specs=(column(n), column(n)),
        compiler_params=pltpu.CompilerParams(vmem_limit_bytes=48 * 1024 * 1024),
        name="lift",
    )(rows, weight, bias)


def widen_kernel(block, size, down, up, out, query, low, o_down, o_up, o_out, o_query, o_low, *lines):
    o_down[...] = down[...].astype(F32)
    o_out[...] = out[...].astype(F32)
    o_query[...] = query[...].astype(F32)
    _, count, rows, hidden = up.shape
    for source in range(count):
        for k in range(hidden // block):
            o_up[:, pl.ds((k * count + source) * block, block)] = up[0, source, :, pl.ds(k * block, block)].astype(F32)

    @pl.when(pl.program_id(0) == 0)
    def _():
        for half in range(2):
            o_low[half * size : (half + 1) * size, :] = low[half, :size, :].astype(F32)
            sums = low[half, size : size + 16, :size].astype(F32)
            for v in range(8):
                lines[v][:, half * size : (half + 1) * size] = sums[v : v + 1, :]
            tail = low[half, size + 16 :, :].astype(F32)
            wide = tail.shape[1]
            for r in range(hidden // 2 // wide):
                start = half * hidden // 2 + r * wide
                lines[8][:, start : start + wide] = tail[r : r + 1, :]


def widen(full, block):
    down, up, out, query, low = full
    flat = lambda x: x.reshape(-1, x.shape[-1])
    down, out, query, low = flat(down), flat(out), flat(query), low[:, 0]
    _, count, rows, hidden = up.shape
    steps = 16
    step = 2 * rows // steps
    size = out.shape[0] // 2
    row = lambda x: pl.BlockSpec((x.shape[0] // steps, x.shape[1]), lambda i: (i, 0))
    still = lambda *shape: pl.BlockSpec(shape, lambda i: (0,) * len(shape))
    shape = lambda *dims: jax.ShapeDtypeStruct(dims, F32)
    vectors = [(1, 2 * size)] * 8 + [(1, hidden)]
    return pl.pallas_call(
        partial(widen_kernel, block, size),
        out_shape=(
            shape(*down.shape), shape(2 * rows, count * hidden), shape(*out.shape), shape(*query.shape),
            shape(2 * size, low.shape[2]),
        ) + tuple(shape(*v) for v in vectors),
        grid=(steps,),
        in_specs=[
            row(down), pl.BlockSpec((1, count, step, hidden), lambda i: (i // (steps // 2), 0, i % (steps // 2), 0)),
            row(out), row(query), still(*low.shape),
        ],
        out_specs=(
            row(down), pl.BlockSpec((step, count * hidden), lambda i: (i, 0)), row(out), row(query),
            still(2 * size, low.shape[2]),
        ) + tuple(still(*v) for v in vectors),
        name="widen",
    )(down, up, out, query, low)


def used(lengths, row):
    total = lengths[row, 0]
    for k in range(1, lengths.shape[1]):
        total = total + lengths[row, k]
    return total


def masked(x, lengths, row):
    places = lax.broadcasted_iota(jnp.int32, x.shape, 0)
    return jnp.where(places < used(lengths, row), x, 0.0)


def take_kernel(order, lengths, x, out):
    out[0] = masked(x[0].astype(F32), lengths, pl.program_id(0)).astype(BF)


def take_rows(values, order, lengths):
    _, length, width = values.shape
    spec = lambda f: pl.BlockSpec((1, length, width), f)
    return pl.pallas_call(
        take_kernel,
        out_shape=jax.ShapeDtypeStruct(values.shape, BF),
        grid_spec=pltpu.PrefetchScalarGridSpec(
            num_scalar_prefetch=2,
            grid=(values.shape[0],),
            in_specs=[spec(lambda r, order, lengths: (order[r], 0, 0))],
            out_specs=spec(lambda r, order, lengths: (r, 0, 0)),
        ),
        name="take_rows",
    )(order, lengths, values)


def finish_kernel(deal, lengths, place, x, middle, table, out):
    row = deal[pl.program_id(0)]
    micro = middle.shape[0]
    term = x[0].astype(F32)
    own = lax.div(row, micro) == place[0]

    @pl.when(own)
    def _():
        whole = term + middle[lax.rem(row, micro)] + table[6:7, :]
        out[0] = masked(whole, lengths, row).astype(BF)

    @pl.when(jnp.logical_not(own))
    def _():
        out[0] = masked(term, lengths, row).astype(BF)


def finish_rows(values, deal, lengths, me, middle, table):
    _, length, width = values.shape
    spec = lambda f: pl.BlockSpec((1, length, width), f)
    return pl.pallas_call(
        finish_kernel,
        out_shape=jax.ShapeDtypeStruct(values.shape, BF),
        grid_spec=pltpu.PrefetchScalarGridSpec(
            num_scalar_prefetch=3,
            grid=(values.shape[0],),
            in_specs=[
                spec(lambda j, deal, lengths, me: (deal[j], 0, 0)),
                pl.BlockSpec(middle.shape, lambda j, deal, lengths, me: (0, 0, 0)),
                pl.BlockSpec(table.shape, lambda j, deal, lengths, me: (0, 0)),
            ],
            out_specs=spec(lambda j, deal, lengths, me: (j, 0, 0)),
        ),
        name="finish_rows",
    )(deal, lengths, me.reshape(1), values, middle, table)


def cut_kernel(groups, count, block, x, out):
    for to in range(count):
        for k in range(groups):
            out[to, :, k * block : (k + 1) * block] = x[:, (k * count + to) * block : (k * count + to + 1) * block]


def shards(
    groups,
    count,
    tokens,
    cotangent,
    lengths,
    dealing,
    first_gain,
    first_shift,
    query_weight,
    query_bias,
    keyval_weight,
    value_bias,
    out_weight,
    out_bias,
    second_gain,
    second_shift,
    up_weight,
    up_bias,
    down_weight,
    down_bias,
):
    both = ("grp", "shard")
    micro, length, width = tokens.shape
    group_rows = dealing.shape[0]
    group = lax.axis_index("grp")
    me = lax.axis_index("shard")
    half = micro // 2
    block = down_weight.shape[0]
    hidden = block * groups
    rows = micro * length

    deal = dealing - group * group_rows
    steps = jnp.arange(group_rows, dtype=jnp.int32)
    inverse = jnp.sum(jnp.where(deal[:, None] == steps[None, :], steps[:, None], 0), axis=0)

    line = lambda x: jnp.pad(x, (0, 128 - x.shape[0]))
    piece = first_gain.shape[0]
    device = group * count + me
    value_line = lax.dynamic_update_slice(
        jnp.zeros((128,), BF), value_bias, (device * value_bias.shape[0],)
    )
    small = [first_gain, first_shift, query_bias, out_bias, second_gain, second_shift, down_bias]
    small = [line(x) for x in small] + [value_line]
    small += [line(up_bias[k * piece : (k + 1) * piece]) for k in range(block // piece)]
    small = jnp.stack(small + [jnp.zeros((128,), BF)] * (16 - len(small)))
    up_rows = up_weight.shape[0]
    up_cut = pl.pallas_call(
        partial(cut_kernel, groups, count, block),
        out_shape=jax.ShapeDtypeStruct((count, up_rows, hidden), BF),
        name="cut",
    )(up_weight)
    weight_query, weight_out, weight_keyval, small_all, weight_up = gather_all(
        groups, count, query_weight, out_weight, keyval_weight, small, up_cut
    )
    weight_query, weight_out, weight_up, down_weight = lax.optimization_barrier(
        (weight_query, weight_out, weight_up, down_weight)
    )
    weight_down = lax.all_gather(down_weight, "grp", axis=0, tiled=True)

    flat_tokens = tokens.reshape(rows, width)
    (
        normed_two, cot_rows, normed_one, queries, keyvals, attended, middle, table, up_part, bias,
    ) = attend(
        groups, count, flat_tokens, small_all, lengths, cotangent.reshape(rows, width),
        weight_query, weight_out, weight_keyval, hidden, length,
    )
    grad_down = take_rows(cot_rows.reshape(group_rows, length, width), inverse, lengths)
    grad_down = grad_down.reshape(group_rows * length, width)

    activated, slope = lift(normed_two, weight_up, up_part)
    result = mm(activated, weight_down).astype(BF).reshape(group_rows, length, width)
    result = finish_rows(result, deal, lengths, me, middle.reshape(micro, length, width), table)
    block_output = lax.psum_scatter(
        result.reshape(group_rows * length, width), "shard", scatter_dimension=0, tiled=True
    ).reshape(micro, length, width)

    full, input_grad = back_all(
        groups, count,
        (activated, slope, grad_down, weight_down, normed_two, weight_up, weight_query, weight_out, middle),
        (attended, queries, normed_one, flat_tokens), (keyvals, bias, table, weight_keyval),
    )
    input_grad = input_grad.reshape(micro, length, width)

    down_full, up_full, out_full, query_full, keyval_full, *lines = widen(full, block)
    lines = [line.reshape(-1) for line in lines]
    gain_two_grad, shift_two_grad, out_bias_grad, gain_one_grad, shift_one_grad, query_bias_grad = lines[:6]
    short = value_bias.shape[0] * groups
    value_bias_grad = lax.dynamic_slice(lines[6], (me * short,), (short,))
    down_bias_grad, up_bias_grad = lines[7:]

    return (
        block_output, input_grad, gain_one_grad, shift_one_grad, query_full, query_bias_grad, keyval_full,
        value_bias_grad, out_full, out_bias_grad, gain_two_grad, shift_two_grad, up_full, up_bias_grad,
        down_full, down_bias_grad,
    )


def solution(mesh):
    rows = P(("grp", "shard"), None, None)
    flat = P(("grp", "shard"))
    tall = P(("grp", "shard"), None)
    vector, matrix = P("shard"), P("shard", None)
    return jax.shard_map(
        partial(shards, mesh.shape["grp"], mesh.shape["shard"]),
        mesh=mesh,
        in_specs=(
            rows, rows, P("grp", None), P("grp"), flat, flat, tall, flat, tall, flat,
            tall, flat, flat, flat, tall, flat, tall, flat,
        ),
        out_specs=(
            rows, rows, vector, vector, matrix, vector, matrix, vector,
            matrix, vector, vector, vector, matrix, vector, matrix, vector,
        ),
        check_vma=False,
    )
```

```python
from functools import partial

import jax
import jax.numpy as jnp
from jax import lax
from jax.experimental import pallas as pl
from jax.experimental.pallas import tpu as pltpu
from jax.sharding import PartitionSpec as P

HEADS = 16
HD = 128
EPS = 1e-05
NEGATIVE = -1e30
BF = jnp.bfloat16
F32 = jnp.float32
MESH = pl.DeviceIdType.MESH
LAG_MID = 2
LAG_OUT = 6
BUDGET = 8.0
TILE_COST = 4.0
NORM_STEP = 15
RING = 6


def cube_tree(count, parity, q):
    order = list(range(count.bit_length() - 1))
    if parity:
        order = order[::-1]
    at = max([i for i, d in enumerate(order) if q >> d & 1], default=-1)
    return [1 << d for d in order[at + 1 :]]


def near_first(count):
    return sorted(range(1, count), key=lambda q: (bin(q).count("1"), q))


def gather_kernel(
    groups, count, wq, wo, wkv, small, upc, q_all, o_all, kv_all, small_all, up_all,
    zs, zr, ps, pr, bs, br, us, ur, loc,
):
    chips = groups // 2
    g, me = lax.axis_index("grp"), lax.axis_index("shard")
    p, c = lax.div(g, 2), lax.rem(g, 2)

    barrier = pltpu.get_barrier_semaphore()

    def greet(target):
        pl.semaphore_signal(barrier, inc=1, device_id=target, device_id_type=MESH)

    greet((g + 1 - 2 * c, me))
    for q in range(1, count):
        greet((g, lax.bitwise_xor(me, q)))

    @pl.when(p < chips - 1)
    def _():
        greet((g + 2, me))

    @pl.when(p > 0)
    def _():
        greet((g - 2, me))

    ends = (p == 0).astype(jnp.int32) + (p == chips - 1).astype(jnp.int32)
    pl.semaphore_wait(barrier, count + 2 - ends)

    def send(src, dst, send_sem, recv_sem, target):
        pltpu.make_async_remote_copy(
            src_ref=src, dst_ref=dst, send_sem=send_sem, recv_sem=recv_sem,
            device_id=target, device_id_type=MESH,
        ).start()

    def wait(ref, sem):
        pltpu.make_async_copy(ref, ref, sem).wait()

    own = (wq, wo, wkv, small)
    whole = (q_all, o_all, kv_all, small_all)
    parity = (0, 1, 0, 1)
    size = [x.shape[0] for x in own]
    full = len(own)
    cuts = (full, full + 1)
    up_size = upc.shape[1]
    up_half = up_size * count // 2

    def spot(a, z, col):
        if a < full:
            at = ((z * 2 + c) * count + col) * size[a]
            return whole[a].at[pl.ds(pl.multiple_of(at, 16), size[a])]
        at = (z * 2 + c) * up_half * 2 + (a - full) * up_half
        return up_all.at[pl.ds(pl.multiple_of(at, 16), up_half)]

    def along(a, way, hop, src, z):
        step = 1 - 2 * way
        send(src, spot(a, z, me), zs.at[a, way, hop], zr.at[a, way, hop], (g + 2 * step, me))

    def across(a, src, z, q):
        for m in cube_tree(count, parity[a], q):
            send(
                src, spot(a, z, lax.bitwise_xor(me, q)), ps.at[a], pr.at[a, z, q ^ m],
                (g, lax.bitwise_xor(me, m)),
            )

    def aside(a, src, z, q):
        send(src, spot(a, z, lax.bitwise_xor(me, q)), bs.at[a], br.at[a], (g + 1 - 2 * c, me))

    def may_send(way, hop):
        if way == 0:
            return (p >= hop - 1) & (p < chips - 1)
        return (p + hop - 1 <= chips - 1) & (p > 0)

    def may_take(way, hop):
        return p >= hop if way == 0 else p + hop <= chips - 1

    up_rows = lambda col: up_all.at[pl.ds(pl.multiple_of((g * count + col) * up_size, 16), up_size)]
    for q in near_first(count):
        to = lax.bitwise_xor(me, q)
        send(upc.at[to], up_rows(me), us, ur.at[q], (g, to))
    mine = [pltpu.make_async_copy(upc.at[me], up_rows(me), loc.at[full])]
    for a in range(full):
        mine.append(pltpu.make_async_copy(own[a], spot(a, p, me), loc.at[a]))
    for copy in mine:
        copy.start()

    def first(a, src):
        for way in range(2):
            pl.when(may_send(way, 1))(partial(along, a, way, 1, src, p))
        aside(a, src, p, 0)

    for a in range(full):
        first(a, own[a])
        across(a, own[a], p, 0)
    mine[0].wait()
    for q in near_first(count):
        wait(up_rows(me), ur.at[q])
    for a in cuts:
        first(a, spot(a, p, me))

    def plane(z, far):
        for q in near_first(count):
            if far != (q & (q - 1) != 0):
                continue
            for a in range(full):
                ref = spot(a, z, lax.bitwise_xor(me, q))
                wait(ref, pr.at[a, z, q])
                across(a, ref, z, q)
                aside(a, ref, z, q)

    def planes(hop, far):
        if hop == 0:
            plane(p, far)
            return
        for way in range(2):
            z = p - hop if way == 0 else p + hop
            pl.when(may_take(way, hop))(partial(plane, z, far))

    def arrive(a, hop):
        for way in range(2):

            @pl.when(may_take(way, hop))
            def _():
                z = p - hop if way == 0 else p + hop
                ref = spot(a, z, me)
                wait(ref, zr.at[a, way, hop])
                if hop + 1 < chips:
                    pl.when(may_send(way, hop + 1))(
                        partial(along, a, way, hop + 1, ref, z)
                    )
                if a < full:
                    across(a, ref, z, 0)
                aside(a, ref, z, 0)

    for hop in range(1, chips):
        for a in range(full):
            arrive(a, hop)
        planes(hop - 1, False)
        if hop > 1:
            planes(hop - 2, True)
        for a in cuts:
            arrive(a, hop)
    planes(chips - 1, False)
    for hop in (chips - 2, chips - 1):
        planes(hop, True)

    for copy in mine[1:]:
        copy.wait()
    for a in range(full + 2):
        for way in range(2):
            for hop in range(1, chips):
                pl.when(may_send(way, hop))(
                    partial(wait, spot(a, p, me), zs.at[a, way, hop])
                )
    for a in range(full):
        wait(whole[a].at[pl.ds(0, chips * (count - 1) * size[a])], ps.at[a])
        wait(whole[a].at[pl.ds(0, chips * count * size[a])], bs.at[a])
        wait(whole[a].at[pl.ds(0, chips * count * size[a])], br.at[a])
    for a in cuts:
        wait(up_all.at[pl.ds(0, chips * up_half)], bs.at[a])
        wait(up_all.at[pl.ds(0, chips * up_half)], br.at[a])
    wait(up_all.at[pl.ds(0, (count - 1) * up_size)], us)


def gather_all(groups, count, wq, wo, wkv, small, upc):
    chips = groups // 2
    n = groups * count
    any_ = pl.BlockSpec(memory_space=pl.ANY)
    dma = pltpu.SemaphoreType.DMA
    tall = lambda x: jax.ShapeDtypeStruct((n * x.shape[0], x.shape[1]), x.dtype)
    return pl.pallas_call(
        partial(gather_kernel, groups, count),
        out_shape=(
            tall(wq), tall(wo), tall(wkv), tall(small),
            jax.ShapeDtypeStruct((n * upc.shape[1], upc.shape[2]), upc.dtype),
        ),
        in_specs=[any_] * 5,
        out_specs=(any_,) * 5,
        scratch_shapes=[
            dma((6, 2, chips)), dma((6, 2, chips)), dma((4,)), dma((4, chips, count)),
            dma((6,)), dma((6,)), dma, dma((count,)), dma((5,)),
        ],
        compiler_params=pltpu.CompilerParams(collective_id=1, has_side_effects=True),
        cost_estimate=pl.CostEstimate(flops=0, bytes_accessed=100_000_000, transcendentals=0),
        name="gather_all",
    )(wq, wo, wkv, small, upc)


def attend_kernel(
    groups, count, tokens, small_all, lengths, cot, wq, wo, wkv,
    near_all, cot_all, normed, queries, keyvals, attended, middle, vectors, up_part, bias,
    wq_v, wo_v, wkv_v, second, ws, ns, nr, cs, cr, loc,
):
    g, me = lax.axis_index("grp"), lax.axis_index("shard")
    barrier = pltpu.get_barrier_semaphore()
    nearest = [1 << d for d in range(count.bit_length() - 1)]
    for m in nearest:
        pl.semaphore_signal(
            barrier, inc=1, device_id=(g, lax.bitwise_xor(me, m)), device_id_type=MESH
        )
    pl.semaphore_wait(barrier, len(nearest))

    loads = [
        pltpu.make_async_copy(a, b, ws.at[i])
        for i, (a, b) in enumerate(((wkv, wkv_v), (wq, wq_v), (wo, wo_v)))
    ]
    for load in loads:
        load.start()

    rows, width = tokens.shape
    length = bias.shape[1]
    half = rows // 2
    near = near_first(count)
    place = lambda ref, k, col: ref.at[pl.ds(pl.multiple_of(col * rows + k * half, 16), half)]

    def send(src, dst, send_sem, recv_sem, m):
        pltpu.make_async_remote_copy(
            src_ref=src, dst_ref=dst, send_sem=send_sem, recv_sem=recv_sem,
            device_id=(g, lax.bitwise_xor(me, m)), device_id_type=MESH,
        ).start()

    def wait(ref, sem):
        pltpu.make_async_copy(ref, ref, sem).wait()

    def pass_on(ref, src, k, q, sends, gets):
        for m in cube_tree(count, k, q):
            send(src, place(ref, k, lax.bitwise_xor(me, q)), sends.at[k], gets.at[k, q ^ m], m)

    def take(ref, sends, gets, far):
        for q in near:
            if far != (q & (q - 1) != 0):
                continue
            for k in range(2):
                got = place(ref, k, lax.bitwise_xor(me, q))
                wait(got, gets.at[k, q])
                pass_on(ref, got, k, q, sends, gets)

    for k in range(2):
        pass_on(cot_all, cot.at[pl.ds(k * half, half)], k, 0, cs, cr)
    own_cot = pltpu.make_async_copy(cot, cot_all.at[pl.ds(pl.multiple_of(me * rows, 16), rows)], loc.at[0])
    own_cot.start()

    lot = small_all.shape[0] // (groups * count)
    piece = width // (groups * count)
    join = 128 // piece
    for k in range(width // 128):
        parts = [
            small_all[(k * join + i) * lot : (k * join + i) * lot + 16, :piece].astype(F32) for i in range(join)
        ]
        vectors[:, k * 128 : (k + 1) * 128] = jnp.concatenate(parts, axis=1)
    total = small_all[0:16, :].astype(F32)
    for d in range(1, groups * count):
        total = total + small_all[d * lot : d * lot + 16, :].astype(F32)
    vectors[7:8, :128] = total[7:8, :]
    pieces = []
    for k in range(groups):
        at = pl.multiple_of((k * count + me) * lot, 16)
        mine = small_all[pl.ds(at, 16), :].astype(F32)
        pieces += [mine[8 + r : 9 + r, :piece] for r in range(up_part.shape[1] // groups // piece)]
    for k in range(up_part.shape[1] // 128):
        up_part[:, k * 128 : (k + 1) * 128] = jnp.concatenate(pieces[k * join : (k + 1) * join], axis=1)

    band = 32
    spots = [lax.broadcasted_iota(jnp.int32, (length, length), d) for d in range(2)]
    for m in range(rows // length):
        segments = [jnp.zeros((length, length), jnp.int32)] * 2
        stop = 0
        for k in range(lengths.shape[1]):
            stop = stop + lengths[me * (rows // length) + m, k]
            segments = [a + (spot >= stop).astype(jnp.int32) for a, spot in zip(segments, spots)]
        allowed = (segments[0] == segments[1]) & (spots[1] <= spots[0])
        bias[m * length : (m + 1) * length, :] = jnp.where(allowed, 0.0, NEGATIVE)

    def norm(x, gain, shift):
        offset = x - jnp.mean(x, axis=1, keepdims=True)
        rate = lax.rsqrt(jnp.mean(offset * offset, axis=1, keepdims=True) + EPS)
        return (offset * rate * gain + shift).astype(BF)

    @pl.loop(0, rows // band)
    def _(i):
        at = pl.ds(pl.multiple_of(i * band, band), band)
        normed[at, :] = norm(tokens[at, :].astype(F32), vectors[0:1, :], vectors[1:2, :])

    loads[0].wait()
    kv = jnp.dot(normed[...], wkv_v[...], preferred_element_type=F32)
    keyvals[:, :HD] = kv[:, :HD].astype(BF)
    keyvals[:, HD:] = (kv[:, HD:] + vectors[7:8, :HD]).astype(BF)
    loads[1].wait()
    tile = 2 * HD
    scale = HD**-0.5
    fold = lambda x: jnp.concatenate([x[:, h * HD : (h + 1) * HD] for h in range(tile // HD)], axis=0)

    @pl.loop(0, width // tile)
    def _(i):
        cols = pl.ds(pl.multiple_of(i * tile, tile), tile)
        query = jnp.dot(normed[...], wq_v[:, cols], preferred_element_type=F32)
        query = (query + vectors[2:3, cols]).astype(BF)
        queries[:, cols] = query
        for m in range(rows // length):
            at = pl.ds(m * length, length)
            q = fold(query[m * length : (m + 1) * length])
            k, v = keyvals[at, :HD], keyvals[at, HD:]
            shut = jnp.concatenate([bias[at, :]] * (tile // HD), axis=0)
            s = lax.dot_general(q, k, (((1,), (1,)), ((), ())), preferred_element_type=F32) * scale + shut
            e = jnp.exp(s - jnp.max(s, axis=1, keepdims=True))
            probs = (e / jnp.sum(e, axis=1, keepdims=True)).astype(BF)
            got = jnp.dot(probs, v, preferred_element_type=F32).astype(BF)
            for h in range(tile // HD):
                attended[at, pl.ds(pl.multiple_of(i * tile + h * HD, HD), HD)] = got[
                    h * length : (h + 1) * length
                ]

    take(cot_all, cs, cr, False)
    loads[2].wait()
    wide = min(512, width)

    @pl.loop(0, width // wide)
    def _(i):
        cols = pl.ds(pl.multiple_of(i * wide, wide), wide)
        branch = jnp.dot(attended[...], wo_v[:, cols], preferred_element_type=F32)
        middle[:, cols] = tokens[:, cols].astype(F32) + branch + vectors[3:4, cols]

    for k in range(2):

        @pl.loop(k * half // band, (k + 1) * half // band)
        def _(i):
            at = pl.ds(pl.multiple_of(i * band, band), band)
            second[at, :] = norm(middle[at, :], vectors[4:5, :], vectors[5:6, :])

        pass_on(near_all, second.at[pl.ds(k * half, half)], k, 0, ns, nr)
    own = pltpu.make_async_copy(second, near_all.at[pl.ds(pl.multiple_of(me * rows, 16), rows)], loc.at[1])
    own.start()
    take(cot_all, cs, cr, True)
    take(near_all, ns, nr, False)
    take(near_all, ns, nr, True)
    own_cot.wait()
    own.wait()
    for k in range(2):
        wait(cot_all.at[pl.ds(0, (count - 1) * half)], cs.at[k])
        wait(near_all.at[pl.ds(0, (count - 1) * half)], ns.at[k])


def attend(groups, count, tokens, small_all, lengths, cot, wq, wo, wkv, hidden, length):
    rows, width = tokens.shape
    any_, vmem = pl.BlockSpec(memory_space=pl.ANY), pl.BlockSpec(memory_space=pltpu.VMEM)
    dma = pltpu.SemaphoreType.DMA
    shape = jax.ShapeDtypeStruct
    return pl.pallas_call(
        partial(attend_kernel, groups, count),
        out_shape=(
            shape((count * rows, width), BF), shape((count * rows, width), BF), shape((rows, width), BF),
            shape((rows, width), BF), shape((rows, 2 * HD), BF), shape((rows, width), BF),
            shape((rows, width), F32), shape((16, width), F32), shape((1, hidden), F32),
            shape((rows, length), F32),
        ),
        in_specs=[vmem, vmem, pl.BlockSpec(memory_space=pltpu.SMEM), any_, any_, any_, any_],
        out_specs=(any_, any_) + (vmem,) * 8,
        scratch_shapes=[
            pltpu.VMEM(wq.shape, BF), pltpu.VMEM(wo.shape, BF), pltpu.VMEM(wkv.shape, BF),
            pltpu.VMEM((rows, width), BF), dma((3,)), dma((2,)), dma((2, count)), dma((2,)),
            dma((2, count)), dma((2,)),
        ],
        compiler_params=pltpu.CompilerParams(
            collective_id=3, has_side_effects=True, vmem_limit_bytes=48 * 1024 * 1024
        ),
        cost_estimate=pl.CostEstimate(flops=5_000_000_000, bytes_accessed=100_000_000, transcendentals=0),
        name="attend",
    )(tokens, small_all, lengths, cot, wq, wo, wkv)


def back_kernel(groups, count, subs, plain, sizes, share, *refs):
    n = len(subs)
    take = iter(refs)
    many = lambda k: [next(take) for _ in range(k)]
    act, slope, down_rows, wdn, normed_two, wup, wq, wo, middle_far = many(9)
    far_rows = many(4)
    keyvals, bias, gains, wkv = many(4)
    final, land = many(n), many(n)
    slices = next(take)
    input_grad = next(take)
    own_part = {m: next(take) for m in range(n) if share[m] == m}
    part = [own_part[share[m]] for m in range(n)]
    held = many(n)
    ring_of = sorted(set(sizes))
    load, outer, mid = many(len(ring_of)), many(len(ring_of)), many(len(ring_of))
    load = [load[ring_of.index(size)] for size in sizes]
    down_all, grad_hidden, strips, slices_stage, middle, grad_out, grad_mid, branch, grad_q, tiles, stage, stage_kv, grad_kv, sums, up_sums = many(15)
    attended, queries, normed, tokens = many(4)
    sib, ld, sent, came, zs, z_in, z_mid, os, z_fin, xs, xr, loc, ss, gs, gr, ws, ms, ts, ps, free_in, free_mid, ready = take
    chips = groups // 2
    g, me = lax.axis_index("grp"), lax.axis_index("shard")
    p, c = lax.div(g, 2), lax.rem(g, 2)
    low = p < chips // 2
    inn = jnp.where(low, g + 2, g - 2)
    out = jnp.where(low, g - 2, g + 2)
    end = (p == 0) | (p == chips - 1)
    middle_chip = (p == chips // 2 - 1) | (p == chips // 2)
    other = g + 1 - 2 * c
    near = near_first(count)

    barrier = pltpu.get_barrier_semaphore()

    def greet(target):
        pl.semaphore_signal(barrier, inc=1, device_id=target, device_id_type=MESH)

    greet((other, me))
    greet((inn, me))
    for q in range(1, count):
        greet((g, lax.bitwise_xor(me, q)))

    @pl.when(jnp.logical_not(end))
    def _():
        greet((out, me))

    pl.semaphore_wait(barrier, count + 2 - end.astype(jnp.int32))

    def send(src, dst, send_sem, recv_sem, target):
        pltpu.make_async_remote_copy(
            src_ref=src, dst_ref=dst, send_sem=send_sem, recv_sem=recv_sem,
            device_id=target, device_id_type=MESH,
        ).start()

    def wait(ref, sem):
        pltpu.make_async_copy(ref, ref, sem).wait()

    def add(dst, *more):
        @pl.loop(0, dst.shape[0] // 16)
        def _(i):
            at = pl.ds(pl.multiple_of(i * 16, 16), 16)
            total = dst[at].astype(F32)
            for ref in more:
                total = total + ref[at].astype(F32)
            dst[at] = total.astype(BF)

    cut = lambda m, j: pl.ds(j * sizes[m][0], sizes[m][0])
    away = lambda q: lax.bitwise_xor(me, q)

    rows, width = attended.shape
    hidden = grad_hidden.shape[1]
    everyone = down_all.shape[0]
    arrived = lambda q: down_all.at[pl.ds(q * rows, rows)]
    whole_down = pltpu.make_async_copy(down_rows, down_all, ms.at[6])
    whole_down.start()
    span = pl.ds(pl.multiple_of(me * attended.shape[0], 16), attended.shape[0])
    own_copies = [
        pltpu.make_async_copy(middle_far, middle, ms.at[0]),
        pltpu.make_async_copy(down_rows.at[span], grad_out, ms.at[1]),
    ]
    for i, (a, b) in enumerate(zip(far_rows, (attended, queries, normed, tokens))):
        own_copies.append(pltpu.make_async_copy(a, b, ms.at[2 + i]))
    for copy in own_copies:
        copy.start()

    def send_slices():
        pl.semaphore_wait(ready, count - 1)
        part_of = lambda col: slices.at[pl.ds(pl.multiple_of(col * rows, 16), rows)]
        for q in near:
            send(part_of(away(q)), arrived(q), gs.at[q], gr.at[q], (g, away(q)))
        pltpu.make_async_copy(part_of(me), arrived(0), gr.at[0]).start()


    pair_tasks = [
        [(m, j, q) for q in [0] + near for j in range(subs[m])]
        if plain[m]
        else [(m, j, q) for j in range(subs[m]) for q in near + [0]]
        for m in range(n)
    ]
    flat = [task for tasks in pair_tasks for task in tasks]

    begun, paired_set = set(), set()

    def spot(m, q):
        return part[m].at[q - 1] if q else held[m].at[me]

    def loads(k):
        m, j, q = flat[k]
        slot = k % 2
        return [pltpu.make_async_copy(land[m].at[q, cut(m, j)], load[m].at[slot], ld.at[slot])]

    def begin(k):
        m, j, q = flat[k]
        if j == 0:
            wait(land[m].at[q], sib.at[m, q])
        begun.add(k)
        for copy in loads(k):
            copy.start()

    def pair(k):
        m, j, q = flat[k]
        paired_set.add(k)
        if k not in begun:
            begin(k)
        if k + 1 < len(flat) and flat[k + 1][0] == m and (flat[k + 1][1] > j or not plain[m]):
            begin(k + 1)
        for copy in loads(k):
            copy.wait()
        ref = spot(m, q).at[cut(m, j)]
        add(ref, load[m].at[k % 2])
        if q:
            send(ref, held[m].at[me, cut(m, j)], sent.at[m], came.at[m, j, q], (g, away(q)))

    units = []
    for m in range(n):
        units += [(m, j, q) for q in ([0] + near if plain[m] else [0]) for j in range(subs[m])]
    rings = [ring_of.index(sizes[m]) for m, j, q in units]
    index = [rings[:u].count(rings[u]) for u in range(len(units))]
    total_in = [rings.count(r) for r in range(len(ring_of))]
    slot_of = lambda u: index[u] % outer[rings[u]].shape[0]
    reused = lambda u: index[u] >= outer[rings[u]].shape[0]
    again = lambda u: index[u] + outer[rings[u]].shape[0] < total_in[rings[u]]

    def value(u):
        m, j, q = units[u]
        return held[m].at[away(q), cut(m, j)]

    def result(u, half):
        m, j, q = units[u]
        return final[m].at[half, away(q) if plain[m] else 0, cut(m, j)]

    def inward(u):
        m, j, q = units[u]
        ref = value(u)
        if plain[m]:
            if q:
                wait(ref, came.at[m, j, q])
        else:
            others = [held[m].at[away(r), cut(m, j)] for r in near]
            for r, other_ref in zip(near, others):
                wait(other_ref, came.at[m, j, r])
            add(ref, *others)
        box, slot = rings[u], slot_of(u)

        @pl.when(jnp.logical_not(end))
        def _():
            wait(outer[box].at[slot], z_in.at[u])
            add(ref, outer[box].at[slot])
            if again(u):
                pl.semaphore_signal(free_in.at[box, slot], inc=1, device_id=(out, me), device_id_type=MESH)

        @pl.when(middle_chip)
        def _():
            if reused(u):
                pl.semaphore_wait(free_mid.at[box, slot], 1)
            send(ref, mid[box].at[slot], zs.at[u], z_mid.at[u], (inn, me))

        @pl.when(jnp.logical_not(middle_chip))
        def _():
            if reused(u):
                pl.semaphore_wait(free_in.at[box, slot], 1)
            send(ref, outer[box].at[slot], zs.at[u], z_in.at[u], (inn, me))

    def centre(u):
        box, slot = rings[u], slot_of(u)

        @pl.when(middle_chip)
        def _():
            ref = value(u)
            wait(ref, zs.at[u])
            wait(mid[box].at[slot], z_mid.at[u])
            add(ref, mid[box].at[slot])
            if again(u):
                pl.semaphore_signal(free_mid.at[box, slot], inc=1, device_id=(inn, me), device_id_type=MESH)
            pl.when(jnp.logical_not(end))(
                lambda: send(ref, result(u, c), os.at[u], z_fin.at[u], (out, me))
            )
            send(ref, result(u, c), xs.at[u], xr.at[u], (other, me))
            pltpu.make_async_copy(ref, result(u, c), loc.at[u]).start()

    def outward(u):
        @pl.when(jnp.logical_not(middle_chip))
        def _():
            ref = result(u, c)
            wait(ref, z_fin.at[u])
            pl.when(jnp.logical_not(end))(
                lambda: send(ref, ref, os.at[u], z_fin.at[u], (out, me))
            )
            send(ref, ref, xs.at[u], xr.at[u], (other, me))

    length = bias.shape[1]
    scale = HD**-0.5
    band = 32
    column = lambda at, size: pl.ds(pl.multiple_of(at, 128), size)

    def moments(x):
        centre_ = jnp.mean(x, axis=1, keepdims=True)
        offset = x - centre_
        rate = lax.rsqrt(jnp.mean(offset * offset, axis=1, keepdims=True) + EPS)
        return offset * rate, rate

    def clear():
        sums[...] = jnp.zeros_like(sums)
        grad_kv[...] = jnp.zeros_like(grad_kv)

    def tally(k, x):
        sums[k : k + 1, :] += jnp.sum(x, axis=0, keepdims=True)

    def second_norm(lo, hi):
        gain = gains[4:5, :]

        @pl.loop(lo, hi)
        def _(i):
            at = pl.ds(pl.multiple_of(i * band, band), band)
            grad = jnp.zeros((band, width), F32)
            for q in range(count):
                grad = grad + down_all[pl.ds(pl.multiple_of(q * rows + i * band, band), band), :].astype(F32)
            unit, rate = moments(middle[at, :])
            tally(0, grad * unit)
            tally(1, grad)
            e = grad * gain
            back = rate * (
                e - jnp.mean(e, axis=1, keepdims=True) - unit * jnp.mean(e * unit, axis=1, keepdims=True)
            )
            away_grad = grad_out[at, :].astype(F32)
            tally(7, away_grad)
            whole = back + away_grad
            grad_mid[at, :] = whole
            short = whole.astype(BF)
            branch[at, :] = short
            tally(2, short.astype(F32))

    def first_norm(lo, hi):
        gain = gains[0:1, :]

        @pl.loop(lo, hi)
        def _(i):
            at = pl.ds(pl.multiple_of(i * band, band), band)
            grad = middle[at, :]
            unit, rate = moments(tokens[at, :].astype(F32))
            tally(3, grad * unit)
            tally(4, grad)
            e = grad * gain
            back = rate * (
                e - jnp.mean(e, axis=1, keepdims=True) - unit * jnp.mean(e * unit, axis=1, keepdims=True)
            )
            input_grad[at, :] = (back + grad_mid[at, :]).astype(BF)
            tally(5, grad_q[at, :].astype(F32))

    part_cols = min(512, width)

    def outer_product(dst, left, start, size, right):
        lhs = left[:, start : start + size] if isinstance(start, int) else left[:, column(start, size)]

        @pl.loop(0, right.shape[1] // min(part_cols, right.shape[1]))
        def _(k):
            cols = column(k * min(part_cols, right.shape[1]), min(part_cols, right.shape[1]))
            dst[:, cols] = lax.dot_general(
                lhs, right[:, cols], (((0,), (0,)), ((), ())), preferred_element_type=F32
            ).astype(BF)

    staged = []

    def stage_slot(m, q, size):
        k = len(staged)
        if k >= 2:
            before = staged[k - 2]
            wait(stage.at[k % 2, pl.ds(0, sizes[before[0]][0] * subs[before[0]]), : sizes[before[0]][1]], ss.at[before[0], before[1]])
        staged.append((m, q))
        return stage.at[k % 2, pl.ds(0, size), : sizes[m][1]]

    def weight_terms(m, left, right, some):
        size = width // count // 2
        for q in some:
            slot = stage_slot(m, q, size)
            outer_product(slot, left, (away(q) * 2 + 1 - c) * size, size, right)
            send(slot, land[m].at[q], ss.at[m, q], sib.at[m, q], (other, me))
            outer_product(spot(m, q), left, (away(q) * 2 + c) * size, size, right)

    strip_jobs = []

    def strip(source, start, size):
        strip_jobs.append((source, start, size))

    def strip_copy(k):
        source, start, size = strip_jobs[k]
        return pltpu.make_async_copy(
            source.at[:, column(start, size)], strips.at[k % 2, :, pl.ds(0, size)], ts.at[k % 2]
        )

    def use_strip(k):
        strip_copy(k).wait()
        return strips.at[k % 2]

    def next_strip(k):
        if k < len(strip_jobs):
            strip_copy(k).start()

    down_size = hidden // count // 2
    up_size = width // count // 2
    tile = tiles.shape[1]
    for q in [0] + near:
        strip(act, away(q) * 2 * down_size, 2 * down_size)
    for f in range(hidden // tile):
        strip(slope, f * tile, tile)
    for q in [0] + near:
        strip(normed_two, (away(q) * 2 + 1 - c) * up_size, up_size)
        strip(normed_two, (away(q) * 2 + c) * up_size, up_size)

    def down_terms(i):
        q = ([0] + near)[i]
        if i == 0:
            whole_down.wait()
        left = use_strip(i)
        slot = stage_slot(0, q, down_size)
        for k in range(2):

            @pl.when(c == k)
            def _():
                outer_product(slot, left, (1 - k) * down_size, down_size, down_all)

        send(slot, land[0].at[q], ss.at[0, q], sib.at[0, q], (other, me))
        for k in range(2):

            @pl.when(c == k)
            def _():
                outer_product(spot(0, q), left, k * down_size, down_size, down_all)

        next_strip(i + 2)

    block = hidden // (groups)

    def hidden_tile(f):
        k = count + f
        gate = use_strip(k)
        if f + 1 < hidden // tile:
            weight_rows(wdn, f + 1, width).start()
        weight_rows(wdn, f, width).wait()
        up_sums[pl.ds(f * (tile // block), tile // block), :] = jnp.zeros((tile // block, block), F32)

        @pl.loop(0, everyone // rows)
        def _(i):
            at = pl.ds(pl.multiple_of(i * rows, rows), rows)
            got = lax.dot_general(
                down_all[at, :], tiles[f % 2], (((1,), (1,)), ((), ())), preferred_element_type=F32
            )
            low_grad = (got * gate[at, :tile].astype(F32)).astype(BF)
            grad_hidden[at, f * tile : (f + 1) * tile] = low_grad
            total = jnp.sum(low_grad.astype(F32), axis=0, keepdims=True)
            for b in range(tile // block):
                k_ = f * (tile // block) + b
                up_sums[k_ : k_ + 1, :] += total[:, b * block : (b + 1) * block]

        next_strip(k + 2)
        if f + 1 == hidden // tile:
            for q in near:
                pl.semaphore_signal(ready, inc=1, device_id=(g, away(q)), device_id_type=MESH)

    def up_terms(i):
        q = ([0] + near)[i]
        k = count + hidden // tile + 2 * i
        slot = stage_slot(1, q, up_size)
        outer_product(slot, use_strip(k), 0, up_size, grad_hidden)
        next_strip(k + 2)
        send(slot, land[1].at[q], ss.at[1, q], sib.at[1, q], (other, me))
        outer_product(spot(1, q), use_strip(k + 1), 0, up_size, grad_hidden)
        next_strip(k + 3)

    def weight_rows(source, i, size):
        return pltpu.make_async_copy(
            source.at[pl.ds(i * tile, tile)], tiles.at[i % 2, :, pl.ds(0, size)], ws.at[i % 2]
        )

    def slice_out(d):
        return pltpu.make_async_copy(
            slices_stage.at[d % 2], slices.at[:, pl.ds(d * tile, tile)], ps.at[d % 2]
        )

    def slice_tile(d):
        if d + 1 < width // tile:
            weight_rows(wup, d + 1, hidden).start()
        weight_rows(wup, d, hidden).wait()
        if d >= 2:
            slice_out(d - 2).wait()

        @pl.loop(0, everyone // rows)
        def _(i):
            at = pl.ds(pl.multiple_of(i * rows, rows), rows)
            slices_stage[d % 2, at, :] = lax.dot_general(
                grad_hidden[at, :], tiles[d % 2, :, :hidden], (((1,), (1,)), ((), ())),
                preferred_element_type=F32,
            ).astype(BF)

        slice_out(d).start()
        if d + 1 == width // tile:
            slice_out(d - 1).wait()
            slice_out(d).wait()

    tile_rows = tiles.shape[1]
    tile_count = width // tile_rows

    def weight_tile(source, i):
        at = pl.multiple_of(i * tile_rows, tile_rows)
        slot = lax.rem(i, 2)
        return pltpu.make_async_copy(source.at[pl.ds(at, tile_rows)], tiles.at[slot], ws.at[slot])

    def attention_tiles(lo, hi):
        @pl.loop(lo, hi)
        def _(i):
            pl.when(i + 1 < tile_count)(lambda: weight_tile(wo, i + 1).start())
            weight_tile(wo, i).wait()
            cols = column(i * tile_rows, tile_rows)
            grad_att = lax.dot_general(
                branch[...], tiles[lax.rem(i, 2)], (((1,), (1,)), ((), ())), preferred_element_type=F32
            ).astype(BF)
            query = queries[:, cols]
            heads = tile_rows // HD
            fold = lambda x: jnp.concatenate([x[:, h * HD : (h + 1) * HD] for h in range(heads)], axis=0)
            for m in range(rows // length):
                at = pl.ds(m * length, length)
                q = fold(query[m * length : (m + 1) * length])
                ga = fold(grad_att[m * length : (m + 1) * length])
                k, v = keyvals[at, :HD], keyvals[at, HD:]
                shut = jnp.concatenate([bias[at, :]] * heads, axis=0)
                s = lax.dot_general(q, k, (((1,), (1,)), ((), ())), preferred_element_type=F32) * scale + shut
                e = jnp.exp(s - jnp.max(s, axis=1, keepdims=True))
                probs = e / jnp.sum(e, axis=1, keepdims=True)
                gp = lax.dot_general(ga, v, (((1,), (1,)), ((), ())), preferred_element_type=F32)
                ds = (probs * (gp - jnp.sum(probs * gp, axis=1, keepdims=True))).astype(BF)
                dq = (jnp.dot(ds, k, preferred_element_type=F32) * scale).astype(BF)
                for h in range(heads):
                    grad_q[at, column(i * tile_rows + h * HD, HD)] = dq[h * length : (h + 1) * length]
                tn = (((0,), (0,)), ((), ()))
                dk = lax.dot_general(ds, q, tn, preferred_element_type=F32) * scale
                dv = lax.dot_general(probs.astype(BF), ga, tn, preferred_element_type=F32)
                grad_kv[at, :HD] += dk
                grad_kv[at, HD:] += dv

    def query_tiles(lo, hi):
        low_kv = grad_kv[...].astype(BF)

        @pl.loop(lo, hi)
        def _(i):
            pl.when(i + 1 < tile_count)(lambda: weight_tile(wq, i + 1).start())
            weight_tile(wq, i).wait()
            cols = column(i * tile_rows, tile_rows)
            nt = (((1,), (1,)), ((), ()))
            middle[:, cols] = lax.dot_general(
                grad_q[...], tiles[lax.rem(i, 2)], nt, preferred_element_type=F32
            ) + lax.dot_general(
                low_kv, wkv[pl.ds(pl.multiple_of(i * tile_rows, tile_rows), tile_rows)], nt,
                preferred_element_type=F32,
            )

    def keyval_terms():
        low_kv = grad_kv[...].astype(BF)
        size = width // count // 2
        last = n - 1
        line = jnp.sum(low_kv[:, HD:].astype(F32), axis=0, keepdims=True)
        for k in range(width // size):
            sums[6:7, k * size : k * size + HD] = line
        for q in near + [0]:
            for ref, which in ((stage_kv.at[q], 1 - c), (spot(last, q), c)):
                start = (away(q) * 2 + which) * size
                ref[pl.ds(0, size), :] = lax.dot_general(
                    normed[:, column(start, size)], low_kv, (((0,), (0,)), ((), ())),
                    preferred_element_type=F32,
                ).astype(BF)
                ref[pl.ds(size, 16), :] = jnp.zeros((16, 2 * HD), BF)
                ref[pl.ds(size, 16), :size] = sums[:, column(start, size)].astype(BF)
                mine = up_sums[pl.ds(away(q) * 2 + which, 1), :]
                mine = jnp.concatenate([mine] * (2 * HD // block), axis=1)
                flat_at = lax.broadcasted_iota(jnp.int32, (16, 2 * HD), 0) * (2 * HD)
                flat_at = flat_at + lax.broadcasted_iota(jnp.int32, (16, 2 * HD), 1)
                own_place = lax.div(flat_at, block) == me
                ref[pl.ds(size + 16, 16), :] = jnp.where(own_place, mine, 0.0).astype(BF)
            send(stage_kv.at[q], land[last].at[q], ss.at[last, q], sib.at[last, q], (other, me))

    def reuse(m):
        if share[m] != m:
            wait(part[m], sent.at[share[m]])

    bands = rows // band
    plan = {}

    def at_step(step, *work):
        plan.setdefault(step, []).extend(work)

    P_ = partial
    starts = [sum(len(t) for t in pair_tasks[:m]) for m in range(n)]
    pairs_ = lambda m, lo, hi: [P_(pair, starts[m] + k) for k in range(lo, min(hi, len(pair_tasks[m])))]
    def got_slices():
        clear()
        for copy in own_copies:
            copy.wait()
        for q in [0] + near:
            wait(arrived(q), gr.at[q])

    order = near + [0]
    quarter = lambda k: (k * bands // 4, (k + 1) * bands // 4)
    tile_of = lambda k: (k * tile_count // 8, (k + 1) * tile_count // 8)
    subs_0, subs_1 = subs[0], subs[1]

    def begin_all():
        next_strip(0)
        next_strip(1)
        down_terms(0)
        for work in pairs_(0, 0, subs_0):
            work()

    queue = []
    for i in range(1, count):
        queue += [(3.5, P_(down_terms, i))] + [(0.3, x) for x in pairs_(0, i * subs_0, (i + 1) * subs_0)]
    queue += [(0.0, lambda: weight_rows(wdn, 0, width).start())]
    queue += [(12.0 / (hidden // tile), P_(hidden_tile, f)) for f in range(hidden // tile)]
    queue += [(0.0, lambda: weight_rows(wup, 0, hidden).start())]
    queue += [(1.5, P_(slice_tile, d)) for d in range(width // tile)]
    queue += [(0.0, send_slices)]
    for i in range(count):
        queue += [(3.5, P_(up_terms, i))] + [(0.3, x) for x in pairs_(1, i * subs_1, (i + 1) * subs_1)]
    later = [(0.0, got_slices)]
    later += [(2.5, P_(second_norm, *quarter(k))) for k in range(4)]
    later += [(0.0, lambda: weight_tile(wo, 0).start()), (0.0, P_(reuse, 2))]
    later += [(16.0 / count, P_(weight_terms, 2, attended, branch, [q])) for q in order]
    pairs_2, pairs_3 = pairs_(2, 0, 99), pairs_(3, 0, 99)
    share_of = lambda work, k: [(0.4, x) for x in work[k * len(work) // 4 : (k + 1) * len(work) // 4]]
    for k in range(8):
        later += [(TILE_COST, P_(attention_tiles, *tile_of(k)))]
        later += share_of(pairs_2, k) if k < 4 else []
    later += [(0.0, lambda: weight_tile(wq, 0).start()), (0.0, P_(reuse, 3))]
    later += [(16.0 / count, P_(weight_terms, 3, normed, grad_q, [q])) for q in order]
    for k in range(8):
        later += [(0.8, P_(query_tiles, *tile_of(k)))]
        later += share_of(pairs_3, k) if k < 4 else []
    later += [(2.5, P_(first_norm, *quarter(k))) for k in range(4)]
    later += [(4.0, keyval_terms)]
    later += [(1.0, work) for work in pairs_(4, 0, 99)]
    step, spent = 0, 0.0
    for some, start in ((queue, 0), (later, NORM_STEP)):
        if start > step:
            step, spent = start, 0.0
        for cost, work in some:
            if spent + cost > BUDGET and spent:
                spent, step = 0.0, step + 1
            spent += cost
            at_step(step, work)
    needs = {}
    for m, per_unit in ((0, 1), (1, 1), (2, count), (3, count), (4, count)):
        base_unit = [u for u in range(len(units)) if units[u][0] == m][0]
        for k, work in enumerate(pair_tasks[m]):
            needs.setdefault(base_unit + k // per_unit, []).append((m, k))
    begin_all()
    cursor = [0]
    steps = max(len(units) + LAG_OUT, max(plan) + 1)
    for step in range(steps):
        if step < len(units):
            while any(starts[m] + k not in paired_set for m, k in needs[step]):
                while not plan.get(cursor[0]):
                    cursor[0] += 1
                plan[cursor[0]].pop(0)()
            inward(step)
        if 0 <= step - LAG_MID < len(units):
            centre(step - LAG_MID)
        if 0 <= step - LAG_OUT < len(units):
            outward(step - LAG_OUT)
        for at in range(cursor[0], step + 1):
            for work in plan.pop(at, ()):
                work()
        cursor[0] = max(cursor[0], step + 1)

    for m in range(n):
        if m not in share[m + 1 :]:
            wait(part[m], sent.at[m])
        for q in near + [0]:
            if m == n - 1 or (m, q) in staged[-2:]:
                wait(land[m].at[q], ss.at[m, q])
    for q in near:
        wait(arrived(q), gs.at[q])
    for u in range(len(units)):
        wait(result(u, 1 - c), xr.at[u])
        wait(result(u, c), xs.at[u])
        pl.when(jnp.logical_not(end))(partial(wait, result(u, c), os.at[u]))
        pl.when(middle_chip)(partial(wait, result(u, c), loc.at[u]))
        pl.when(jnp.logical_not(middle_chip))(partial(wait, value(u), zs.at[u]))


def back_all(groups, count, far, own, near_by):
    rows, width = own[0].shape
    everyone, hidden = far[0].shape
    size = width // count // 2
    tile = 2 * HD
    low = (size + 32, 2 * HD)
    shapes = [(hidden // count // 2, width), (size, hidden), (size, width), (size, width), low]
    plain, subs = (True, True, False, False, False), (4, 4, 4, 4, 1)
    n = len(shapes)
    sizes = [(s[0] // k, s[1]) for s, k in zip(shapes, subs)]
    share = list(range(n))
    for m in (2, 3):
        share[m] = m - 2 if shapes[m] == shapes[m - 2] else 2
    rings = sorted(set(sizes))
    units = sum(s * (count if f else 1) for s, f in zip(subs, plain))
    slots = [min(RING, sum(s * (count if f else 1) for s, f, z in zip(subs, plain, sizes) if z == r)) for r in rings]
    any_, vmem = pl.BlockSpec(memory_space=pl.ANY), pl.BlockSpec(memory_space=pltpu.VMEM)
    dma, regular = pltpu.SemaphoreType.DMA, pltpu.SemaphoreType.REGULAR
    out = [jax.ShapeDtypeStruct((2, count if f else 1) + s, BF) for s, f in zip(shapes, plain)]
    out += [jax.ShapeDtypeStruct((count,) + s, BF) for s in shapes]
    scratch = [pltpu.VMEM((count - 1,) + shapes[m], BF) for m in range(n) if share[m] == m]
    scratch += [pltpu.VMEM((count,) + s, BF) for s in shapes]
    scratch += [pltpu.VMEM((2,) + r, BF) for r in rings]
    scratch += [pltpu.VMEM((k,) + r, BF) for k, r in zip(slots, rings)] * 2
    scratch += [
        pltpu.VMEM((everyone, width), BF), pltpu.VMEM((everyone, hidden), BF),
        pltpu.VMEM((2, everyone, max(2 * hidden // count // 2, tile)), BF), pltpu.VMEM((2, everyone, tile), BF),
        pltpu.VMEM((rows, width), F32), pltpu.VMEM((rows, width), BF), pltpu.VMEM((rows, width), F32),
        pltpu.VMEM((rows, width), BF), pltpu.VMEM((rows, width), BF), pltpu.VMEM((2, tile, width), BF),
        pltpu.VMEM((2, max(s[0] for s in shapes[:4]), width), BF), pltpu.VMEM((count,) + low, BF),
        pltpu.VMEM((rows, 2 * HD), F32),
        pltpu.VMEM((16, width), F32), pltpu.VMEM((max(16, groups), hidden // groups), F32),
        pltpu.VMEM((rows, width), BF), pltpu.VMEM((rows, width), BF), pltpu.VMEM((rows, width), BF),
        pltpu.VMEM((rows, width), BF),
        dma((n, count)), dma((2,)), dma((n,)), dma((n, max(subs), count)), dma((units,)), dma((units,)),
        dma((units,)), dma((units,)), dma((units,)), dma((units,)), dma((units,)), dma((units,)),
        dma((n, count)), dma((count,)), dma((count,)), dma((2,)), dma((7,)), dma((2,)), dma((2,)),
        regular((len(rings), max(slots))), regular((len(rings), max(slots))), regular,
    ]
    got = pl.pallas_call(
        partial(back_kernel, groups, count, subs, plain, sizes, share),
        out_shape=tuple(out) + (jax.ShapeDtypeStruct((everyone, width), BF), jax.ShapeDtypeStruct((rows, width), BF)),
        in_specs=[any_] * 13 + [vmem] * 4,
        out_specs=(any_,) * (2 * n + 1) + (vmem,),
        scratch_shapes=scratch,
        compiler_params=pltpu.CompilerParams(
            collective_id=2, has_side_effects=True, vmem_limit_bytes=60 * 1024 * 1024
        ),
        cost_estimate=pl.CostEstimate(flops=0, bytes_accessed=200_000_000, transcendentals=0),
        name="back_all",
    )(*far, *own, *near_by)
    return got[:n], got[-1]


def lift_kernel(rows, weight, bias, act, slope):
    u = jnp.dot(rows[...], weight[...], preferred_element_type=F32) + bias[...]
    root = 0.7978845608028654
    t = jnp.tanh(root * (u + 0.044715 * (u * u * u)))
    half = 0.5 * (1.0 + t)
    act[...] = (u * half).astype(BF)
    slope[...] = (half + 0.5 * u * (1.0 - t * t) * (root * (1.0 + 3 * 0.044715 * (u * u)))).astype(BF)


def lift(rows, weight, bias):
    n, hidden = rows.shape[0], weight.shape[1]
    tile = 2 * HD
    out = jax.ShapeDtypeStruct((n, hidden), BF)
    column = lambda k: pl.BlockSpec((k, tile), lambda i: (0, i))
    return pl.pallas_call(
        lift_kernel,
        out_shape=(out, out),
        grid=(hidden // tile,),
        in_specs=[pl.BlockSpec(rows.shape, lambda i: (0, 0)), column(weight.shape[0]), column(1)],
        out_specs=(column(n), column(n)),
        compiler_params=pltpu.CompilerParams(vmem_limit_bytes=48 * 1024 * 1024),
        name="lift",
    )(rows, weight, bias)


def widen_kernel(block, size, down, up, out, query, low, o_down, o_up, o_out, o_query, o_low, *lines):
    o_down[...] = down[...].astype(F32)
    o_out[...] = out[...].astype(F32)
    o_query[...] = query[...].astype(F32)
    _, count, rows, hidden = up.shape
    for source in range(count):
        for k in range(hidden // block):
            o_up[:, pl.ds((k * count + source) * block, block)] = up[0, source, :, pl.ds(k * block, block)].astype(F32)

    @pl.when(pl.program_id(0) == 0)
    def _():
        for half in range(2):
            o_low[half * size : (half + 1) * size, :] = low[half, :size, :].astype(F32)
            sums = low[half, size : size + 16, :size].astype(F32)
            for v in range(8):
                lines[v][:, half * size : (half + 1) * size] = sums[v : v + 1, :]
            tail = low[half, size + 16 :, :].astype(F32)
            wide = tail.shape[1]
            for r in range(hidden // 2 // wide):
                start = half * hidden // 2 + r * wide
                lines[8][:, start : start + wide] = tail[r : r + 1, :]


def widen(full, block):
    down, up, out, query, low = full
    flat = lambda x: x.reshape(-1, x.shape[-1])
    down, out, query, low = flat(down), flat(out), flat(query), low[:, 0]
    _, count, rows, hidden = up.shape
    steps = 16
    step = 2 * rows // steps
    size = out.shape[0] // 2
    row = lambda x: pl.BlockSpec((x.shape[0] // steps, x.shape[1]), lambda i: (i, 0))
    still = lambda *shape: pl.BlockSpec(shape, lambda i: (0,) * len(shape))
    shape = lambda *dims: jax.ShapeDtypeStruct(dims, F32)
    vectors = [(1, 2 * size)] * 8 + [(1, hidden)]
    return pl.pallas_call(
        partial(widen_kernel, block, size),
        out_shape=(
            shape(*down.shape), shape(2 * rows, count * hidden), shape(*out.shape), shape(*query.shape),
            shape(2 * size, low.shape[2]),
        ) + tuple(shape(*v) for v in vectors),
        grid=(steps,),
        in_specs=[
            row(down), pl.BlockSpec((1, count, step, hidden), lambda i: (i // (steps // 2), 0, i % (steps // 2), 0)),
            row(out), row(query), still(*low.shape),
        ],
        out_specs=(
            row(down), pl.BlockSpec((step, count * hidden), lambda i: (i, 0)), row(out), row(query),
            still(2 * size, low.shape[2]),
        ) + tuple(still(*v) for v in vectors),
        name="widen",
    )(down, up, out, query, low)


def used(lengths, row):
    total = lengths[row, 0]
    for k in range(1, lengths.shape[1]):
        total = total + lengths[row, k]
    return total


def masked(x, lengths, row):
    places = lax.broadcasted_iota(jnp.int32, x.shape, 0)
    return jnp.where(places < used(lengths, row), x, 0.0)


def take_kernel(order, lengths, values, out, held, got, put):
    count = held.shape[0]
    takes = [pltpu.make_async_copy(values.at[order[r]], held.at[r], got.at[r]) for r in range(count)]
    puts = [pltpu.make_async_copy(held.at[r], out.at[r], put.at[r]) for r in range(count)]
    for take in takes:
        take.start()
    for r in range(count):
        takes[r].wait()
        held[r] = masked(held[r].astype(F32), lengths, r).astype(BF)
        puts[r].start()
    for copy in puts:
        copy.wait()


def take_rows(values, order, lengths):
    count = values.shape[0]
    smem, any_ = pl.BlockSpec(memory_space=pltpu.SMEM), pl.BlockSpec(memory_space=pl.ANY)
    return pl.pallas_call(
        take_kernel,
        out_shape=jax.ShapeDtypeStruct(values.shape, BF),
        in_specs=[smem, smem, any_],
        out_specs=any_,
        scratch_shapes=[
            pltpu.VMEM(values.shape, BF), pltpu.SemaphoreType.DMA((count,)), pltpu.SemaphoreType.DMA((count,)),
        ],
        compiler_params=pltpu.CompilerParams(vmem_limit_bytes=32 * 1024 * 1024),
        name="take_rows",
    )(order, lengths, values)


def finish_kernel(deal, lengths, place, first, second, weight, middle, table, out):
    step = pl.program_id(0)
    micro, length, width = middle.shape
    wide = min(512, width)
    left = jnp.concatenate([first[0], second[0]], axis=0)
    for k in range(width // wide):
        cols = pl.ds(k * wide, wide)
        got = jnp.dot(left, weight[:, cols], preferred_element_type=F32)
        for i in range(2):
            row = deal[2 * step + i]
            term = got[i * length : (i + 1) * length]
            own = lax.div(row, micro) == place[0]
            extra = middle[lax.rem(row, micro), :, cols] + table[6:7, cols]
            out[i, :, cols] = masked(term + jnp.where(own, extra, 0.0), lengths, row).astype(BF)


def finish_rows(values, weight, deal, lengths, me, middle, table):
    count, length, depth = values.shape
    width = weight.shape[1]
    row = lambda i: pl.BlockSpec((1, length, depth), lambda j, deal, lengths, me: (deal[2 * j + i], 0, 0))
    still = lambda x: pl.BlockSpec(x.shape, lambda j, deal, lengths, me: (0,) * x.ndim)
    return pl.pallas_call(
        finish_kernel,
        out_shape=jax.ShapeDtypeStruct((count, length, width), BF),
        grid_spec=pltpu.PrefetchScalarGridSpec(
            num_scalar_prefetch=3,
            grid=(count // 2,),
            in_specs=[row(0), row(1), still(weight), still(middle), still(table)],
            out_specs=pl.BlockSpec((2, length, width), lambda j, deal, lengths, me: (j, 0, 0)),
        ),
        compiler_params=pltpu.CompilerParams(vmem_limit_bytes=48 * 1024 * 1024),
        name="finish_rows",
    )(deal, lengths, me.reshape(1), values, values, weight, middle, table)


def cut_kernel(groups, count, block, x, out):
    for to in range(count):
        for k in range(groups):
            out[to, :, k * block : (k + 1) * block] = x[:, (k * count + to) * block : (k * count + to + 1) * block]


def shards(
    groups,
    count,
    tokens,
    cotangent,
    lengths,
    dealing,
    first_gain,
    first_shift,
    query_weight,
    query_bias,
    keyval_weight,
    value_bias,
    out_weight,
    out_bias,
    second_gain,
    second_shift,
    up_weight,
    up_bias,
    down_weight,
    down_bias,
):
    both = ("grp", "shard")
    micro, length, width = tokens.shape
    group_rows = dealing.shape[0]
    group = lax.axis_index("grp")
    me = lax.axis_index("shard")
    half = micro // 2
    block = down_weight.shape[0]
    hidden = block * groups
    rows = micro * length

    deal = dealing - group * group_rows
    steps = jnp.arange(group_rows, dtype=jnp.int32)
    inverse = jnp.sum(jnp.where(deal[:, None] == steps[None, :], steps[:, None], 0), axis=0)

    line = lambda x: jnp.pad(x, (0, 128 - x.shape[0]))
    piece = first_gain.shape[0]
    device = group * count + me
    value_line = lax.dynamic_update_slice(
        jnp.zeros((128,), BF), value_bias, (device * value_bias.shape[0],)
    )
    small = [first_gain, first_shift, query_bias, out_bias, second_gain, second_shift, down_bias]
    small = [line(x) for x in small] + [value_line]
    small += [line(up_bias[k * piece : (k + 1) * piece]) for k in range(block // piece)]
    small = jnp.stack(small + [jnp.zeros((128,), BF)] * (16 - len(small)))
    up_rows = up_weight.shape[0]
    up_cut = pl.pallas_call(
        partial(cut_kernel, groups, count, block),
        out_shape=jax.ShapeDtypeStruct((count, up_rows, hidden), BF),
        name="cut",
    )(up_weight)
    weight_query, weight_out, weight_keyval, small_all, weight_up = gather_all(
        groups, count, query_weight, out_weight, keyval_weight, small, up_cut
    )
    weight_query, weight_out, weight_up, down_weight = lax.optimization_barrier(
        (weight_query, weight_out, weight_up, down_weight)
    )
    weight_down = lax.all_gather(down_weight, "grp", axis=0, tiled=True)

    flat_tokens = tokens.reshape(rows, width)
    (
        normed_two, cot_rows, normed_one, queries, keyvals, attended, middle, table, up_part, bias,
    ) = attend(
        groups, count, flat_tokens, small_all, lengths, cotangent.reshape(rows, width),
        weight_query, weight_out, weight_keyval, hidden, length,
    )
    grad_down = take_rows(cot_rows.reshape(group_rows, length, width), inverse, lengths)
    grad_down = grad_down.reshape(group_rows * length, width)

    activated, slope = lift(normed_two, weight_up, up_part)
    result = finish_rows(
        activated.reshape(group_rows, length, hidden), weight_down, deal, lengths, me,
        middle.reshape(micro, length, width), table,
    )
    block_output = lax.psum_scatter(
        result.reshape(group_rows * length, width), "shard", scatter_dimension=0, tiled=True
    ).reshape(micro, length, width)

    full, input_grad = back_all(
        groups, count,
        (activated, slope, grad_down, weight_down, normed_two, weight_up, weight_query, weight_out, middle),
        (attended, queries, normed_one, flat_tokens), (keyvals, bias, table, weight_keyval),
    )
    input_grad = input_grad.reshape(micro, length, width)

    down_full, up_full, out_full, query_full, keyval_full, *lines = widen(full, block)
    lines = [line.reshape(-1) for line in lines]
    gain_two_grad, shift_two_grad, out_bias_grad, gain_one_grad, shift_one_grad, query_bias_grad = lines[:6]
    short = value_bias.shape[0] * groups
    value_bias_grad = lax.dynamic_slice(lines[6], (me * short,), (short,))
    down_bias_grad, up_bias_grad = lines[7:]

    return (
        block_output, input_grad, gain_one_grad, shift_one_grad, query_full, query_bias_grad, keyval_full,
        value_bias_grad, out_full, out_bias_grad, gain_two_grad, shift_two_grad, up_full, up_bias_grad,
        down_full, down_bias_grad,
    )


def solution(mesh):
    rows = P(("grp", "shard"), None, None)
    flat = P(("grp", "shard"))
    tall = P(("grp", "shard"), None)
    vector, matrix = P("shard"), P("shard", None)
    return jax.shard_map(
        partial(shards, mesh.shape["grp"], mesh.shape["shard"]),
        mesh=mesh,
        in_specs=(
            rows, rows, P("grp", None), P("grp"), flat, flat, tall, flat, tall, flat,
            tall, flat, flat, flat, tall, flat, tall, flat,
        ),
        out_specs=(
            rows, rows, vector, vector, matrix, vector, matrix, vector,
            matrix, vector, vector, vector, matrix, vector, matrix, vector,
        ),
        check_vma=False,
    )
```

```python
from functools import partial

import jax
import jax.numpy as jnp
from jax import lax
from jax.experimental import pallas as pl
from jax.experimental.pallas import tpu as pltpu
from jax.sharding import PartitionSpec as P

HEADS = 16
HD = 128
EPS = 1e-05
NEGATIVE = -1e30
BF = jnp.bfloat16
F32 = jnp.float32
MESH = pl.DeviceIdType.MESH
LAG_MID = 1
LAG_OUT = 6
BUDGET = 8.0
TILE_COST = 4.0
NORM_STEP = 15
RING = 6


def cube_tree(count, parity, q):
    order = list(range(count.bit_length() - 1))
    if parity:
        order = order[::-1]
    at = max([i for i, d in enumerate(order) if q >> d & 1], default=-1)
    return [1 << d for d in order[at + 1 :]]


def near_first(count):
    return sorted(range(1, count), key=lambda q: (bin(q).count("1"), q))


def gather_kernel(
    groups, count, wq, wo, wkv, small, upc, q_all, o_all, kv_all, small_all, up_all,
    zs, zr, ps, pr, bs, br, us, ur, loc,
):
    chips = groups // 2
    g, me = lax.axis_index("grp"), lax.axis_index("shard")
    p, c = lax.div(g, 2), lax.rem(g, 2)

    barrier = pltpu.get_barrier_semaphore()

    def greet(target):
        pl.semaphore_signal(barrier, inc=1, device_id=target, device_id_type=MESH)

    greet((g + 1 - 2 * c, me))
    for q in range(1, count):
        greet((g, lax.bitwise_xor(me, q)))

    @pl.when(p < chips - 1)
    def _():
        greet((g + 2, me))

    @pl.when(p > 0)
    def _():
        greet((g - 2, me))

    ends = (p == 0).astype(jnp.int32) + (p == chips - 1).astype(jnp.int32)
    pl.semaphore_wait(barrier, count + 2 - ends)

    def send(src, dst, send_sem, recv_sem, target):
        pltpu.make_async_remote_copy(
            src_ref=src, dst_ref=dst, send_sem=send_sem, recv_sem=recv_sem,
            device_id=target, device_id_type=MESH,
        ).start()

    def wait(ref, sem):
        pltpu.make_async_copy(ref, ref, sem).wait()

    own = (wq, wo, wkv, small)
    whole = (q_all, o_all, kv_all, small_all)
    parity = (0, 1, 0, 1)
    size = [x.shape[0] for x in own]
    full = len(own)
    cuts = (full, full + 1)
    up_size = upc.shape[1]
    up_half = up_size * count // 2

    def spot(a, z, col):
        if a < full:
            at = ((z * 2 + c) * count + col) * size[a]
            return whole[a].at[pl.ds(pl.multiple_of(at, 16), size[a])]
        at = (z * 2 + c) * up_half * 2 + (a - full) * up_half
        return up_all.at[pl.ds(pl.multiple_of(at, 16), up_half)]

    def along(a, way, hop, src, z):
        step = 1 - 2 * way
        send(src, spot(a, z, me), zs.at[a, way, hop], zr.at[a, way, hop], (g + 2 * step, me))

    def across(a, src, z, q):
        for m in cube_tree(count, parity[a], q):
            send(
                src, spot(a, z, lax.bitwise_xor(me, q)), ps.at[a], pr.at[a, z, q ^ m],
                (g, lax.bitwise_xor(me, m)),
            )

    def aside(a, src, z, q):
        send(src, spot(a, z, lax.bitwise_xor(me, q)), bs.at[a], br.at[a], (g + 1 - 2 * c, me))

    def may_send(way, hop):
        if way == 0:
            return (p >= hop - 1) & (p < chips - 1)
        return (p + hop - 1 <= chips - 1) & (p > 0)

    def may_take(way, hop):
        return p >= hop if way == 0 else p + hop <= chips - 1

    up_rows = lambda col: up_all.at[pl.ds(pl.multiple_of((g * count + col) * up_size, 16), up_size)]
    for q in near_first(count):
        to = lax.bitwise_xor(me, q)
        send(upc.at[to], up_rows(me), us, ur.at[q], (g, to))
    mine = [pltpu.make_async_copy(upc.at[me], up_rows(me), loc.at[full])]
    for a in range(full):
        mine.append(pltpu.make_async_copy(own[a], spot(a, p, me), loc.at[a]))
    for copy in mine:
        copy.start()

    def first(a, src):
        for way in range(2):
            pl.when(may_send(way, 1))(partial(along, a, way, 1, src, p))
        aside(a, src, p, 0)

    for a in range(full):
        first(a, own[a])
        across(a, own[a], p, 0)
    mine[0].wait()
    for q in near_first(count):
        wait(up_rows(me), ur.at[q])
    for a in cuts:
        first(a, spot(a, p, me))

    def plane(z, far):
        for q in near_first(count):
            if far != (q & (q - 1) != 0):
                continue
            for a in range(full):
                ref = spot(a, z, lax.bitwise_xor(me, q))
                wait(ref, pr.at[a, z, q])
                across(a, ref, z, q)
                aside(a, ref, z, q)

    def planes(hop, far):
        if hop == 0:
            plane(p, far)
            return
        for way in range(2):
            z = p - hop if way == 0 else p + hop
            pl.when(may_take(way, hop))(partial(plane, z, far))

    def arrive(a, hop):
        for way in range(2):

            @pl.when(may_take(way, hop))
            def _():
                z = p - hop if way == 0 else p + hop
                ref = spot(a, z, me)
                wait(ref, zr.at[a, way, hop])
                if hop + 1 < chips:
                    pl.when(may_send(way, hop + 1))(
                        partial(along, a, way, hop + 1, ref, z)
                    )
                if a < full:
                    across(a, ref, z, 0)
                aside(a, ref, z, 0)

    for hop in range(1, chips):
        for a in range(full):
            arrive(a, hop)
        planes(hop - 1, False)
        if hop > 1:
            planes(hop - 2, True)
        for a in cuts:
            arrive(a, hop)
    planes(chips - 1, False)
    for hop in (chips - 2, chips - 1):
        planes(hop, True)

    for copy in mine[1:]:
        copy.wait()
    for a in range(full + 2):
        for way in range(2):
            for hop in range(1, chips):
                pl.when(may_send(way, hop))(
                    partial(wait, spot(a, p, me), zs.at[a, way, hop])
                )
    for a in range(full):
        wait(whole[a].at[pl.ds(0, chips * (count - 1) * size[a])], ps.at[a])
        wait(whole[a].at[pl.ds(0, chips * count * size[a])], bs.at[a])
        wait(whole[a].at[pl.ds(0, chips * count * size[a])], br.at[a])
    for a in cuts:
        wait(up_all.at[pl.ds(0, chips * up_half)], bs.at[a])
        wait(up_all.at[pl.ds(0, chips * up_half)], br.at[a])
    wait(up_all.at[pl.ds(0, (count - 1) * up_size)], us)


def gather_all(groups, count, wq, wo, wkv, small, upc):
    chips = groups // 2
    n = groups * count
    any_ = pl.BlockSpec(memory_space=pl.ANY)
    dma = pltpu.SemaphoreType.DMA
    tall = lambda x: jax.ShapeDtypeStruct((n * x.shape[0], x.shape[1]), x.dtype)
    return pl.pallas_call(
        partial(gather_kernel, groups, count),
        out_shape=(
            tall(wq), tall(wo), tall(wkv), tall(small),
            jax.ShapeDtypeStruct((n * upc.shape[1], upc.shape[2]), upc.dtype),
        ),
        in_specs=[any_] * 5,
        out_specs=(any_,) * 5,
        scratch_shapes=[
            dma((6, 2, chips)), dma((6, 2, chips)), dma((4,)), dma((4, chips, count)),
            dma((6,)), dma((6,)), dma, dma((count,)), dma((5,)),
        ],
        compiler_params=pltpu.CompilerParams(collective_id=1, has_side_effects=True),
        cost_estimate=pl.CostEstimate(flops=0, bytes_accessed=100_000_000, transcendentals=0),
        name="gather_all",
    )(wq, wo, wkv, small, upc)


def attend_kernel(
    groups, count, tokens, small_all, lengths, cot, wq, wo, wkv,
    near_all, cot_all, normed, queries, keyvals, attended, middle, vectors, up_part, bias,
    wq_v, wo_v, wkv_v, second, ws, ns, nr, cs, cr, loc,
):
    g, me = lax.axis_index("grp"), lax.axis_index("shard")
    barrier = pltpu.get_barrier_semaphore()
    nearest = [1 << d for d in range(count.bit_length() - 1)]
    for m in nearest:
        pl.semaphore_signal(
            barrier, inc=1, device_id=(g, lax.bitwise_xor(me, m)), device_id_type=MESH
        )
    pl.semaphore_wait(barrier, len(nearest))

    loads = [
        pltpu.make_async_copy(a, b, ws.at[i])
        for i, (a, b) in enumerate(((wkv, wkv_v), (wq, wq_v), (wo, wo_v)))
    ]
    for load in loads:
        load.start()

    rows, width = tokens.shape
    length = bias.shape[1]
    half = rows // 2
    near = near_first(count)
    place = lambda ref, k, col: ref.at[pl.ds(pl.multiple_of(col * rows + k * half, 16), half)]

    def send(src, dst, send_sem, recv_sem, m):
        pltpu.make_async_remote_copy(
            src_ref=src, dst_ref=dst, send_sem=send_sem, recv_sem=recv_sem,
            device_id=(g, lax.bitwise_xor(me, m)), device_id_type=MESH,
        ).start()

    def wait(ref, sem):
        pltpu.make_async_copy(ref, ref, sem).wait()

    def pass_on(ref, src, k, q, sends, gets):
        for m in cube_tree(count, k, q):
            send(src, place(ref, k, lax.bitwise_xor(me, q)), sends.at[k], gets.at[k, q ^ m], m)

    def take(ref, sends, gets, far):
        for q in near:
            if far != (q & (q - 1) != 0):
                continue
            for k in range(2):
                got = place(ref, k, lax.bitwise_xor(me, q))
                wait(got, gets.at[k, q])
                pass_on(ref, got, k, q, sends, gets)

    for k in range(2):
        pass_on(cot_all, cot.at[pl.ds(k * half, half)], k, 0, cs, cr)
    own_cot = pltpu.make_async_copy(cot, cot_all.at[pl.ds(pl.multiple_of(me * rows, 16), rows)], loc.at[0])
    own_cot.start()

    lot = small_all.shape[0] // (groups * count)
    piece = width // (groups * count)
    join = 128 // piece
    for k in range(width // 128):
        parts = [
            small_all[(k * join + i) * lot : (k * join + i) * lot + 16, :piece].astype(F32) for i in range(join)
        ]
        vectors[:, k * 128 : (k + 1) * 128] = jnp.concatenate(parts, axis=1)
    total = small_all[0:16, :].astype(F32)
    for d in range(1, groups * count):
        total = total + small_all[d * lot : d * lot + 16, :].astype(F32)
    vectors[7:8, :128] = total[7:8, :]
    pieces = []
    for k in range(groups):
        at = pl.multiple_of((k * count + me) * lot, 16)
        mine = small_all[pl.ds(at, 16), :].astype(F32)
        pieces += [mine[8 + r : 9 + r, :piece] for r in range(up_part.shape[1] // groups // piece)]
    for k in range(up_part.shape[1] // 128):
        up_part[:, k * 128 : (k + 1) * 128] = jnp.concatenate(pieces[k * join : (k + 1) * join], axis=1)

    band = 32
    spots = [lax.broadcasted_iota(jnp.int32, (length, length), d) for d in range(2)]
    for m in range(rows // length):
        segments = [jnp.zeros((length, length), jnp.int32)] * 2
        stop = 0
        for k in range(lengths.shape[1]):
            stop = stop + lengths[me * (rows // length) + m, k]
            segments = [a + (spot >= stop).astype(jnp.int32) for a, spot in zip(segments, spots)]
        allowed = (segments[0] == segments[1]) & (spots[1] <= spots[0])
        bias[m * length : (m + 1) * length, :] = jnp.where(allowed, 0.0, NEGATIVE)

    def norm(x, gain, shift):
        offset = x - jnp.mean(x, axis=1, keepdims=True)
        rate = lax.rsqrt(jnp.mean(offset * offset, axis=1, keepdims=True) + EPS)
        return (offset * rate * gain + shift).astype(BF)

    @pl.loop(0, rows // band)
    def _(i):
        at = pl.ds(pl.multiple_of(i * band, band), band)
        normed[at, :] = norm(tokens[at, :].astype(F32), vectors[0:1, :], vectors[1:2, :])

    loads[0].wait()
    kv = jnp.dot(normed[...], wkv_v[...], preferred_element_type=F32)
    keyvals[:, :HD] = kv[:, :HD].astype(BF)
    keyvals[:, HD:] = (kv[:, HD:] + vectors[7:8, :HD]).astype(BF)
    loads[1].wait()
    tile = 2 * HD
    scale = HD**-0.5
    fold = lambda x: jnp.concatenate([x[:, h * HD : (h + 1) * HD] for h in range(tile // HD)], axis=0)

    @pl.loop(0, width // tile)
    def _(i):
        cols = pl.ds(pl.multiple_of(i * tile, tile), tile)
        query = jnp.dot(normed[...], wq_v[:, cols], preferred_element_type=F32)
        query = (query + vectors[2:3, cols]).astype(BF)
        queries[:, cols] = query
        for m in range(rows // length):
            at = pl.ds(m * length, length)
            q = fold(query[m * length : (m + 1) * length])
            k, v = keyvals[at, :HD], keyvals[at, HD:]
            shut = jnp.concatenate([bias[at, :]] * (tile // HD), axis=0)
            s = lax.dot_general(q, k, (((1,), (1,)), ((), ())), preferred_element_type=F32) * scale + shut
            e = jnp.exp(s - jnp.max(s, axis=1, keepdims=True))
            probs = (e / jnp.sum(e, axis=1, keepdims=True)).astype(BF)
            got = jnp.dot(probs, v, preferred_element_type=F32).astype(BF)
            for h in range(tile // HD):
                attended[at, pl.ds(pl.multiple_of(i * tile + h * HD, HD), HD)] = got[
                    h * length : (h + 1) * length
                ]

    take(cot_all, cs, cr, False)
    loads[2].wait()
    wide = min(512, width)

    @pl.loop(0, width // wide)
    def _(i):
        cols = pl.ds(pl.multiple_of(i * wide, wide), wide)
        branch = jnp.dot(attended[...], wo_v[:, cols], preferred_element_type=F32)
        middle[:, cols] = tokens[:, cols].astype(F32) + branch + vectors[3:4, cols]

    for k in range(2):

        @pl.loop(k * half // band, (k + 1) * half // band)
        def _(i):
            at = pl.ds(pl.multiple_of(i * band, band), band)
            second[at, :] = norm(middle[at, :], vectors[4:5, :], vectors[5:6, :])

        pass_on(near_all, second.at[pl.ds(k * half, half)], k, 0, ns, nr)
    own = pltpu.make_async_copy(second, near_all.at[pl.ds(pl.multiple_of(me * rows, 16), rows)], loc.at[1])
    own.start()
    take(cot_all, cs, cr, True)
    take(near_all, ns, nr, False)
    take(near_all, ns, nr, True)
    own_cot.wait()
    own.wait()
    for k in range(2):
        wait(cot_all.at[pl.ds(0, (count - 1) * half)], cs.at[k])
        wait(near_all.at[pl.ds(0, (count - 1) * half)], ns.at[k])


def attend(groups, count, tokens, small_all, lengths, cot, wq, wo, wkv, hidden, length):
    rows, width = tokens.shape
    any_, vmem = pl.BlockSpec(memory_space=pl.ANY), pl.BlockSpec(memory_space=pltpu.VMEM)
    dma = pltpu.SemaphoreType.DMA
    shape = jax.ShapeDtypeStruct
    return pl.pallas_call(
        partial(attend_kernel, groups, count),
        out_shape=(
            shape((count * rows, width), BF), shape((count * rows, width), BF), shape((rows, width), BF),
            shape((rows, width), BF), shape((rows, 2 * HD), BF), shape((rows, width), BF),
            shape((rows, width), F32), shape((16, width), F32), shape((1, hidden), F32),
            shape((rows, length), F32),
        ),
        in_specs=[vmem, vmem, pl.BlockSpec(memory_space=pltpu.SMEM), any_, any_, any_, any_],
        out_specs=(any_, any_) + (vmem,) * 8,
        scratch_shapes=[
            pltpu.VMEM(wq.shape, BF), pltpu.VMEM(wo.shape, BF), pltpu.VMEM(wkv.shape, BF),
            pltpu.VMEM((rows, width), BF), dma((3,)), dma((2,)), dma((2, count)), dma((2,)),
            dma((2, count)), dma((2,)),
        ],
        compiler_params=pltpu.CompilerParams(
            collective_id=3, has_side_effects=True, vmem_limit_bytes=48 * 1024 * 1024
        ),
        cost_estimate=pl.CostEstimate(flops=5_000_000_000, bytes_accessed=100_000_000, transcendentals=0),
        name="attend",
    )(tokens, small_all, lengths, cot, wq, wo, wkv)


def back_kernel(groups, count, subs, plain, sizes, share, *refs):
    n = len(subs)
    take = iter(refs)
    many = lambda k: [next(take) for _ in range(k)]
    act, slope, down_rows, wdn, normed_two, wup, wq, wo, middle_far = many(9)
    far_rows = many(4)
    keyvals, bias, gains, wkv = many(4)
    final, land = many(n), many(n)
    slices = next(take)
    input_grad = next(take)
    own_part = {m: next(take) for m in range(n) if share[m] == m}
    part = [own_part[share[m]] for m in range(n)]
    held = many(n)
    ring_of = sorted(set(sizes))
    load, outer, mid = many(len(ring_of)), many(len(ring_of)), many(len(ring_of))
    load = [load[ring_of.index(size)] for size in sizes]
    down_all, grad_hidden, strips, slices_stage, middle, grad_out, grad_mid, branch, grad_q, tiles, stage, stage_kv, grad_kv, sums, up_sums = many(15)
    attended, queries, normed, tokens = many(4)
    sib, ld, sent, came, zs, z_in, z_mid, os, z_fin, xs, xr, loc, ss, gs, gr, ws, ms, ts, ps, free_in, free_mid, ready = take
    chips = groups // 2
    g, me = lax.axis_index("grp"), lax.axis_index("shard")
    p, c = lax.div(g, 2), lax.rem(g, 2)
    low = p < chips // 2
    inn = jnp.where(low, g + 2, g - 2)
    out = jnp.where(low, g - 2, g + 2)
    end = (p == 0) | (p == chips - 1)
    middle_chip = (p == chips // 2 - 1) | (p == chips // 2)
    other = g + 1 - 2 * c
    near = near_first(count)

    barrier = pltpu.get_barrier_semaphore()

    def greet(target):
        pl.semaphore_signal(barrier, inc=1, device_id=target, device_id_type=MESH)

    greet((other, me))
    greet((inn, me))
    for q in range(1, count):
        greet((g, lax.bitwise_xor(me, q)))

    @pl.when(jnp.logical_not(end))
    def _():
        greet((out, me))

    pl.semaphore_wait(barrier, count + 2 - end.astype(jnp.int32))

    def send(src, dst, send_sem, recv_sem, target):
        pltpu.make_async_remote_copy(
            src_ref=src, dst_ref=dst, send_sem=send_sem, recv_sem=recv_sem,
            device_id=target, device_id_type=MESH,
        ).start()

    def wait(ref, sem):
        pltpu.make_async_copy(ref, ref, sem).wait()

    def add(dst, *more):
        @pl.loop(0, dst.shape[0] // 16)
        def _(i):
            at = pl.ds(pl.multiple_of(i * 16, 16), 16)
            total = dst[at].astype(F32)
            for ref in more:
                total = total + ref[at].astype(F32)
            dst[at] = total.astype(BF)

    cut = lambda m, j: pl.ds(j * sizes[m][0], sizes[m][0])
    away = lambda q: lax.bitwise_xor(me, q)

    rows, width = attended.shape
    hidden = grad_hidden.shape[1]
    everyone = down_all.shape[0]
    arrived = lambda q: down_all.at[pl.ds(q * rows, rows)]
    whole_down = pltpu.make_async_copy(down_rows, down_all, ms.at[6])
    whole_down.start()
    span = pl.ds(pl.multiple_of(me * attended.shape[0], 16), attended.shape[0])
    own_copies = [
        pltpu.make_async_copy(middle_far, middle, ms.at[0]),
        pltpu.make_async_copy(down_rows.at[span], grad_out, ms.at[1]),
    ]
    for i, (a, b) in enumerate(zip(far_rows, (attended, queries, normed, tokens))):
        own_copies.append(pltpu.make_async_copy(a, b, ms.at[2 + i]))
    for copy in own_copies:
        copy.start()

    def send_slices():
        pl.semaphore_wait(ready, count - 1)
        part_of = lambda col: slices.at[pl.ds(pl.multiple_of(col * rows, 16), rows)]
        for q in near:
            send(part_of(away(q)), arrived(q), gs.at[q], gr.at[q], (g, away(q)))
        pltpu.make_async_copy(part_of(me), arrived(0), gr.at[0]).start()


    pair_tasks = [
        [(m, j, q) for q in [0] + near for j in range(subs[m])]
        if plain[m]
        else [(m, j, q) for j in range(subs[m]) for q in near + [0]]
        for m in range(n)
    ]
    flat = [task for tasks in pair_tasks for task in tasks]

    begun, paired_set = set(), set()

    def spot(m, q):
        return part[m].at[q - 1] if q else held[m].at[me]

    def loads(k):
        m, j, q = flat[k]
        slot = k % 2
        return [pltpu.make_async_copy(land[m].at[q, cut(m, j)], load[m].at[slot], ld.at[slot])]

    def begin(k):
        m, j, q = flat[k]
        if j == 0:
            wait(land[m].at[q], sib.at[m, q])
        begun.add(k)
        for copy in loads(k):
            copy.start()

    def pair(k):
        m, j, q = flat[k]
        paired_set.add(k)
        if k not in begun:
            begin(k)
        if k + 1 < len(flat) and flat[k + 1][0] == m and (flat[k + 1][1] > j or not plain[m]):
            begin(k + 1)
        for copy in loads(k):
            copy.wait()
        ref = spot(m, q).at[cut(m, j)]
        add(ref, load[m].at[k % 2])
        if q:
            send(ref, held[m].at[me, cut(m, j)], sent.at[m], came.at[m, j, q], (g, away(q)))

    units = []
    for m in range(n):
        units += [(m, j, q) for q in ([0] + near if plain[m] else [0]) for j in range(subs[m])]
    rings = [ring_of.index(sizes[m]) for m, j, q in units]
    index = [rings[:u].count(rings[u]) for u in range(len(units))]
    total_in = [rings.count(r) for r in range(len(ring_of))]
    slot_of = lambda u: index[u] % outer[rings[u]].shape[0]
    reused = lambda u: index[u] >= outer[rings[u]].shape[0]
    again = lambda u: index[u] + outer[rings[u]].shape[0] < total_in[rings[u]]

    def value(u):
        m, j, q = units[u]
        return held[m].at[away(q), cut(m, j)]

    def result(u, half):
        m, j, q = units[u]
        return final[m].at[half, away(q) if plain[m] else 0, cut(m, j)]

    def inward(u):
        m, j, q = units[u]
        ref = value(u)
        if plain[m]:
            if q:
                wait(ref, came.at[m, j, q])
        else:
            others = [held[m].at[away(r), cut(m, j)] for r in near]
            for r, other_ref in zip(near, others):
                wait(other_ref, came.at[m, j, r])
            add(ref, *others)
        box, slot = rings[u], slot_of(u)

        @pl.when(jnp.logical_not(end))
        def _():
            wait(outer[box].at[slot], z_in.at[u])
            add(ref, outer[box].at[slot])
            if again(u):
                pl.semaphore_signal(free_in.at[box, slot], inc=1, device_id=(out, me), device_id_type=MESH)

        @pl.when(middle_chip)
        def _():
            if reused(u):
                pl.semaphore_wait(free_mid.at[box, slot], 1)
            send(ref, mid[box].at[slot], zs.at[u], z_mid.at[u], (inn, me))

        @pl.when(jnp.logical_not(middle_chip))
        def _():
            if reused(u):
                pl.semaphore_wait(free_in.at[box, slot], 1)
            send(ref, outer[box].at[slot], zs.at[u], z_in.at[u], (inn, me))

    def centre(u):
        box, slot = rings[u], slot_of(u)

        @pl.when(middle_chip)
        def _():
            ref = value(u)
            wait(ref, zs.at[u])
            wait(mid[box].at[slot], z_mid.at[u])
            add(ref, mid[box].at[slot])
            if again(u):
                pl.semaphore_signal(free_mid.at[box, slot], inc=1, device_id=(inn, me), device_id_type=MESH)
            pl.when(jnp.logical_not(end))(
                lambda: send(ref, result(u, c), os.at[u], z_fin.at[u], (out, me))
            )
            send(ref, result(u, c), xs.at[u], xr.at[u], (other, me))
            pltpu.make_async_copy(ref, result(u, c), loc.at[u]).start()

    def outward(u):
        @pl.when(jnp.logical_not(middle_chip))
        def _():
            ref = result(u, c)
            wait(ref, z_fin.at[u])
            pl.when(jnp.logical_not(end))(
                lambda: send(ref, ref, os.at[u], z_fin.at[u], (out, me))
            )
            send(ref, ref, xs.at[u], xr.at[u], (other, me))

    length = bias.shape[1]
    scale = HD**-0.5
    band = 32
    column = lambda at, size: pl.ds(pl.multiple_of(at, 128), size)

    def moments(x):
        centre_ = jnp.mean(x, axis=1, keepdims=True)
        offset = x - centre_
        rate = lax.rsqrt(jnp.mean(offset * offset, axis=1, keepdims=True) + EPS)
        return offset * rate, rate

    def clear():
        sums[...] = jnp.zeros_like(sums)
        grad_kv[...] = jnp.zeros_like(grad_kv)

    def tally(k, x):
        sums[k : k + 1, :] += jnp.sum(x, axis=0, keepdims=True)

    def second_norm(lo, hi):
        gain = gains[4:5, :]

        @pl.loop(lo, hi)
        def _(i):
            at = pl.ds(pl.multiple_of(i * band, band), band)
            grad = jnp.zeros((band, width), F32)
            for q in range(count):
                grad = grad + down_all[pl.ds(pl.multiple_of(q * rows + i * band, band), band), :].astype(F32)
            unit, rate = moments(middle[at, :])
            tally(0, grad * unit)
            tally(1, grad)
            e = grad * gain
            back = rate * (
                e - jnp.mean(e, axis=1, keepdims=True) - unit * jnp.mean(e * unit, axis=1, keepdims=True)
            )
            away_grad = grad_out[at, :].astype(F32)
            tally(7, away_grad)
            whole = back + away_grad
            grad_mid[at, :] = whole
            short = whole.astype(BF)
            branch[at, :] = short
            tally(2, short.astype(F32))

    def first_norm(lo, hi):
        gain = gains[0:1, :]

        @pl.loop(lo, hi)
        def _(i):
            at = pl.ds(pl.multiple_of(i * band, band), band)
            grad = middle[at, :]
            unit, rate = moments(tokens[at, :].astype(F32))
            tally(3, grad * unit)
            tally(4, grad)
            e = grad * gain
            back = rate * (
                e - jnp.mean(e, axis=1, keepdims=True) - unit * jnp.mean(e * unit, axis=1, keepdims=True)
            )
            input_grad[at, :] = (back + grad_mid[at, :]).astype(BF)
            tally(5, grad_q[at, :].astype(F32))

    part_cols = min(512, width)

    def outer_product(dst, left, start, size, right):
        lhs = left[:, start : start + size] if isinstance(start, int) else left[:, column(start, size)]

        @pl.loop(0, right.shape[1] // min(part_cols, right.shape[1]))
        def _(k):
            cols = column(k * min(part_cols, right.shape[1]), min(part_cols, right.shape[1]))
            dst[:, cols] = lax.dot_general(
                lhs, right[:, cols], (((0,), (0,)), ((), ())), preferred_element_type=F32
            ).astype(BF)

    staged = []

    def stage_slot(m, q, size):
        k = len(staged)
        if k >= 2:
            before = staged[k - 2]
            wait(stage.at[k % 2, pl.ds(0, sizes[before[0]][0] * subs[before[0]]), : sizes[before[0]][1]], ss.at[before[0], before[1]])
        staged.append((m, q))
        return stage.at[k % 2, pl.ds(0, size), : sizes[m][1]]

    def weight_terms(m, left, right, some):
        size = width // count // 2
        for q in some:
            slot = stage_slot(m, q, size)
            outer_product(slot, left, (away(q) * 2 + 1 - c) * size, size, right)
            send(slot, land[m].at[q], ss.at[m, q], sib.at[m, q], (other, me))
            outer_product(spot(m, q), left, (away(q) * 2 + c) * size, size, right)

    strip_jobs = []

    def strip(source, start, size):
        strip_jobs.append((source, start, size))

    def strip_copy(k):
        source, start, size = strip_jobs[k]
        return pltpu.make_async_copy(
            source.at[:, column(start, size)], strips.at[k % 2, :, pl.ds(0, size)], ts.at[k % 2]
        )

    def use_strip(k):
        strip_copy(k).wait()
        return strips.at[k % 2]

    def next_strip(k):
        if k < len(strip_jobs):
            strip_copy(k).start()

    down_size = hidden // count // 2
    up_size = width // count // 2
    tile = tiles.shape[1]
    for q in [0] + near:
        strip(act, away(q) * 2 * down_size, 2 * down_size)
    for f in range(hidden // tile):
        strip(slope, f * tile, tile)
    for q in [0] + near:
        strip(normed_two, (away(q) * 2 + 1 - c) * up_size, up_size)
        strip(normed_two, (away(q) * 2 + c) * up_size, up_size)

    def down_terms(i):
        q = ([0] + near)[i]
        if i == 0:
            whole_down.wait()
        left = use_strip(i)
        slot = stage_slot(0, q, down_size)
        for k in range(2):

            @pl.when(c == k)
            def _():
                outer_product(slot, left, (1 - k) * down_size, down_size, down_all)

        send(slot, land[0].at[q], ss.at[0, q], sib.at[0, q], (other, me))
        for k in range(2):

            @pl.when(c == k)
            def _():
                outer_product(spot(0, q), left, k * down_size, down_size, down_all)

        next_strip(i + 2)

    block = hidden // (groups)

    def hidden_tile(f):
        k = count + f
        gate = use_strip(k)
        if f + 1 < hidden // tile:
            weight_rows(wdn, f + 1, width).start()
        weight_rows(wdn, f, width).wait()
        up_sums[pl.ds(f * (tile // block), tile // block), :] = jnp.zeros((tile // block, block), F32)

        @pl.loop(0, everyone // rows)
        def _(i):
            at = pl.ds(pl.multiple_of(i * rows, rows), rows)
            got = lax.dot_general(
                down_all[at, :], tiles[f % 2], (((1,), (1,)), ((), ())), preferred_element_type=F32
            )
            low_grad = (got * gate[at, :tile].astype(F32)).astype(BF)
            grad_hidden[at, f * tile : (f + 1) * tile] = low_grad
            total = jnp.sum(low_grad.astype(F32), axis=0, keepdims=True)
            for b in range(tile // block):
                k_ = f * (tile // block) + b
                up_sums[k_ : k_ + 1, :] += total[:, b * block : (b + 1) * block]

        next_strip(k + 2)
        if f + 1 == hidden // tile:
            for q in near:
                pl.semaphore_signal(ready, inc=1, device_id=(g, away(q)), device_id_type=MESH)

    def up_terms(i):
        q = ([0] + near)[i]
        k = count + hidden // tile + 2 * i
        slot = stage_slot(1, q, up_size)
        outer_product(slot, use_strip(k), 0, up_size, grad_hidden)
        next_strip(k + 2)
        send(slot, land[1].at[q], ss.at[1, q], sib.at[1, q], (other, me))
        outer_product(spot(1, q), use_strip(k + 1), 0, up_size, grad_hidden)
        next_strip(k + 3)

    def weight_rows(source, i, size):
        return pltpu.make_async_copy(
            source.at[pl.ds(i * tile, tile)], tiles.at[i % 2, :, pl.ds(0, size)], ws.at[i % 2]
        )

    def slice_out(d):
        return pltpu.make_async_copy(
            slices_stage.at[d % 2], slices.at[:, pl.ds(d * tile, tile)], ps.at[d % 2]
        )

    def slice_tile(d):
        if d + 1 < width // tile:
            weight_rows(wup, d + 1, hidden).start()
        weight_rows(wup, d, hidden).wait()
        if d >= 2:
            slice_out(d - 2).wait()

        @pl.loop(0, everyone // rows)
        def _(i):
            at = pl.ds(pl.multiple_of(i * rows, rows), rows)
            slices_stage[d % 2, at, :] = lax.dot_general(
                grad_hidden[at, :], tiles[d % 2, :, :hidden], (((1,), (1,)), ((), ())),
                preferred_element_type=F32,
            ).astype(BF)

        slice_out(d).start()
        if d + 1 == width // tile:
            slice_out(d - 1).wait()
            slice_out(d).wait()

    tile_rows = tiles.shape[1]
    tile_count = width // tile_rows

    def weight_tile(source, i):
        at = pl.multiple_of(i * tile_rows, tile_rows)
        slot = lax.rem(i, 2)
        return pltpu.make_async_copy(source.at[pl.ds(at, tile_rows)], tiles.at[slot], ws.at[slot])

    def attention_tiles(lo, hi):
        @pl.loop(lo, hi)
        def _(i):
            pl.when(i + 1 < tile_count)(lambda: weight_tile(wo, i + 1).start())
            weight_tile(wo, i).wait()
            cols = column(i * tile_rows, tile_rows)
            grad_att = lax.dot_general(
                branch[...], tiles[lax.rem(i, 2)], (((1,), (1,)), ((), ())), preferred_element_type=F32
            ).astype(BF)
            query = queries[:, cols]
            heads = tile_rows // HD
            fold = lambda x: jnp.concatenate([x[:, h * HD : (h + 1) * HD] for h in range(heads)], axis=0)
            for m in range(rows // length):
                at = pl.ds(m * length, length)
                q = fold(query[m * length : (m + 1) * length])
                ga = fold(grad_att[m * length : (m + 1) * length])
                k, v = keyvals[at, :HD], keyvals[at, HD:]
                shut = jnp.concatenate([bias[at, :]] * heads, axis=0)
                s = lax.dot_general(q, k, (((1,), (1,)), ((), ())), preferred_element_type=F32) * scale + shut
                e = jnp.exp(s - jnp.max(s, axis=1, keepdims=True))
                probs = e / jnp.sum(e, axis=1, keepdims=True)
                gp = lax.dot_general(ga, v, (((1,), (1,)), ((), ())), preferred_element_type=F32)
                ds = (probs * (gp - jnp.sum(probs * gp, axis=1, keepdims=True))).astype(BF)
                dq = (jnp.dot(ds, k, preferred_element_type=F32) * scale).astype(BF)
                for h in range(heads):
                    grad_q[at, column(i * tile_rows + h * HD, HD)] = dq[h * length : (h + 1) * length]
                tn = (((0,), (0,)), ((), ()))
                dk = lax.dot_general(ds, q, tn, preferred_element_type=F32) * scale
                dv = lax.dot_general(probs.astype(BF), ga, tn, preferred_element_type=F32)
                grad_kv[at, :HD] += dk
                grad_kv[at, HD:] += dv

    def query_tiles(lo, hi):
        low_kv = grad_kv[...].astype(BF)

        @pl.loop(lo, hi)
        def _(i):
            pl.when(i + 1 < tile_count)(lambda: weight_tile(wq, i + 1).start())
            weight_tile(wq, i).wait()
            cols = column(i * tile_rows, tile_rows)
            nt = (((1,), (1,)), ((), ()))
            middle[:, cols] = lax.dot_general(
                grad_q[...], tiles[lax.rem(i, 2)], nt, preferred_element_type=F32
            ) + lax.dot_general(
                low_kv, wkv[pl.ds(pl.multiple_of(i * tile_rows, tile_rows), tile_rows)], nt,
                preferred_element_type=F32,
            )

    def keyval_terms():
        low_kv = grad_kv[...].astype(BF)
        size = width // count // 2
        last = n - 1
        line = jnp.sum(low_kv[:, HD:].astype(F32), axis=0, keepdims=True)
        for k in range(width // size):
            sums[6:7, k * size : k * size + HD] = line
        for q in near + [0]:
            for ref, which in ((stage_kv.at[q], 1 - c), (spot(last, q), c)):
                start = (away(q) * 2 + which) * size
                ref[pl.ds(0, size), :] = lax.dot_general(
                    normed[:, column(start, size)], low_kv, (((0,), (0,)), ((), ())),
                    preferred_element_type=F32,
                ).astype(BF)
                ref[pl.ds(size, 16), :] = jnp.zeros((16, 2 * HD), BF)
                ref[pl.ds(size, 16), :size] = sums[:, column(start, size)].astype(BF)
                mine = up_sums[pl.ds(away(q) * 2 + which, 1), :]
                mine = jnp.concatenate([mine] * (2 * HD // block), axis=1)
                flat_at = lax.broadcasted_iota(jnp.int32, (16, 2 * HD), 0) * (2 * HD)
                flat_at = flat_at + lax.broadcasted_iota(jnp.int32, (16, 2 * HD), 1)
                own_place = lax.div(flat_at, block) == me
                ref[pl.ds(size + 16, 16), :] = jnp.where(own_place, mine, 0.0).astype(BF)
            send(stage_kv.at[q], land[last].at[q], ss.at[last, q], sib.at[last, q], (other, me))

    def reuse(m):
        if share[m] != m:
            wait(part[m], sent.at[share[m]])

    bands = rows // band
    plan = {}

    def at_step(step, *work):
        plan.setdefault(step, []).extend(work)

    P_ = partial
    starts = [sum(len(t) for t in pair_tasks[:m]) for m in range(n)]
    pairs_ = lambda m, lo, hi: [P_(pair, starts[m] + k) for k in range(lo, min(hi, len(pair_tasks[m])))]
    def got_slices():
        clear()
        for copy in own_copies:
            copy.wait()
        for q in [0] + near:
            wait(arrived(q), gr.at[q])

    order = near + [0]
    quarter = lambda k: (k * bands // 4, (k + 1) * bands // 4)
    tile_of = lambda k: (k * tile_count // 8, (k + 1) * tile_count // 8)
    subs_0, subs_1 = subs[0], subs[1]

    def begin_all():
        next_strip(0)
        next_strip(1)
        down_terms(0)
        for work in pairs_(0, 0, subs_0):
            work()

    queue = []
    for i in range(1, count):
        queue += [(3.5, P_(down_terms, i))] + [(0.3, x) for x in pairs_(0, i * subs_0, (i + 1) * subs_0)]
    queue += [(0.0, lambda: weight_rows(wdn, 0, width).start())]
    queue += [(12.0 / (hidden // tile), P_(hidden_tile, f)) for f in range(hidden // tile)]
    queue += [(0.0, lambda: weight_rows(wup, 0, hidden).start())]
    queue += [(1.5, P_(slice_tile, d)) for d in range(width // tile)]
    queue += [(0.0, send_slices)]
    for i in range(count):
        queue += [(3.5, P_(up_terms, i))] + [(0.3, x) for x in pairs_(1, i * subs_1, (i + 1) * subs_1)]
    later = [(0.0, got_slices)]
    later += [(2.5, P_(second_norm, *quarter(k))) for k in range(4)]
    later += [(0.0, lambda: weight_tile(wo, 0).start()), (0.0, P_(reuse, 2))]
    later += [(16.0 / count, P_(weight_terms, 2, attended, branch, [q])) for q in order]
    pairs_2, pairs_3 = pairs_(2, 0, 99), pairs_(3, 0, 99)
    share_of = lambda work, k: [(0.4, x) for x in work[k * len(work) // 4 : (k + 1) * len(work) // 4]]
    for k in range(8):
        later += [(TILE_COST, P_(attention_tiles, *tile_of(k)))]
        later += share_of(pairs_2, k) if k < 4 else []
    later += [(0.0, lambda: weight_tile(wq, 0).start()), (0.0, P_(reuse, 3))]
    later += [(16.0 / count, P_(weight_terms, 3, normed, grad_q, [q])) for q in order]
    for k in range(8):
        later += [(0.8, P_(query_tiles, *tile_of(k)))]
        later += share_of(pairs_3, k) if k < 4 else []
    later += [(2.5, P_(first_norm, *quarter(k))) for k in range(4)]
    later += [(4.0, keyval_terms)]
    later += [(1.0, work) for work in pairs_(4, 0, 99)]
    step, spent = 0, 0.0
    for some, start in ((queue, 0), (later, NORM_STEP)):
        if start > step:
            step, spent = start, 0.0
        for cost, work in some:
            if spent + cost > BUDGET and spent:
                spent, step = 0.0, step + 1
            spent += cost
            at_step(step, work)
    needs = {}
    for m, per_unit in ((0, 1), (1, 1), (2, count), (3, count), (4, count)):
        base_unit = [u for u in range(len(units)) if units[u][0] == m][0]
        for k, work in enumerate(pair_tasks[m]):
            needs.setdefault(base_unit + k // per_unit, []).append((m, k))
    begin_all()
    cursor = [0]
    steps = max(len(units) + LAG_OUT, max(plan) + 1)
    for step in range(steps):
        if step < len(units):
            while any(starts[m] + k not in paired_set for m, k in needs[step]):
                while not plan.get(cursor[0]):
                    cursor[0] += 1
                plan[cursor[0]].pop(0)()
            inward(step)
        if 0 <= step - LAG_MID < len(units):
            centre(step - LAG_MID)
        if 0 <= step - LAG_OUT < len(units):
            outward(step - LAG_OUT)
        for at in range(cursor[0], step + 1):
            for work in plan.pop(at, ()):
                work()
        cursor[0] = max(cursor[0], step + 1)

    for m in range(n):
        if m not in share[m + 1 :]:
            wait(part[m], sent.at[m])
        for q in near + [0]:
            if m == n - 1 or (m, q) in staged[-2:]:
                wait(land[m].at[q], ss.at[m, q])
    for q in near:
        wait(arrived(q), gs.at[q])
    for u in range(len(units)):
        wait(result(u, 1 - c), xr.at[u])
        wait(result(u, c), xs.at[u])
        pl.when(jnp.logical_not(end))(partial(wait, result(u, c), os.at[u]))
        pl.when(middle_chip)(partial(wait, result(u, c), loc.at[u]))
        pl.when(jnp.logical_not(middle_chip))(partial(wait, value(u), zs.at[u]))


def back_all(groups, count, far, own, near_by):
    rows, width = own[0].shape
    everyone, hidden = far[0].shape
    size = width // count // 2
    tile = 2 * HD
    low = (size + 32, 2 * HD)
    shapes = [(hidden // count // 2, width), (size, hidden), (size, width), (size, width), low]
    plain, subs = (True, True, False, False, False), (4, 4, 4, 4, 1)
    n = len(shapes)
    sizes = [(s[0] // k, s[1]) for s, k in zip(shapes, subs)]
    share = list(range(n))
    for m in (2, 3):
        share[m] = m - 2 if shapes[m] == shapes[m - 2] else 2
    rings = sorted(set(sizes))
    units = sum(s * (count if f else 1) for s, f in zip(subs, plain))
    slots = [min(RING, sum(s * (count if f else 1) for s, f, z in zip(subs, plain, sizes) if z == r)) for r in rings]
    any_, vmem = pl.BlockSpec(memory_space=pl.ANY), pl.BlockSpec(memory_space=pltpu.VMEM)
    dma, regular = pltpu.SemaphoreType.DMA, pltpu.SemaphoreType.REGULAR
    out = [jax.ShapeDtypeStruct((2, count if f else 1) + s, BF) for s, f in zip(shapes, plain)]
    out += [jax.ShapeDtypeStruct((count,) + s, BF) for s in shapes]
    scratch = [pltpu.VMEM((count - 1,) + shapes[m], BF) for m in range(n) if share[m] == m]
    scratch += [pltpu.VMEM((count,) + s, BF) for s in shapes]
    scratch += [pltpu.VMEM((2,) + r, BF) for r in rings]
    scratch += [pltpu.VMEM((k,) + r, BF) for k, r in zip(slots, rings)] * 2
    scratch += [
        pltpu.VMEM((everyone, width), BF), pltpu.VMEM((everyone, hidden), BF),
        pltpu.VMEM((2, everyone, max(2 * hidden // count // 2, tile)), BF), pltpu.VMEM((2, everyone, tile), BF),
        pltpu.VMEM((rows, width), F32), pltpu.VMEM((rows, width), BF), pltpu.VMEM((rows, width), F32),
        pltpu.VMEM((rows, width), BF), pltpu.VMEM((rows, width), BF), pltpu.VMEM((2, tile, width), BF),
        pltpu.VMEM((2, max(s[0] for s in shapes[:4]), width), BF), pltpu.VMEM((count,) + low, BF),
        pltpu.VMEM((rows, 2 * HD), F32),
        pltpu.VMEM((16, width), F32), pltpu.VMEM((max(16, groups), hidden // groups), F32),
        pltpu.VMEM((rows, width), BF), pltpu.VMEM((rows, width), BF), pltpu.VMEM((rows, width), BF),
        pltpu.VMEM((rows, width), BF),
        dma((n, count)), dma((2,)), dma((n,)), dma((n, max(subs), count)), dma((units,)), dma((units,)),
        dma((units,)), dma((units,)), dma((units,)), dma((units,)), dma((units,)), dma((units,)),
        dma((n, count)), dma((count,)), dma((count,)), dma((2,)), dma((7,)), dma((2,)), dma((2,)),
        regular((len(rings), max(slots))), regular((len(rings), max(slots))), regular,
    ]
    got = pl.pallas_call(
        partial(back_kernel, groups, count, subs, plain, sizes, share),
        out_shape=tuple(out) + (jax.ShapeDtypeStruct((everyone, width), BF), jax.ShapeDtypeStruct((rows, width), BF)),
        in_specs=[any_] * 13 + [vmem] * 4,
        out_specs=(any_,) * (2 * n + 1) + (vmem,),
        scratch_shapes=scratch,
        compiler_params=pltpu.CompilerParams(
            collective_id=2, has_side_effects=True, vmem_limit_bytes=60 * 1024 * 1024
        ),
        cost_estimate=pl.CostEstimate(flops=0, bytes_accessed=200_000_000, transcendentals=0),
        name="back_all",
    )(*far, *own, *near_by)
    return got[:n], got[-1]


def lift_kernel(rows, weight, bias, act, slope):
    u = jnp.dot(rows[...], weight[...], preferred_element_type=F32) + bias[...]
    root = 0.7978845608028654
    t = jnp.tanh(root * (u + 0.044715 * (u * u * u)))
    half = 0.5 * (1.0 + t)
    act[...] = (u * half).astype(BF)
    slope[...] = (half + 0.5 * u * (1.0 - t * t) * (root * (1.0 + 3 * 0.044715 * (u * u)))).astype(BF)


def lift(rows, weight, bias):
    n, hidden = rows.shape[0], weight.shape[1]
    tile = 2 * HD
    out = jax.ShapeDtypeStruct((n, hidden), BF)
    column = lambda k: pl.BlockSpec((k, tile), lambda i: (0, i))
    return pl.pallas_call(
        lift_kernel,
        out_shape=(out, out),
        grid=(hidden // tile,),
        in_specs=[pl.BlockSpec(rows.shape, lambda i: (0, 0)), column(weight.shape[0]), column(1)],
        out_specs=(column(n), column(n)),
        compiler_params=pltpu.CompilerParams(vmem_limit_bytes=48 * 1024 * 1024),
        name="lift",
    )(rows, weight, bias)


def widen_kernel(block, size, down, up, out, query, low, o_down, o_up, o_out, o_query, o_low, *lines):
    o_down[...] = down[...].astype(F32)
    o_out[...] = out[...].astype(F32)
    o_query[...] = query[...].astype(F32)
    _, count, rows, hidden = up.shape
    for source in range(count):
        for k in range(hidden // block):
            o_up[:, pl.ds((k * count + source) * block, block)] = up[0, source, :, pl.ds(k * block, block)].astype(F32)

    @pl.when(pl.program_id(0) == 0)
    def _():
        for half in range(2):
            o_low[half * size : (half + 1) * size, :] = low[half, :size, :].astype(F32)
            sums = low[half, size : size + 16, :size].astype(F32)
            for v in range(8):
                lines[v][:, half * size : (half + 1) * size] = sums[v : v + 1, :]
            tail = low[half, size + 16 :, :].astype(F32)
            wide = tail.shape[1]
            for r in range(hidden // 2 // wide):
                start = half * hidden // 2 + r * wide
                lines[8][:, start : start + wide] = tail[r : r + 1, :]


def widen(full, block):
    down, up, out, query, low = full
    flat = lambda x: x.reshape(-1, x.shape[-1])
    down, out, query, low = flat(down), flat(out), flat(query), low[:, 0]
    _, count, rows, hidden = up.shape
    steps = 16
    step = 2 * rows // steps
    size = out.shape[0] // 2
    row = lambda x: pl.BlockSpec((x.shape[0] // steps, x.shape[1]), lambda i: (i, 0))
    still = lambda *shape: pl.BlockSpec(shape, lambda i: (0,) * len(shape))
    shape = lambda *dims: jax.ShapeDtypeStruct(dims, F32)
    vectors = [(1, 2 * size)] * 8 + [(1, hidden)]
    return pl.pallas_call(
        partial(widen_kernel, block, size),
        out_shape=(
            shape(*down.shape), shape(2 * rows, count * hidden), shape(*out.shape), shape(*query.shape),
            shape(2 * size, low.shape[2]),
        ) + tuple(shape(*v) for v in vectors),
        grid=(steps,),
        in_specs=[
            row(down), pl.BlockSpec((1, count, step, hidden), lambda i: (i // (steps // 2), 0, i % (steps // 2), 0)),
            row(out), row(query), still(*low.shape),
        ],
        out_specs=(
            row(down), pl.BlockSpec((step, count * hidden), lambda i: (i, 0)), row(out), row(query),
            still(2 * size, low.shape[2]),
        ) + tuple(still(*v) for v in vectors),
        name="widen",
    )(down, up, out, query, low)


def used(lengths, row):
    total = lengths[row, 0]
    for k in range(1, lengths.shape[1]):
        total = total + lengths[row, k]
    return total


def masked(x, lengths, row):
    places = lax.broadcasted_iota(jnp.int32, x.shape, 0)
    return jnp.where(places < used(lengths, row), x, 0.0)


def take_kernel(order, lengths, values, out, held, got, put):
    count = held.shape[0]
    takes = [pltpu.make_async_copy(values.at[order[r]], held.at[r], got.at[r]) for r in range(count)]
    puts = [pltpu.make_async_copy(held.at[r], out.at[r], put.at[r]) for r in range(count)]
    for take in takes:
        take.start()
    for r in range(count):
        takes[r].wait()
        held[r] = masked(held[r].astype(F32), lengths, r).astype(BF)
        puts[r].start()
    for copy in puts:
        copy.wait()


def take_rows(values, order, lengths):
    count = values.shape[0]
    smem, any_ = pl.BlockSpec(memory_space=pltpu.SMEM), pl.BlockSpec(memory_space=pl.ANY)
    return pl.pallas_call(
        take_kernel,
        out_shape=jax.ShapeDtypeStruct(values.shape, BF),
        in_specs=[smem, smem, any_],
        out_specs=any_,
        scratch_shapes=[
            pltpu.VMEM(values.shape, BF), pltpu.SemaphoreType.DMA((count,)), pltpu.SemaphoreType.DMA((count,)),
        ],
        compiler_params=pltpu.CompilerParams(vmem_limit_bytes=32 * 1024 * 1024),
        name="take_rows",
    )(order, lengths, values)


def finish_kernel(deal, lengths, place, first, second, weight, middle, table, out):
    step = pl.program_id(0)
    micro, length, width = middle.shape
    wide = min(512, width)
    left = jnp.concatenate([first[0], second[0]], axis=0)
    for k in range(width // wide):
        cols = pl.ds(k * wide, wide)
        got = jnp.dot(left, weight[:, cols], preferred_element_type=F32)
        for i in range(2):
            row = deal[2 * step + i]
            term = got[i * length : (i + 1) * length]
            own = lax.div(row, micro) == place[0]
            extra = middle[lax.rem(row, micro), :, cols] + table[6:7, cols]
            out[i, :, cols] = masked(term + jnp.where(own, extra, 0.0), lengths, row).astype(BF)


def finish_rows(values, weight, deal, lengths, me, middle, table):
    count, length, depth = values.shape
    width = weight.shape[1]
    row = lambda i: pl.BlockSpec((1, length, depth), lambda j, deal, lengths, me: (deal[2 * j + i], 0, 0))
    still = lambda x: pl.BlockSpec(x.shape, lambda j, deal, lengths, me: (0,) * x.ndim)
    return pl.pallas_call(
        finish_kernel,
        out_shape=jax.ShapeDtypeStruct((count, length, width), BF),
        grid_spec=pltpu.PrefetchScalarGridSpec(
            num_scalar_prefetch=3,
            grid=(count // 2,),
            in_specs=[row(0), row(1), still(weight), still(middle), still(table)],
            out_specs=pl.BlockSpec((2, length, width), lambda j, deal, lengths, me: (j, 0, 0)),
        ),
        compiler_params=pltpu.CompilerParams(vmem_limit_bytes=48 * 1024 * 1024),
        name="finish_rows",
    )(deal, lengths, me.reshape(1), values, values, weight, middle, table)


def cut_kernel(groups, count, block, x, out):
    for to in range(count):
        for k in range(groups):
            out[to, :, k * block : (k + 1) * block] = x[:, (k * count + to) * block : (k * count + to + 1) * block]


def shards(
    groups,
    count,
    tokens,
    cotangent,
    lengths,
    dealing,
    first_gain,
    first_shift,
    query_weight,
    query_bias,
    keyval_weight,
    value_bias,
    out_weight,
    out_bias,
    second_gain,
    second_shift,
    up_weight,
    up_bias,
    down_weight,
    down_bias,
):
    both = ("grp", "shard")
    micro, length, width = tokens.shape
    group_rows = dealing.shape[0]
    group = lax.axis_index("grp")
    me = lax.axis_index("shard")
    half = micro // 2
    block = down_weight.shape[0]
    hidden = block * groups
    rows = micro * length

    deal = dealing - group * group_rows
    steps = jnp.arange(group_rows, dtype=jnp.int32)
    inverse = jnp.sum(jnp.where(deal[:, None] == steps[None, :], steps[:, None], 0), axis=0)

    line = lambda x: jnp.pad(x, (0, 128 - x.shape[0]))
    piece = first_gain.shape[0]
    device = group * count + me
    value_line = lax.dynamic_update_slice(
        jnp.zeros((128,), BF), value_bias, (device * value_bias.shape[0],)
    )
    small = [first_gain, first_shift, query_bias, out_bias, second_gain, second_shift, down_bias]
    small = [line(x) for x in small] + [value_line]
    small += [line(up_bias[k * piece : (k + 1) * piece]) for k in range(block // piece)]
    small = jnp.stack(small + [jnp.zeros((128,), BF)] * (16 - len(small)))
    up_rows = up_weight.shape[0]
    up_cut = pl.pallas_call(
        partial(cut_kernel, groups, count, block),
        out_shape=jax.ShapeDtypeStruct((count, up_rows, hidden), BF),
        name="cut",
    )(up_weight)
    weight_query, weight_out, weight_keyval, small_all, weight_up = gather_all(
        groups, count, query_weight, out_weight, keyval_weight, small, up_cut
    )
    weight_query, weight_out, weight_up, down_weight = lax.optimization_barrier(
        (weight_query, weight_out, weight_up, down_weight)
    )
    weight_down = lax.all_gather(down_weight, "grp", axis=0, tiled=True)

    flat_tokens = tokens.reshape(rows, width)
    (
        normed_two, cot_rows, normed_one, queries, keyvals, attended, middle, table, up_part, bias,
    ) = attend(
        groups, count, flat_tokens, small_all, lengths, cotangent.reshape(rows, width),
        weight_query, weight_out, weight_keyval, hidden, length,
    )
    grad_down = take_rows(cot_rows.reshape(group_rows, length, width), inverse, lengths)
    grad_down = grad_down.reshape(group_rows * length, width)

    activated, slope = lift(normed_two, weight_up, up_part)
    result = finish_rows(
        activated.reshape(group_rows, length, hidden), weight_down, deal, lengths, me,
        middle.reshape(micro, length, width), table,
    )
    block_output = lax.psum_scatter(
        result.reshape(group_rows * length, width), "shard", scatter_dimension=0, tiled=True
    ).reshape(micro, length, width)

    full, input_grad = back_all(
        groups, count,
        (activated, slope, grad_down, weight_down, normed_two, weight_up, weight_query, weight_out, middle),
        (attended, queries, normed_one, flat_tokens), (keyvals, bias, table, weight_keyval),
    )
    input_grad = input_grad.reshape(micro, length, width)

    down_full, up_full, out_full, query_full, keyval_full, *lines = widen(full, block)
    lines = [line.reshape(-1) for line in lines]
    gain_two_grad, shift_two_grad, out_bias_grad, gain_one_grad, shift_one_grad, query_bias_grad = lines[:6]
    short = value_bias.shape[0] * groups
    value_bias_grad = lax.dynamic_slice(lines[6], (me * short,), (short,))
    down_bias_grad, up_bias_grad = lines[7:]

    return (
        block_output, input_grad, gain_one_grad, shift_one_grad, query_full, query_bias_grad, keyval_full,
        value_bias_grad, out_full, out_bias_grad, gain_two_grad, shift_two_grad, up_full, up_bias_grad,
        down_full, down_bias_grad,
    )


def solution(mesh):
    rows = P(("grp", "shard"), None, None)
    flat = P(("grp", "shard"))
    tall = P(("grp", "shard"), None)
    vector, matrix = P("shard"), P("shard", None)
    return jax.shard_map(
        partial(shards, mesh.shape["grp"], mesh.shape["shard"]),
        mesh=mesh,
        in_specs=(
            rows, rows, P("grp", None), P("grp"), flat, flat, tall, flat, tall, flat,
            tall, flat, flat, flat, tall, flat, tall, flat,
        ),
        out_specs=(
            rows, rows, vector, vector, matrix, vector, matrix, vector,
            matrix, vector, vector, vector, matrix, vector, matrix, vector,
        ),
        check_vma=False,
    )
```
